32 devices in a mesh: dp: 4 (over y, core), ctx: 2 (over x), tensor: 4 (over z).
Axes of the slice: x: 2, y: 2, z: 4, core: 2. Of those that a mesh axis runs over, the one named last changes fastest.
Arguments:
- inputs: bfloat16 [4, 2048, 2048], P('dp', 'ctx'), may hold values from -6 to 6
- cotangent: bfloat16 [4, 2048, 2048], P('dp', 'ctx'), may hold values from -6 to 6
- skip_mask: int32 [4], P('dp'), may hold values from 0 to 1, as said below
- group_ids: int32 [4], P('dp'), may hold values from 0 to 1, as said below
- span_order: int32 [4, 4], P('dp'), may hold values from 0 to 3, each once within a row
- exit_scale: float32 [2], replicated, may hold values from 0.5 to 2
- attn_gain: float32 [2048], replicated, may hold values from 0.5 to 1.5
- ffn_gain: float32 [2048], replicated, may hold values from 0.5 to 1.5
- w_query: bfloat16 [2048, 2048], P(None, 'tensor'), may hold values from -0.125 to 0.125
- w_key: bfloat16 [2048, 1024], P(None, 'tensor'), may hold values from -0.125 to 0.125
- w_value: bfloat16 [2048, 1024], P(None, 'tensor'), may hold values from -0.125 to 0.125
- w_output: bfloat16 [2048, 2048], P('tensor'), may hold values from -2 to 2
- w_gate: bfloat16 [2048, 5632], P(None, 'tensor'), may hold values from -0.125 to 0.125
- w_up: bfloat16 [2048, 5632], P(None, 'tensor'), may hold values from -0.125 to 0.125
- w_down: bfloat16 [5632, 2048], P('tensor'), may hold values from -0.078125 to 0.078125
Outputs:
- output: bfloat16 [4, 2048, 2048], P('dp', 'ctx')
- input_grad: float32 [4, 2048, 2048], P('dp', 'ctx')
- attn_gain_grad: float32 [2048], replicated
- ffn_gain_grad: float32 [2048], replicated
- query_grad: float32 [2048, 2048], P(None, 'tensor')
- key_grad: float32 [2048, 1024], P(None, 'tensor')
- value_grad: float32 [2048, 1024], P(None, 'tensor')
- out_proj_grad: float32 [2048, 2048], P('tensor')
- gate_grad: float32 [2048, 5632], P(None, 'tensor')
- up_grad: float32 [2048, 5632], P(None, 'tensor')
- down_grad: float32 [5632, 2048], P('tensor')
The draws below stay inside these ranges and needn't reach their ends.
Inputs may be any that keep to these rules, and one draw needn't show every extreme that they name: `skip_mask`: at least one sequence runs the block and at least one skips it. `group_ids`: both groups are present.
All inputs are finite; a program needn't handle non-finite values.
Results may differ from the reference program's by a relative error of at most 0.014.
Values may be sent and summed in bfloat16 or wider, within the bound.
A program may use at most 320 MiB of HBM per device.

```python
import math
import jax
import jax.numpy as jnp
from jax import lax

D = 2048
HEADS = 16
KV_HEADS = 8
HEAD_DIM = 128
FF = 5632
LENGTH = 2048
SEQS = 4
SPANS = 4


def draw_skip_mask(key, part):
    key = jax.random.fold_in(key, 11)
    first_key, second_key = jax.random.split(key)
    raw = jax.random.randint(first_key, (SEQS,), 0, 2, dtype=jnp.int32)
    picks = jax.random.permutation(second_key, SEQS)
    raw = raw.at[picks[0]].set(1)
    raw = raw.at[picks[1]].set(0)
    return raw


def draw_group_ids(key, part):
    key = jax.random.fold_in(key, 12)
    first_key, second_key = jax.random.split(key)
    raw = jax.random.randint(first_key, (SEQS,), 0, 2, dtype=jnp.int32)
    picks = jax.random.permutation(second_key, SEQS)
    raw = raw.at[picks[0]].set(0)
    raw = raw.at[picks[1]].set(1)
    return raw


def level_of(key, dims, shards, smallest, high):
    def one(axis_at, shards_of):
        steps = jax.random.uniform(jax.random.fold_in(jax.random.fold_in(key, 6), axis_at), (shards_of,), jnp.float32, smallest / len(shards), high / len(shards))
        return jnp.repeat(jnp.exp(steps), dims[axis_at] // shards_of).reshape((-1,) + (1,) * (len(dims) - axis_at - 1))

    loudness = one(*shards[0])
    for cut in shards[1:]:
        loudness = loudness * one(*cut)
    return loudness


def noise(key, shape, scale, reach, cuts=(), held_as=jnp.bfloat16):
    entries = scale * jax.random.normal(key, shape, jnp.float32)
    if cuts:
        entries = entries * level_of(key, shape, cuts, -0.22, 0.18)
    return jnp.clip(entries, -reach, reach).astype(held_as)


def setup_inputs(seed: int = 0) -> dict:
    key_list = jax.random.split(jax.random.key(seed), 16)
    return {
        "inputs": noise(key_list[0], (SEQS, LENGTH, D), 1.0, 6.0, ((0, 4), (1, 2))),
        "cotangent": noise(key_list[1], (SEQS, LENGTH, D), 1.0, 6.0, ((0, 4), (1, 2))),
        "skip_mask": draw_skip_mask(jax.random.fold_in(key_list[15], 71), 0),
        "group_ids": draw_group_ids(jax.random.fold_in(key_list[15], 71), 0),
        "span_order": jax.vmap(lambda own: jax.random.permutation(own, SPANS))(jax.random.split(key_list[4], SEQS)).reshape((SEQS, SPANS)).astype(jnp.int32),
        "exit_scale": jnp.clip(jnp.exp(jax.random.uniform(key_list[5], (2,), jnp.float32, math.log(0.5), math.log(2.0))), 0.5, 2.0),
        "attn_gain": jnp.clip(1.0 + 0.1 * jax.random.normal(key_list[6], (D,), jnp.float32), 0.5, 1.5),
        "ffn_gain": jnp.clip(1.0 + 0.1 * jax.random.normal(key_list[7], (D,), jnp.float32), 0.5, 1.5),
        "w_query": noise(key_list[8], (D, HEADS * HEAD_DIM), D ** -0.5, 0.125, ((1, 4),)),
        "w_key": noise(key_list[9], (D, KV_HEADS * HEAD_DIM), D ** -0.5, 0.125, ((1, 4),)),
        "w_value": noise(key_list[10], (D, KV_HEADS * HEAD_DIM), D ** -0.5, 0.125, ((1, 4),)),
        "w_output": noise(key_list[11], (HEADS * HEAD_DIM, D), (max(2, HEADS * HEAD_DIM // 256)) ** -0.5, 2.0, ((0, 4),)),
        "w_gate": noise(key_list[12], (D, FF), D ** -0.5, 0.125, ((1, 4),)),
        "w_up": noise(key_list[13], (D, FF), D ** -0.5, 0.125, ((1, 4),)),
        "w_down": noise(key_list[14], (FF, D), FF ** -0.5, 0.078125, ((0, 4),)),
    }


EPSILON = 1e-05
NEG_BIG = -1e+30
HIGHEST = lax.Precision.HIGHEST

@jax.custom_vjp
def low(v):
    return lax.optimization_barrier(v.astype(jnp.bfloat16)).astype(jnp.float32)

@jax.custom_vjp
def low_back(v):
    return v

def low_keep(v):
    return (low(v), None)

def low_pass(kept, grad):
    return (grad,)

def back_keep(v):
    return (v, None)

def back_low(kept, grad):
    return (low(grad),)
low.defvjp(low_keep, low_pass)
low_back.defvjp(back_keep, back_low)

def sequence_positions(order_row, length):
    spans = order_row.shape[0]
    stride = length // spans
    places = jnp.arange(length, dtype=jnp.int32)
    onehot = (places // stride)[:, None] == jnp.arange(spans, dtype=jnp.int32)[None, :]
    starts = lax.optimization_barrier(jnp.sum(jnp.where(onehot, order_row[None, :], 0), axis=1)).astype(jnp.int32)
    return starts * stride + places % stride

def rotary_tables(positions):
    inverse = 1.0 / 10000.0 ** (jnp.arange(0, HEAD_DIM, 2, dtype=jnp.float32) / HEAD_DIM)
    angle = positions.astype(jnp.float32)[:, None] * inverse[None, :]
    return (jnp.cos(angle), jnp.sin(angle))

def rotate(field, cosine, sine):
    half = field.shape[-1] // 2
    leading, trailing = (field[..., :half], field[..., half:])
    cosine, sine = (cosine[:, None, :], sine[:, None, :])
    return jnp.concatenate([leading * cosine - trailing * sine, trailing * cosine + leading * sine], axis=-1)

def matmul(left, right):
    return jnp.dot(left, right, precision=HIGHEST, preferred_element_type=jnp.float32)

def attention_one(packed):
    query, keys, values, places = packed
    repeat = HEADS // KV_HEADS
    keys = jnp.repeat(keys, repeat, axis=1)
    values = jnp.repeat(values, repeat, axis=1)
    scores = jnp.einsum('qhd,khd->hqk', query, keys, precision=HIGHEST) * HEAD_DIM ** (-0.5)
    scores = low_back(scores)
    allowed = places[None, :] <= places[:, None]
    scores = jnp.where(allowed[None], scores, NEG_BIG)
    probs = low(jax.nn.softmax(scores, axis=-1))
    return jnp.einsum('hqk,khd->qhd', probs, values, precision=HIGHEST)

def forward(inputs, attn_gain, ffn_gain, w_query, w_key, w_value, w_output, w_gate, w_up, w_down, places, keep_rows):
    seqs, length, width = inputs.shape
    flat = inputs.reshape(-1, width)
    cosine, sine = rotary_tables(places.reshape(-1))
    inv_one = lax.rsqrt(lax.optimization_barrier(jnp.mean(flat * flat, axis=-1, keepdims=True)) + EPSILON)
    normed_one = low(flat * inv_one * attn_gain)
    q_proj = low_back(matmul(normed_one, w_query)).reshape(-1, HEADS, HEAD_DIM)
    queries = low(rotate(q_proj, cosine, sine))
    k_proj = low_back(matmul(normed_one, w_key)).reshape(-1, KV_HEADS, HEAD_DIM)
    keys = low(rotate(k_proj, cosine, sine))
    values = low(low_back(matmul(normed_one, w_value))).reshape(-1, KV_HEADS, HEAD_DIM)
    mixed = lax.map(jax.checkpoint(attention_one), (queries.reshape(seqs, length, HEADS, HEAD_DIM), keys.reshape(seqs, length, KV_HEADS, HEAD_DIM), values.reshape(seqs, length, KV_HEADS, HEAD_DIM), places))
    mixed = low(low_back(mixed)).reshape(-1, HEADS * HEAD_DIM)
    attn_branch = low_back(matmul(mixed, w_output))
    hidden_in = flat + attn_branch
    inv_two = lax.rsqrt(lax.optimization_barrier(jnp.mean(hidden_in * hidden_in, axis=-1, keepdims=True)) + EPSILON)
    normed_two = low(hidden_in * inv_two * ffn_gain)
    gate = low_back(matmul(normed_two, w_gate))
    upward = low_back(matmul(normed_two, w_up))
    acted = low(jax.nn.silu(gate) * upward)
    ffn_branch = low_back(matmul(acted, w_down))
    return (flat + keep_rows * (attn_branch + ffn_branch)).reshape(inputs.shape)

def reference(inputs, cotangent, skip_mask, group_ids, span_order, exit_scale, attn_gain, ffn_gain, w_query, w_key, w_value, w_output, w_gate, w_up, w_down):
    places = jax.vmap(lambda row: sequence_positions(row, LENGTH))(span_order)
    keep_rows = jnp.repeat(skip_mask.astype(jnp.float32), LENGTH)[:, None]
    chosen = jnp.where(group_ids == 1, exit_scale[1], exit_scale[0])
    primals = (inputs.astype(jnp.float32), attn_gain, ffn_gain, w_query.astype(jnp.float32), w_key.astype(jnp.float32), w_value.astype(jnp.float32), w_output.astype(jnp.float32), w_gate.astype(jnp.float32), w_up.astype(jnp.float32), w_down.astype(jnp.float32))

    def wrapped(*params):
        return forward(*params, places, keep_rows)
    result, pullback = jax.vjp(wrapped, *primals)
    scaled = cotangent.astype(jnp.float32) * chosen[:, None, None]
    grads = pullback(scaled)
    return (result.astype(jnp.bfloat16), grads[0], grads[1], grads[2], grads[3], grads[4], grads[5], grads[6], grads[7], grads[8], grads[9])
```

```python
import functools

import jax
import jax.numpy as jnp
from jax import lax
from jax.experimental import pallas as pl
from jax.experimental.pallas import tpu as pltpu
from jax.sharding import PartitionSpec as P

HEAD_DIM = 128
EPSILON = 1e-05
NEG_BIG = -1e30
FACTOR = HEAD_DIM ** (-0.5)
LOG2E = 1.4426950408889634
QUERY_BLOCK = 256
BF16 = jnp.bfloat16
F32 = jnp.float32

NT = (((1,), (1,)), ((), ()))


def nt_dot(left, right):
    return lax.dot_general(left, right, NT, preferred_element_type=F32)


def nn_dot(left, right):
    return jnp.dot(left, right, preferred_element_type=F32)


def stack_heads(block, group):
    return jnp.concatenate(
        [block[:, h * HEAD_DIM : (h + 1) * HEAD_DIM] for h in range(group)], axis=0
    )


def hide_later(scores, first_row, rows, fill):
    key_row = lax.broadcasted_iota(jnp.int32, scores.shape, 0)
    query_row = lax.broadcasted_iota(jnp.int32, scores.shape, 1) % rows + first_row
    return jnp.where(key_row <= query_row, scores, fill)


def attend_kernel(
    group, span, query_order, key_order, q_ref, k_ref, vt_ref, o_ref, lse_ref, top, total, acc
):
    rows = q_ref.shape[0]
    step = pl.program_id(1)
    first = step * rows
    order = query_order[first // span]
    queries = stack_heads(q_ref[...], group)
    top[...] = jnp.full_like(top, NEG_BIG)
    total[...] = jnp.zeros_like(total)
    acc[...] = jnp.zeros_like(acc)

    def visit(place, diagonal):
        keys = k_ref[pl.ds(place, span), :]
        scores = nt_dot(keys, queries) * (FACTOR * LOG2E)
        if diagonal:
            scores = hide_later(scores, first % span, rows, NEG_BIG)
        before = top[...]
        now = jnp.maximum(before, jnp.max(scores, axis=0, keepdims=True))
        weights = jnp.exp2(scores - now)
        shrink = jnp.exp2(before - now)
        top[...] = now
        total[...] = total[...] * shrink + jnp.sum(weights, axis=0, keepdims=True)
        acc[...] = acc[...] * shrink + nn_dot(
            vt_ref[:, pl.ds(place, span)], weights.astype(BF16)
        )

    def one_span(j, carry):
        place = pl.multiple_of(j * span, span)
        pl.when(key_order[j] < order)(lambda: visit(place, False))
        pl.when(key_order[j] == order)(lambda: visit(place, True))
        return carry

    lax.fori_loop(0, k_ref.shape[0] // span, one_span, 0)
    mixed = acc[...] / total[...]
    logs = top[...] + jnp.log2(total[...])
    for h in range(group):
        part = slice(h * rows, (h + 1) * rows)
        o_ref[:, h * HEAD_DIM : (h + 1) * HEAD_DIM] = mixed[:, part].T.astype(BF16)
        lse_ref[0, h : h + 1, :] = logs[:, part]


def attend(queries, keys, values, query_order, key_order, span):
    rows, width = queries.shape
    full, kv_width = keys.shape
    kv_heads = kv_width // HEAD_DIM
    group = width // kv_width
    block = min(QUERY_BLOCK, span)
    query_spec = pl.BlockSpec((block, group * HEAD_DIM), lambda g, i, *_: (i, g))
    return pl.pallas_call(
        functools.partial(attend_kernel, group, span),
        grid_spec=pltpu.PrefetchScalarGridSpec(
            num_scalar_prefetch=2,
            grid=(kv_heads, rows // block),
            in_specs=[
                query_spec,
                pl.BlockSpec((full, HEAD_DIM), lambda g, i, *_: (0, g)),
                pl.BlockSpec((HEAD_DIM, full), lambda g, i, *_: (g, 0)),
            ],
            out_specs=[
                query_spec,
                pl.BlockSpec((1, group, block), lambda g, i, *_: (g, 0, i)),
            ],
            scratch_shapes=[
                pltpu.VMEM((1, group * block), F32),
                pltpu.VMEM((1, group * block), F32),
                pltpu.VMEM((HEAD_DIM, group * block), F32),
            ],
        ),
        out_shape=[
            jax.ShapeDtypeStruct((rows, width), BF16),
            jax.ShapeDtypeStruct((kv_heads, group, rows), F32),
        ],
        compiler_params=pltpu.CompilerParams(vmem_limit_bytes=32 * 2**20),
        cost_estimate=pl.CostEstimate(
            flops=4 * rows * full * width,
            bytes_accessed=4 * rows * width + 4 * full * kv_width,
            transcendentals=rows * full * width // HEAD_DIM,
        ),
    )(query_order, key_order, queries, keys, values.T)


def attend_back_kernel(
    group,
    span,
    query_order,
    key_order,
    q_ref,
    do_ref,
    o_ref,
    lse_ref,
    cos_ref,
    sin_ref,
    k_ref,
    v_ref,
    kt_ref,
    dq_ref,
    dk_ref,
    dv_ref,
    acc,
):
    rows = q_ref.shape[0]
    step = pl.program_id(1)
    first = step * rows
    order = query_order[first // span]
    queries = stack_heads(q_ref[...], group)
    dmixed = stack_heads(do_ref[...], group)
    mixed = stack_heads(o_ref[...], group)
    product = dmixed.astype(F32) * mixed.astype(F32)
    delta = jnp.sum(product.T, axis=0, keepdims=True)
    logs = jnp.concatenate([lse_ref[0, h : h + 1, :] for h in range(group)], axis=1)
    acc[...] = jnp.zeros_like(acc)

    @pl.when(step == 0)
    def _():
        dk_ref[...] = jnp.zeros_like(dk_ref)
        dv_ref[...] = jnp.zeros_like(dv_ref)

    def visit(place, diagonal):
        here = pl.ds(place, span)
        scores = nt_dot(k_ref[here, :], queries) * (FACTOR * LOG2E)
        probs = jnp.exp2(scores - logs)
        if diagonal:
            probs = hide_later(probs, first % span, rows, 0.0)
        dprobs = nt_dot(v_ref[here, :], dmixed)
        dscore = (probs * (dprobs - delta)).astype(BF16)
        dv_ref[here, :] += nn_dot(probs.astype(BF16), dmixed)
        dk_ref[here, :] += nn_dot(dscore, queries)
        acc[...] += nn_dot(kt_ref[:, here], dscore)

    def one_span(j, carry):
        place = pl.multiple_of(j * span, span)
        pl.when(key_order[j] < order)(lambda: visit(place, False))
        pl.when(key_order[j] == order)(lambda: visit(place, True))
        return carry

    lax.fori_loop(0, k_ref.shape[0] // span, one_span, 0)
    half = HEAD_DIM // 2
    cosine, sine = cos_ref[...], sin_ref[...]
    for h in range(group):
        grad = acc[:, h * rows : (h + 1) * rows] * FACTOR
        leading, trailing = grad[:half], grad[half:]
        turned = jnp.concatenate(
            [leading * cosine + trailing * sine, trailing * cosine - leading * sine], axis=0
        )
        dq_ref[:, h * HEAD_DIM : (h + 1) * HEAD_DIM] = turned.T.astype(BF16)

    @pl.when(step == pl.num_programs(1) - 1)
    def _():
        dk_ref[...] = dk_ref[...] * FACTOR


def attend_back(
    queries, dmixed, mixed, logs, cosine, sine, keys, values, query_order, key_order, span
):
    rows, width = queries.shape
    full, kv_width = keys.shape
    kv_heads = kv_width // HEAD_DIM
    group = width // kv_width
    block = min(QUERY_BLOCK, span)
    half = HEAD_DIM // 2
    query_spec = pl.BlockSpec((block, group * HEAD_DIM), lambda g, i, *_: (i, g))
    key_spec = pl.BlockSpec((full, HEAD_DIM), lambda g, i, *_: (0, g))
    table_spec = pl.BlockSpec((half, block), lambda g, i, *_: (0, i))
    return pl.pallas_call(
        functools.partial(attend_back_kernel, group, span),
        grid_spec=pltpu.PrefetchScalarGridSpec(
            num_scalar_prefetch=2,
            grid=(kv_heads, rows // block),
            in_specs=[
                query_spec,
                query_spec,
                query_spec,
                pl.BlockSpec((1, group, block), lambda g, i, *_: (g, 0, i)),
                table_spec,
                table_spec,
                key_spec,
                key_spec,
                pl.BlockSpec((HEAD_DIM, full), lambda g, i, *_: (g, 0)),
            ],
            out_specs=[query_spec, key_spec, key_spec],
            scratch_shapes=[pltpu.VMEM((HEAD_DIM, group * block), F32)],
        ),
        out_shape=[
            jax.ShapeDtypeStruct((rows, width), BF16),
            jax.ShapeDtypeStruct((full, kv_width), F32),
            jax.ShapeDtypeStruct((full, kv_width), F32),
        ],
        compiler_params=pltpu.CompilerParams(vmem_limit_bytes=32 * 2**20),
        cost_estimate=pl.CostEstimate(
            flops=10 * rows * full * width,
            bytes_accessed=8 * rows * width + 14 * full * kv_width,
            transcendentals=rows * full * width // HEAD_DIM,
        ),
    )(
        query_order,
        key_order,
        queries,
        dmixed,
        mixed,
        logs,
        cosine.T,
        sine.T,
        keys,
        values,
        keys.T,
    )


def fold_steps(dp_size, ctx_size):
    steps = []
    bit = 1
    while bit < ctx_size:
        steps.append(("ctx", bit))
        bit *= 2
    along = []
    bit = 2
    while bit < dp_size:
        along.append(("dp", bit))
        bit *= 2
    even, odd = steps + along, along + steps
    plan = [((("dp", 1)), (("dp", 1)))] if dp_size > 1 else []
    return plan + list(zip(even, odd))


def step_perm(step, dp_size, ctx_size):
    pairs = []
    for d in range(dp_size):
        for c in range(ctx_size):
            axis, bit = step[d % 2]
            other = (d ^ bit, c) if axis == "dp" else (d, c ^ bit)
            pairs.append((d * ctx_size + c, other[0] * ctx_size + other[1]))
    return pairs


def step_bit(step):
    d, c = lax.axis_index("dp"), lax.axis_index("ctx")

    def of(axis, bit):
        return jnp.where(((d if axis == "dp" else c) & bit) != 0, 1, 0)

    return jnp.where(d % 2 == 0, of(*step[0]), of(*step[1]))


def sum_plane(grad, dp_size, ctx_size):
    plan = fold_steps(dp_size, ctx_size)
    pieces = grad
    perms = [step_perm(s, dp_size, ctx_size) for s in plan]
    bits = [step_bit(s) for s in plan]
    for perm, bit in zip(perms, bits):
        half = pieces.shape[0] // 2
        kept = lax.dynamic_slice_in_dim(pieces, bit * half, half, 0)
        sent = lax.dynamic_slice_in_dim(pieces, (1 - bit) * half, half, 0).astype(BF16)
        pieces = kept.astype(F32) + lax.ppermute(sent, ("dp", "ctx"), perm).astype(F32)
        if perm is not perms[-1]:
            pieces = pieces.astype(BF16)
    pieces = pieces.astype(BF16)
    for perm, bit in zip(perms[::-1], bits[::-1]):
        other = lax.ppermute(pieces, ("dp", "ctx"), perm)
        pieces = jnp.where(
            bit == 0,
            jnp.concatenate([pieces, other], 0),
            jnp.concatenate([other, pieces], 0),
        )
    return pieces.astype(F32)


def sequence_positions(order_row, length):
    spans = order_row.shape[0]
    stride = length // spans
    places = jnp.arange(length, dtype=jnp.int32)
    onehot = (places // stride)[:, None] == jnp.arange(spans, dtype=jnp.int32)[None, :]
    starts = jnp.sum(jnp.where(onehot, order_row[None, :], 0), axis=1)
    return starts * stride + places % stride


def rotary_tables(positions):
    inverse = 1.0 / 10000.0 ** (jnp.arange(0, HEAD_DIM, 2, dtype=F32) / HEAD_DIM)
    angle = positions.astype(F32)[:, None] * inverse[None, :]
    return (jnp.cos(angle), jnp.sin(angle))


def rotate(field, cosine, sine):
    half = field.shape[-1] // 2
    leading, trailing = (field[..., :half], field[..., half:])
    cosine, sine = (cosine[:, None, :], sine[:, None, :])
    return jnp.concatenate(
        [leading * cosine - trailing * sine, trailing * cosine + leading * sine], axis=-1
    )


def rotate_back(grad, cosine, sine):
    return rotate(grad, cosine, -sine)


def contract_rows(left, right):
    return jnp.einsum("rd,rf->df", left, right, preferred_element_type=F32)


def contract_cols(left, right):
    return jnp.einsum("rc,dc->rd", left, right, preferred_element_type=F32)


def norm_back(dnormed, unit, inverse, gain):
    scaled = dnormed * gain
    return inverse * (scaled - unit * jnp.mean(scaled * unit, axis=-1, keepdims=True))


def scatter_sum(part):
    return lax.psum_scatter(
        part.astype(BF16), "tensor", scatter_dimension=0, tiled=True
    ).astype(F32)


def gather_rows(part):
    return lax.all_gather(part.astype(BF16), "tensor", axis=0, tiled=True)


def swap_ctx(part, ctx_size):
    return [
        lax.ppermute(part, "ctx", [(i, (i + s) % ctx_size) for i in range(ctx_size)])
        for s in range(1, ctx_size)
    ]


def per_device(
    inputs,
    cotangent,
    skip_mask,
    group_ids,
    span_order,
    exit_scale,
    attn_gain,
    ffn_gain,
    w_query,
    w_key,
    w_value,
    w_output,
    w_gate,
    w_up,
    w_down,
):
    _, rows, width = inputs.shape
    dp_size, ctx_size, tensor_size = (lax.axis_size(a) for a in ("dp", "ctx", "tensor"))
    full_len = rows * ctx_size
    spans = span_order.shape[1]
    span = full_len // spans
    kv_local = w_key.shape[1] // HEAD_DIM
    ctx = lax.axis_index("ctx")
    offset = ctx * rows
    positions = lax.dynamic_slice_in_dim(sequence_positions(span_order[0], full_len), offset, rows)
    cosine, sine = rotary_tables(positions)
    keep = skip_mask[0].astype(F32)
    scale = jnp.where(group_ids[0] == 1, exit_scale[1], exit_scale[0])

    own_spans = spans // ctx_size
    orders = [
        lax.dynamic_slice_in_dim(span_order[0], ((ctx - s) % ctx_size) * own_spans, own_spans)
        for s in range(ctx_size)
    ]
    query_order, key_order = orders[0], jnp.concatenate(orders)

    x_low = inputs[0]
    flat = x_low.astype(F32)
    inv_one = lax.rsqrt(jnp.mean(flat * flat, axis=-1, keepdims=True) + EPSILON)
    normed_one = (flat * inv_one * attn_gain).astype(BF16)
    k_proj = nn_dot(normed_one, w_key).reshape(rows, kv_local, HEAD_DIM)
    keys_own = rotate(k_proj, cosine, sine).astype(BF16).reshape(rows, -1)
    values_own = nn_dot(normed_one, w_value).astype(BF16)
    keys = jnp.concatenate([keys_own] + swap_ctx(keys_own, ctx_size), 0)
    values = jnp.concatenate([values_own] + swap_ctx(values_own, ctx_size), 0)
    q_proj = nn_dot(normed_one, w_query).reshape(rows, -1, HEAD_DIM)
    queries = rotate(q_proj, cosine, sine).astype(BF16).reshape(rows, -1)
    mixed, logs = attend(queries, keys, values, query_order, key_order, span)

    own = rows // tensor_size
    first = lax.axis_index("tensor") * own
    take = lambda a: lax.dynamic_slice_in_dim(a, first, own, 0)
    x_own = take(x_low).astype(F32)
    dy_own = take(cotangent[0]).astype(F32) * scale
    attn_own = scatter_sum(nn_dot(mixed, w_output))
    hidden = x_own + attn_own
    inv_two = lax.rsqrt(jnp.mean(hidden * hidden, axis=-1, keepdims=True) + EPSILON)
    unit_two = hidden * inv_two
    normed_two = gather_rows(unit_two * ffn_gain)

    dscaled = cotangent[0].astype(F32) * scale
    dffn = (keep * dscaled).astype(BF16)
    dacted = contract_cols(dffn, w_down)
    gate = nn_dot(normed_two, w_gate)
    upward = nn_dot(normed_two, w_up)
    sigmoid_gate = jax.nn.sigmoid(gate)
    silu_gate = gate * sigmoid_gate
    acted = (silu_gate * upward).astype(BF16)
    dgate = (dacted * upward * sigmoid_gate * (1.0 + gate * (1.0 - sigmoid_gate))).astype(BF16)
    dupward = (dacted * silu_gate).astype(BF16)
    dnormed_own = scatter_sum(contract_cols(dgate, w_gate) + contract_cols(dupward, w_up))
    ffn_own = scatter_sum(nn_dot(acted, w_down))
    total = lambda g: sum_plane(g, dp_size, ctx_size)
    grad_down = total(contract_rows(acted, dffn))
    grad_gate = total(contract_rows(normed_two, dgate))
    grad_up = total(contract_rows(normed_two, dupward))
    grad_ffn_gain = jnp.sum(dnormed_own * unit_two, axis=0)
    dhidden = norm_back(dnormed_own, unit_two, inv_two, ffn_gain)
    dattn = gather_rows(keep * dy_own + dhidden)
    output = gather_rows(x_own + keep * (attn_own + ffn_own))
    grad_output = total(contract_rows(mixed, dattn))
    dmixed = contract_cols(dattn, w_output).astype(BF16)

    dq_proj, dkeys, dvalues = attend_back(
        queries, dmixed, mixed, logs, cosine, sine, keys, values, query_order, key_order, span
    )

    def collect(grad):
        parts = grad.reshape(ctx_size, rows, -1)
        summed = parts[0]
        for s in range(1, ctx_size):
            back = [(i, (i - s) % ctx_size) for i in range(ctx_size)]
            summed = summed + lax.ppermute(parts[s].astype(BF16), "ctx", back).astype(F32)
        return summed

    dk_own = collect(dkeys).reshape(rows, kv_local, HEAD_DIM)
    dk_proj = rotate_back(dk_own, cosine, sine).reshape(rows, -1).astype(BF16)
    dv_proj = collect(dvalues).astype(BF16)
    dnormed_one = scatter_sum(
        contract_cols(dq_proj, w_query)
        + contract_cols(dk_proj, w_key)
        + contract_cols(dv_proj, w_value)
    )
    grad_query = total(contract_rows(normed_one, dq_proj))
    grad_key = total(contract_rows(normed_one, dk_proj))
    grad_value = total(contract_rows(normed_one, dv_proj))
    inv_own = take(inv_one)
    unit_own = x_own * inv_own
    grad_attn_gain = jnp.sum(dnormed_one * unit_own, axis=0)
    grad_attn_gain, grad_ffn_gain = lax.psum(
        (grad_attn_gain, grad_ffn_gain), ("dp", "ctx", "tensor")
    )
    through = gather_rows(dhidden + norm_back(dnormed_one, unit_own, inv_own, attn_gain))
    input_grad = dscaled + through.astype(F32)
    return (
        output.reshape(inputs.shape),
        input_grad.reshape(inputs.shape),
        grad_attn_gain,
        grad_ffn_gain,
        grad_query,
        grad_key,
        grad_value,
        grad_output,
        grad_gate,
        grad_up,
        grad_down,
    )


def solution(mesh):
    rows = P("dp", "ctx", None)
    by_column, by_row = P(None, "tensor"), P("tensor", None)
    in_specs = (rows, rows, P("dp"), P("dp"), P("dp", None), P(), P(), P())
    in_specs += (by_column,) * 3 + (by_row,) + (by_column,) * 2 + (by_row,)
    out_specs = (rows, rows, P(), P()) + (by_column,) * 3 + (by_row,) + (by_column,) * 2 + (by_row,)
    return jax.shard_map(
        per_device, mesh=mesh, in_specs=in_specs, out_specs=out_specs, check_vma=False
    )
```

```python
import functools

import jax
import jax.numpy as jnp
from jax import lax
from jax.experimental import pallas as pl
from jax.experimental.pallas import tpu as pltpu
from jax.sharding import PartitionSpec as P

HEAD_DIM = 128
EPSILON = 1e-05
NEG_BIG = -1e30
FACTOR = HEAD_DIM ** (-0.5)
LOG2E = 1.4426950408889634
QUERY_BLOCK = 256
BF16 = jnp.bfloat16
F32 = jnp.float32

NT = (((1,), (1,)), ((), ()))


def nt_dot(left, right):
    return lax.dot_general(left, right, NT, preferred_element_type=F32)


def nn_dot(left, right):
    return jnp.dot(left, right, preferred_element_type=F32)


def stack_heads(block, group):
    return jnp.concatenate(
        [block[:, h * HEAD_DIM : (h + 1) * HEAD_DIM] for h in range(group)], axis=0
    )


def hide_later(scores, first_row, rows, fill):
    key_row = lax.broadcasted_iota(jnp.int32, scores.shape, 0)
    query_row = lax.broadcasted_iota(jnp.int32, scores.shape, 1) % rows + first_row
    return jnp.where(key_row <= query_row, scores, fill)


def attend_kernel(
    group, span, query_order, key_order, q_ref, k_ref, vt_ref, o_ref, lse_ref, top, total, acc
):
    rows = q_ref.shape[0]
    step = pl.program_id(1)
    first = step * rows
    order = query_order[first // span]
    queries = stack_heads(q_ref[...], group)
    top[...] = jnp.full_like(top, NEG_BIG)
    total[...] = jnp.zeros_like(total)
    acc[...] = jnp.zeros_like(acc)

    def visit(place, diagonal):
        keys = k_ref[pl.ds(place, span), :]
        scores = nt_dot(keys, queries) * (FACTOR * LOG2E)
        if diagonal:
            scores = hide_later(scores, first % span, rows, NEG_BIG)
        before = top[...]
        now = jnp.maximum(before, jnp.max(scores, axis=0, keepdims=True))
        weights = jnp.exp2(scores - now)
        shrink = jnp.exp2(before - now)
        top[...] = now
        total[...] = total[...] * shrink + jnp.sum(weights, axis=0, keepdims=True)
        acc[...] = acc[...] * shrink + nn_dot(
            vt_ref[:, pl.ds(place, span)], weights.astype(BF16)
        )

    def one_span(j, carry):
        place = pl.multiple_of(j * span, span)
        pl.when(key_order[j] < order)(lambda: visit(place, False))
        pl.when(key_order[j] == order)(lambda: visit(place, True))
        return carry

    lax.fori_loop(0, k_ref.shape[0] // span, one_span, 0)
    mixed = acc[...] / total[...]
    logs = top[...] + jnp.log2(total[...])
    for h in range(group):
        part = slice(h * rows, (h + 1) * rows)
        o_ref[:, h * HEAD_DIM : (h + 1) * HEAD_DIM] = mixed[:, part].T.astype(BF16)
        lse_ref[0, h : h + 1, :] = logs[:, part]


def attend(queries, keys, values, query_order, key_order, span):
    rows, width = queries.shape
    full, kv_width = keys.shape
    kv_heads = kv_width // HEAD_DIM
    group = width // kv_width
    block = min(QUERY_BLOCK, span)
    query_spec = pl.BlockSpec((block, group * HEAD_DIM), lambda g, i, *_: (i, g))
    return pl.pallas_call(
        functools.partial(attend_kernel, group, span),
        grid_spec=pltpu.PrefetchScalarGridSpec(
            num_scalar_prefetch=2,
            grid=(kv_heads, rows // block),
            in_specs=[
                query_spec,
                pl.BlockSpec((full, HEAD_DIM), lambda g, i, *_: (0, g)),
                pl.BlockSpec((HEAD_DIM, full), lambda g, i, *_: (g, 0)),
            ],
            out_specs=[
                query_spec,
                pl.BlockSpec((1, group, block), lambda g, i, *_: (g, 0, i)),
            ],
            scratch_shapes=[
                pltpu.VMEM((1, group * block), F32),
                pltpu.VMEM((1, group * block), F32),
                pltpu.VMEM((HEAD_DIM, group * block), F32),
            ],
        ),
        out_shape=[
            jax.ShapeDtypeStruct((rows, width), BF16),
            jax.ShapeDtypeStruct((kv_heads, group, rows), F32),
        ],
        compiler_params=pltpu.CompilerParams(vmem_limit_bytes=32 * 2**20),
        cost_estimate=pl.CostEstimate(
            flops=4 * rows * full * width,
            bytes_accessed=4 * rows * width + 4 * full * kv_width,
            transcendentals=rows * full * width // HEAD_DIM,
        ),
    )(query_order, key_order, queries, keys, values.T)


def attend_back_kernel(
    group,
    span,
    query_order,
    key_order,
    q_ref,
    do_ref,
    o_ref,
    lse_ref,
    cos_ref,
    sin_ref,
    k_ref,
    v_ref,
    kt_ref,
    dq_ref,
    dk_ref,
    dv_ref,
    acc,
):
    rows = q_ref.shape[0]
    step = pl.program_id(1)
    first = step * rows
    order = query_order[first // span]
    queries = stack_heads(q_ref[...], group)
    dmixed = stack_heads(do_ref[...], group)
    mixed = stack_heads(o_ref[...], group)
    product = dmixed.astype(F32) * mixed.astype(F32)
    delta = jnp.sum(product.T, axis=0, keepdims=True)
    logs = jnp.concatenate([lse_ref[0, h : h + 1, :] for h in range(group)], axis=1)
    acc[...] = jnp.zeros_like(acc)

    @pl.when(step == 0)
    def _():
        dk_ref[...] = jnp.zeros_like(dk_ref)
        dv_ref[...] = jnp.zeros_like(dv_ref)

    def visit(place, diagonal):
        here = pl.ds(place, span)
        scores = nt_dot(k_ref[here, :], queries) * (FACTOR * LOG2E)
        probs = jnp.exp2(scores - logs)
        if diagonal:
            probs = hide_later(probs, first % span, rows, 0.0)
        dprobs = nt_dot(v_ref[here, :], dmixed)
        dscore = (probs * (dprobs - delta)).astype(BF16)
        dv_ref[here, :] += nn_dot(probs.astype(BF16), dmixed)
        dk_ref[here, :] += nn_dot(dscore, queries)
        acc[...] += nn_dot(kt_ref[:, here], dscore)

    def one_span(j, carry):
        place = pl.multiple_of(j * span, span)
        pl.when(key_order[j] < order)(lambda: visit(place, False))
        pl.when(key_order[j] == order)(lambda: visit(place, True))
        return carry

    lax.fori_loop(0, k_ref.shape[0] // span, one_span, 0)
    half = HEAD_DIM // 2
    cosine, sine = cos_ref[...], sin_ref[...]
    for h in range(group):
        grad = acc[:, h * rows : (h + 1) * rows] * FACTOR
        leading, trailing = grad[:half], grad[half:]
        turned = jnp.concatenate(
            [leading * cosine + trailing * sine, trailing * cosine - leading * sine], axis=0
        )
        dq_ref[:, h * HEAD_DIM : (h + 1) * HEAD_DIM] = turned.T.astype(BF16)

    @pl.when(step == pl.num_programs(1) - 1)
    def _():
        dk_ref[...] = dk_ref[...] * FACTOR


def attend_back(
    queries, dmixed, mixed, logs, cosine, sine, keys, values, query_order, key_order, span
):
    rows, width = queries.shape
    full, kv_width = keys.shape
    kv_heads = kv_width // HEAD_DIM
    group = width // kv_width
    block = min(QUERY_BLOCK, span)
    half = HEAD_DIM // 2
    query_spec = pl.BlockSpec((block, group * HEAD_DIM), lambda g, i, *_: (i, g))
    key_spec = pl.BlockSpec((full, HEAD_DIM), lambda g, i, *_: (0, g))
    table_spec = pl.BlockSpec((half, block), lambda g, i, *_: (0, i))
    return pl.pallas_call(
        functools.partial(attend_back_kernel, group, span),
        grid_spec=pltpu.PrefetchScalarGridSpec(
            num_scalar_prefetch=2,
            grid=(kv_heads, rows // block),
            in_specs=[
                query_spec,
                query_spec,
                query_spec,
                pl.BlockSpec((1, group, block), lambda g, i, *_: (g, 0, i)),
                table_spec,
                table_spec,
                key_spec,
                key_spec,
                pl.BlockSpec((HEAD_DIM, full), lambda g, i, *_: (g, 0)),
            ],
            out_specs=[query_spec, key_spec, key_spec],
            scratch_shapes=[pltpu.VMEM((HEAD_DIM, group * block), F32)],
        ),
        out_shape=[
            jax.ShapeDtypeStruct((rows, width), BF16),
            jax.ShapeDtypeStruct((full, kv_width), F32),
            jax.ShapeDtypeStruct((full, kv_width), F32),
        ],
        compiler_params=pltpu.CompilerParams(vmem_limit_bytes=32 * 2**20),
        cost_estimate=pl.CostEstimate(
            flops=10 * rows * full * width,
            bytes_accessed=8 * rows * width + 14 * full * kv_width,
            transcendentals=rows * full * width // HEAD_DIM,
        ),
    )(
        query_order,
        key_order,
        queries,
        dmixed,
        mixed,
        logs,
        cosine.T,
        sine.T,
        keys,
        values,
        keys.T,
    )


def fold_steps(dp_size, ctx_size):
    steps = []
    bit = 1
    while bit < ctx_size:
        steps.append(("ctx", bit))
        bit *= 2
    along = []
    bit = 2
    while bit < dp_size:
        along.append(("dp", bit))
        bit *= 2
    even, odd = steps + along, along + steps
    plan = [((("dp", 1)), (("dp", 1)))] if dp_size > 1 else []
    return plan + list(zip(even, odd))


def step_perm(step, dp_size, ctx_size):
    pairs = []
    for d in range(dp_size):
        for c in range(ctx_size):
            axis, bit = step[d % 2]
            other = (d ^ bit, c) if axis == "dp" else (d, c ^ bit)
            pairs.append((d * ctx_size + c, other[0] * ctx_size + other[1]))
    return pairs


def step_bit(step):
    d, c = lax.axis_index("dp"), lax.axis_index("ctx")

    def of(axis, bit):
        return jnp.where(((d if axis == "dp" else c) & bit) != 0, 1, 0)

    return jnp.where(d % 2 == 0, of(*step[0]), of(*step[1]))


def sum_plane(grad, dp_size, ctx_size):
    plan = fold_steps(dp_size, ctx_size)
    pieces = grad
    perms = [step_perm(s, dp_size, ctx_size) for s in plan]
    bits = [step_bit(s) for s in plan]
    for perm, bit in zip(perms, bits):
        half = pieces.shape[0] // 2
        kept = lax.dynamic_slice_in_dim(pieces, bit * half, half, 0)
        sent = lax.dynamic_slice_in_dim(pieces, (1 - bit) * half, half, 0).astype(BF16)
        pieces = kept.astype(F32) + lax.ppermute(sent, ("dp", "ctx"), perm).astype(F32)
        if perm is not perms[-1]:
            pieces = pieces.astype(BF16)
    pieces = pieces.astype(BF16)
    for perm, bit in zip(perms[::-1], bits[::-1]):
        other = lax.ppermute(pieces, ("dp", "ctx"), perm)
        pieces = jnp.where(
            bit == 0,
            jnp.concatenate([pieces, other], 0),
            jnp.concatenate([other, pieces], 0),
        )
    return pieces.astype(F32)


LINE_CHUNK = 32


def line_kernel(size, chunk, streams, owners, side_count, out_count, *refs):
    parts, refs = refs[:streams], refs[streams:]
    sides, refs = refs[:side_count], refs[side_count:]
    shared, refs = refs[:streams], refs[streams:]
    kept, refs = refs[:out_count], refs[out_count:]
    inbox, send_up, recv_up, send_back, recv_back = refs
    half = parts[0].shape[0] // 2
    count = half // chunk
    last = size - 1
    me = lax.axis_index("tensor")
    above, below = jnp.minimum(me + 1, last), jnp.maximum(me - 1, 0)
    flows = ((me, above, below), (last - me, below, above))

    barrier = pltpu.get_barrier_semaphore()

    def greet(other):
        pl.semaphore_signal(
            barrier, inc=1, device_id={"tensor": other}, device_id_type=pl.DeviceIdType.MESH
        )

    pl.when(me < last)(lambda: greet(above))
    pl.when(me > 0)(lambda: greet(below))
    pl.semaphore_wait(barrier, jnp.where((me > 0) & (me < last), 2, 1))

    def place(f, i):
        return pl.ds(pl.multiple_of(f * half + i * chunk, chunk), chunk)

    def local(i):
        return pl.ds(pl.multiple_of(i * chunk, chunk), chunk)

    def onward(k, f, i, source):
        return pltpu.make_async_remote_copy(
            src_ref=source,
            dst_ref=inbox.at[k, f, local(i)],
            send_sem=send_up.at[k, f, i],
            recv_sem=recv_up.at[k, f, i],
            device_id={"tensor": flows[f][1]},
            device_id_type=pl.DeviceIdType.MESH,
        )

    def backward(k, f, i):
        block = shared[k].at[place(f, i)]
        return pltpu.make_async_remote_copy(
            src_ref=block,
            dst_ref=block,
            send_sem=send_back.at[k, f, i],
            recv_sem=recv_back.at[k, f, i],
            device_id={"tensor": flows[f][2]},
            device_id_type=pl.DeviceIdType.MESH,
        )

    def reduce_chunk(k, f, i):
        position = flows[f][0]
        mine = parts[k].at[place(f, i)]
        slot = inbox.at[k, f, local(i)]

        @pl.when(position == 0)
        def _():
            onward(k, f, i, mine).start()

        @pl.when(position > 0)
        def _():
            onward(k, f, i, slot).wait_recv()
            total = slot[...].astype(F32) + mine[...].astype(F32)

            @pl.when(position < last)
            def _():
                slot[...] = total.astype(BF16)
                onward(k, f, i, slot).start()

            @pl.when(position == last)
            def _():
                result = owners[k](total, place(f, i), local(i), sides, kept)
                shared[k][place(f, i), :] = result.astype(BF16)
                backward(k, f, i).start()

    def pass_back(k, f, i):
        position = flows[f][0]

        @pl.when((position < last) & (i >= 0) & (i < count))
        def _():
            backward(k, f, i).wait_recv()
            pl.when(position > 0)(lambda: backward(k, f, i).start())

    def step(s, carry):
        @pl.when(s < count)
        def _():
            for k in range(streams):
                for f in range(2):
                    reduce_chunk(k, f, s)

        for k in range(streams):
            for f in range(2):
                pass_back(k, f, s - 2 * (last - flows[f][0]))
        return carry

    for ref in kept:
        if ref.shape[0] == 1:
            ref[...] = jnp.zeros_like(ref)
    lax.fori_loop(0, count + 2 * last, step, 0)

    def drain(i, carry):
        for k in range(streams):
            for f in range(2):
                position = flows[f][0]
                pl.when(position < last)(
                    lambda: onward(k, f, i, inbox.at[k, f, local(i)]).wait_send()
                )
                pl.when(position > 0)(lambda: backward(k, f, i).wait_send())
        return carry

    lax.fori_loop(0, count, drain, 0)


def line_sum(parts, owners, sides, kept, collective_id):
    rows, width = parts[0].shape
    size = lax.axis_size("tensor")
    streams = len(parts)
    chunk = min(LINE_CHUNK, rows // 2)
    count = rows // 2 // chunk
    whole = pl.BlockSpec(memory_space=pltpu.VMEM)
    scalar = pl.BlockSpec(memory_space=pltpu.SMEM)
    sems = pltpu.SemaphoreType.DMA((streams, 2, count))
    outs = [jax.ShapeDtypeStruct((rows, width), BF16)] * streams + list(kept)
    return pl.pallas_call(
        functools.partial(line_kernel, size, chunk, streams, owners, len(sides), len(kept)),
        out_shape=outs,
        in_specs=[whole] * streams + [scalar if s.ndim == 1 else whole for s in sides],
        out_specs=[whole] * len(outs),
        scratch_shapes=[pltpu.VMEM((streams, 2, rows // 2, width), BF16)] + [sems] * 4,
        compiler_params=pltpu.CompilerParams(
            collective_id=collective_id, has_side_effects=True, vmem_limit_bytes=56 * 2**20
        ),
        cost_estimate=pl.CostEstimate(
            flops=streams * rows * width,
            bytes_accessed=streams * 300 * 2**20,
            transcendentals=0,
        ),
    )(*parts, *sides)


def unit_of(rows):
    inverse = lax.rsqrt(jnp.mean(rows * rows, axis=-1, keepdims=True) + EPSILON)
    return rows * inverse, inverse


def own_hidden(total, where, here, sides, kept):
    x_ref, gain_ref = sides
    hidden = x_ref[where, :].astype(F32) + total
    kept[0][here, :] = hidden
    return unit_of(hidden)[0] * gain_ref[...]


def own_dhidden(total, where, here, sides, kept):
    hidden_ref, cot_ref, gain_ref, factor = sides
    unit, inverse = unit_of(hidden_ref[here, :])
    kept[1][...] += jnp.sum(total * unit, axis=0, keepdims=True)
    dhidden = norm_back(total, unit, inverse, gain_ref[...])
    kept[0][here, :] = dhidden
    return cot_ref[where, :].astype(F32) * factor[0] + dhidden


def own_dinput(total, where, here, sides, kept):
    x_ref, hidden_ref, dhidden_ref, gain_ref, factor = sides
    unit, inverse = unit_of(x_ref[where, :].astype(F32))
    kept[0][...] += jnp.sum(total * unit, axis=0, keepdims=True)
    return dhidden_ref[here, :] + norm_back(total, unit, inverse, gain_ref[...])


def own_output(total, where, here, sides, kept):
    x_ref, hidden_ref, dhidden_ref, gain_ref, factor = sides
    x = x_ref[where, :].astype(F32)
    return x + factor[0] * ((hidden_ref[here, :] - x) + total)


def sequence_positions(order_row, length):
    spans = order_row.shape[0]
    stride = length // spans
    places = jnp.arange(length, dtype=jnp.int32)
    onehot = (places // stride)[:, None] == jnp.arange(spans, dtype=jnp.int32)[None, :]
    starts = jnp.sum(jnp.where(onehot, order_row[None, :], 0), axis=1)
    return starts * stride + places % stride


def rotary_tables(positions):
    inverse = 1.0 / 10000.0 ** (jnp.arange(0, HEAD_DIM, 2, dtype=F32) / HEAD_DIM)
    angle = positions.astype(F32)[:, None] * inverse[None, :]
    return (jnp.cos(angle), jnp.sin(angle))


def rotate(field, cosine, sine):
    half = field.shape[-1] // 2
    leading, trailing = (field[..., :half], field[..., half:])
    cosine, sine = (cosine[:, None, :], sine[:, None, :])
    return jnp.concatenate(
        [leading * cosine - trailing * sine, trailing * cosine + leading * sine], axis=-1
    )


def rotate_back(grad, cosine, sine):
    return rotate(grad, cosine, -sine)


def contract_rows(left, right):
    return jnp.einsum("rd,rf->df", left, right, preferred_element_type=F32)


def contract_cols(left, right):
    return jnp.einsum("rc,dc->rd", left, right, preferred_element_type=F32)


def norm_back(dnormed, unit, inverse, gain):
    scaled = dnormed * gain
    return inverse * (scaled - unit * jnp.mean(scaled * unit, axis=-1, keepdims=True))


def swap_ctx(part, ctx_size):
    return [
        lax.ppermute(part, "ctx", [(i, (i + s) % ctx_size) for i in range(ctx_size)])
        for s in range(1, ctx_size)
    ]


def per_device(
    inputs,
    cotangent,
    skip_mask,
    group_ids,
    span_order,
    exit_scale,
    attn_gain,
    ffn_gain,
    w_query,
    w_key,
    w_value,
    w_output,
    w_gate,
    w_up,
    w_down,
):
    _, rows, width = inputs.shape
    dp_size, ctx_size = lax.axis_size("dp"), lax.axis_size("ctx")
    full_len = rows * ctx_size
    spans = span_order.shape[1]
    span = full_len // spans
    kv_local = w_key.shape[1] // HEAD_DIM
    ctx = lax.axis_index("ctx")
    offset = ctx * rows
    positions = lax.dynamic_slice_in_dim(sequence_positions(span_order[0], full_len), offset, rows)
    cosine, sine = rotary_tables(positions)
    keep = skip_mask[0].astype(F32)
    scale = jnp.where(group_ids[0] == 1, exit_scale[1], exit_scale[0])

    own_spans = spans // ctx_size
    orders = [
        lax.dynamic_slice_in_dim(span_order[0], ((ctx - s) % ctx_size) * own_spans, own_spans)
        for s in range(ctx_size)
    ]
    query_order, key_order = orders[0], jnp.concatenate(orders)

    x_low = inputs[0]
    flat = x_low.astype(F32)
    inv_one = lax.rsqrt(jnp.mean(flat * flat, axis=-1, keepdims=True) + EPSILON)
    normed_one = (flat * inv_one * attn_gain).astype(BF16)
    k_proj = nn_dot(normed_one, w_key).reshape(rows, kv_local, HEAD_DIM)
    keys_own = rotate(k_proj, cosine, sine).astype(BF16).reshape(rows, -1)
    values_own = nn_dot(normed_one, w_value).astype(BF16)
    keys = jnp.concatenate([keys_own] + swap_ctx(keys_own, ctx_size), 0)
    values = jnp.concatenate([values_own] + swap_ctx(values_own, ctx_size), 0)
    q_proj = nn_dot(normed_one, w_query).reshape(rows, -1, HEAD_DIM)
    queries = rotate(q_proj, cosine, sine).astype(BF16).reshape(rows, -1)
    mixed, logs = attend(queries, keys, values, query_order, key_order, span)

    half_rows = jax.ShapeDtypeStruct((rows // 2, width), F32)
    gain_row = jax.ShapeDtypeStruct((1, width), F32)
    ffn_row, attn_row = ffn_gain[None, :], attn_gain[None, :]
    attn_part = nn_dot(mixed, w_output).astype(BF16)
    normed_two, hidden = line_sum(
        [attn_part], [own_hidden], [x_low, ffn_row], [half_rows], 1
    )

    dscaled = cotangent[0].astype(F32) * scale
    dffn = (keep * dscaled).astype(BF16)
    dacted = contract_cols(dffn, w_down)
    gate = nn_dot(normed_two, w_gate)
    upward = nn_dot(normed_two, w_up)
    sigmoid_gate = jax.nn.sigmoid(gate)
    silu_gate = gate * sigmoid_gate
    acted = (silu_gate * upward).astype(BF16)
    dgate = (dacted * upward * sigmoid_gate * (1.0 + gate * (1.0 - sigmoid_gate))).astype(BF16)
    dupward = (dacted * silu_gate).astype(BF16)
    dnormed_part = (contract_cols(dgate, w_gate) + contract_cols(dupward, w_up)).astype(BF16)
    ffn_part = nn_dot(acted, w_down).astype(BF16)
    total = lambda g: sum_plane(g, dp_size, ctx_size)
    grad_down = total(contract_rows(acted, dffn))
    grad_gate = total(contract_rows(normed_two, dgate))
    grad_up = total(contract_rows(normed_two, dupward))
    dattn, dhidden, grad_ffn_gain = line_sum(
        [dnormed_part],
        [own_dhidden],
        [hidden, cotangent[0], ffn_row, (keep * scale)[None]],
        [half_rows, gain_row],
        2,
    )
    grad_output = total(contract_rows(mixed, dattn))
    dmixed = contract_cols(dattn, w_output).astype(BF16)

    dq_proj, dkeys, dvalues = attend_back(
        queries, dmixed, mixed, logs, cosine, sine, keys, values, query_order, key_order, span
    )

    def collect(grad):
        parts = grad.reshape(ctx_size, rows, -1)
        summed = parts[0]
        for s in range(1, ctx_size):
            back = [(i, (i - s) % ctx_size) for i in range(ctx_size)]
            summed = summed + lax.ppermute(parts[s].astype(BF16), "ctx", back).astype(F32)
        return summed

    dk_own = collect(dkeys).reshape(rows, kv_local, HEAD_DIM)
    dk_proj = rotate_back(dk_own, cosine, sine).reshape(rows, -1).astype(BF16)
    dv_proj = collect(dvalues).astype(BF16)
    dnormed_one = (
        contract_cols(dq_proj, w_query)
        + contract_cols(dk_proj, w_key)
        + contract_cols(dv_proj, w_value)
    ).astype(BF16)
    grad_query = total(contract_rows(normed_one, dq_proj))
    grad_key = total(contract_rows(normed_one, dk_proj))
    grad_value = total(contract_rows(normed_one, dv_proj))
    through, output, grad_attn_gain = line_sum(
        [dnormed_one, ffn_part],
        [own_dinput, own_output],
        [x_low, hidden, dhidden, attn_row, keep[None]],
        [gain_row],
        3,
    )
    grad_attn_gain, grad_ffn_gain = lax.psum(
        (grad_attn_gain[0], grad_ffn_gain[0]), ("dp", "ctx", "tensor")
    )
    input_grad = dscaled + through.astype(F32)
    return (
        output.reshape(inputs.shape),
        input_grad.reshape(inputs.shape),
        grad_attn_gain,
        grad_ffn_gain,
        grad_query,
        grad_key,
        grad_value,
        grad_output,
        grad_gate,
        grad_up,
        grad_down,
    )


def solution(mesh):
    rows = P("dp", "ctx", None)
    by_column, by_row = P(None, "tensor"), P("tensor", None)
    in_specs = (rows, rows, P("dp"), P("dp"), P("dp", None), P(), P(), P())
    in_specs += (by_column,) * 3 + (by_row,) + (by_column,) * 2 + (by_row,)
    out_specs = (rows, rows, P(), P()) + (by_column,) * 3 + (by_row,) + (by_column,) * 2 + (by_row,)
    return jax.shard_map(
        per_device, mesh=mesh, in_specs=in_specs, out_specs=out_specs, check_vma=False
    )
```

```python
import functools

import jax
import jax.numpy as jnp
from jax import lax
from jax.experimental import pallas as pl
from jax.experimental.pallas import tpu as pltpu
from jax.sharding import PartitionSpec as P

HEAD_DIM = 128
EPSILON = 1e-05
NEG_BIG = -1e30
FACTOR = HEAD_DIM ** (-0.5)
LOG2E = 1.4426950408889634
QUERY_BLOCK = 256
BF16 = jnp.bfloat16
F32 = jnp.float32

NT = (((1,), (1,)), ((), ()))


def nt_dot(left, right):
    return lax.dot_general(left, right, NT, preferred_element_type=F32)


def nn_dot(left, right):
    return jnp.dot(left, right, preferred_element_type=F32)


def stack_heads(block, group):
    return jnp.concatenate(
        [block[:, h * HEAD_DIM : (h + 1) * HEAD_DIM] for h in range(group)], axis=0
    )


def hide_later(scores, first_row, rows, fill):
    key_row = lax.broadcasted_iota(jnp.int32, scores.shape, 0)
    query_row = lax.broadcasted_iota(jnp.int32, scores.shape, 1) % rows + first_row
    return jnp.where(key_row <= query_row, scores, fill)


def attend_kernel(
    group, span, query_order, key_order, q_ref, k_ref, vt_ref, o_ref, lse_ref, top, total, acc
):
    rows = q_ref.shape[0]
    step = pl.program_id(1)
    first = step * rows
    order = query_order[first // span]
    queries = stack_heads(q_ref[...], group)
    top[...] = jnp.full_like(top, NEG_BIG)
    total[...] = jnp.zeros_like(total)
    acc[...] = jnp.zeros_like(acc)

    def visit(place, diagonal):
        keys = k_ref[pl.ds(place, span), :]
        scores = nt_dot(keys, queries) * (FACTOR * LOG2E)
        if diagonal:
            scores = hide_later(scores, first % span, rows, NEG_BIG)
        before = top[...]
        now = jnp.maximum(before, jnp.max(scores, axis=0, keepdims=True))
        weights = jnp.exp2(scores - now)
        shrink = jnp.exp2(before - now)
        top[...] = now
        total[...] = total[...] * shrink + jnp.sum(weights, axis=0, keepdims=True)
        acc[...] = acc[...] * shrink + nn_dot(
            vt_ref[:, pl.ds(place, span)], weights.astype(BF16)
        )

    def one_span(j, carry):
        place = pl.multiple_of(j * span, span)
        pl.when(key_order[j] < order)(lambda: visit(place, False))
        pl.when(key_order[j] == order)(lambda: visit(place, True))
        return carry

    lax.fori_loop(0, k_ref.shape[0] // span, one_span, 0)
    mixed = acc[...] / total[...]
    logs = top[...] + jnp.log2(total[...])
    for h in range(group):
        part = slice(h * rows, (h + 1) * rows)
        o_ref[:, h * HEAD_DIM : (h + 1) * HEAD_DIM] = mixed[:, part].T.astype(BF16)
        lse_ref[0, h : h + 1, :] = logs[:, part]


def attend(queries, keys, values, query_order, key_order, span):
    rows, width = queries.shape
    full, kv_width = keys.shape
    kv_heads = kv_width // HEAD_DIM
    group = width // kv_width
    block = min(QUERY_BLOCK, span)
    query_spec = pl.BlockSpec((block, group * HEAD_DIM), lambda g, i, *_: (i, g))
    return pl.pallas_call(
        functools.partial(attend_kernel, group, span),
        grid_spec=pltpu.PrefetchScalarGridSpec(
            num_scalar_prefetch=2,
            grid=(kv_heads, rows // block),
            in_specs=[
                query_spec,
                pl.BlockSpec((full, HEAD_DIM), lambda g, i, *_: (0, g)),
                pl.BlockSpec((HEAD_DIM, full), lambda g, i, *_: (g, 0)),
            ],
            out_specs=[
                query_spec,
                pl.BlockSpec((1, group, block), lambda g, i, *_: (g, 0, i)),
            ],
            scratch_shapes=[
                pltpu.VMEM((1, group * block), F32),
                pltpu.VMEM((1, group * block), F32),
                pltpu.VMEM((HEAD_DIM, group * block), F32),
            ],
        ),
        out_shape=[
            jax.ShapeDtypeStruct((rows, width), BF16),
            jax.ShapeDtypeStruct((kv_heads, group, rows), F32),
        ],
        compiler_params=pltpu.CompilerParams(vmem_limit_bytes=32 * 2**20),
        cost_estimate=pl.CostEstimate(
            flops=4 * rows * full * width,
            bytes_accessed=4 * rows * width + 4 * full * kv_width,
            transcendentals=rows * full * width // HEAD_DIM,
        ),
    )(query_order, key_order, queries, keys, values.T)


def attend_back_kernel(
    group,
    span,
    query_order,
    key_order,
    q_ref,
    do_ref,
    o_ref,
    lse_ref,
    cos_ref,
    sin_ref,
    k_ref,
    v_ref,
    kt_ref,
    dq_ref,
    dk_ref,
    dv_ref,
    acc,
):
    rows = q_ref.shape[0]
    step = pl.program_id(1)
    first = step * rows
    order = query_order[first // span]
    queries = stack_heads(q_ref[...], group)
    dmixed = stack_heads(do_ref[...], group)
    mixed = stack_heads(o_ref[...], group)
    product = dmixed.astype(F32) * mixed.astype(F32)
    delta = jnp.sum(product.T, axis=0, keepdims=True)
    logs = jnp.concatenate([lse_ref[0, h : h + 1, :] for h in range(group)], axis=1)
    acc[...] = jnp.zeros_like(acc)

    @pl.when(step == 0)
    def _():
        dk_ref[...] = jnp.zeros_like(dk_ref)
        dv_ref[...] = jnp.zeros_like(dv_ref)

    def visit(place, diagonal):
        here = pl.ds(place, span)
        scores = nt_dot(k_ref[here, :], queries) * (FACTOR * LOG2E)
        probs = jnp.exp2(scores - logs)
        if diagonal:
            probs = hide_later(probs, first % span, rows, 0.0)
        dprobs = nt_dot(v_ref[here, :], dmixed)
        dscore = (probs * (dprobs - delta)).astype(BF16)
        dv_ref[here, :] += nn_dot(probs.astype(BF16), dmixed)
        dk_ref[here, :] += nn_dot(dscore, queries)
        acc[...] += nn_dot(kt_ref[:, here], dscore)

    def one_span(j, carry):
        place = pl.multiple_of(j * span, span)
        pl.when(key_order[j] < order)(lambda: visit(place, False))
        pl.when(key_order[j] == order)(lambda: visit(place, True))
        return carry

    lax.fori_loop(0, k_ref.shape[0] // span, one_span, 0)
    half = HEAD_DIM // 2
    cosine, sine = cos_ref[...], sin_ref[...]
    for h in range(group):
        grad = acc[:, h * rows : (h + 1) * rows] * FACTOR
        leading, trailing = grad[:half], grad[half:]
        turned = jnp.concatenate(
            [leading * cosine + trailing * sine, trailing * cosine - leading * sine], axis=0
        )
        dq_ref[:, h * HEAD_DIM : (h + 1) * HEAD_DIM] = turned.T.astype(BF16)

    @pl.when(step == pl.num_programs(1) - 1)
    def _():
        dk_ref[...] = dk_ref[...] * FACTOR


def attend_back(
    queries, dmixed, mixed, logs, cosine, sine, keys, values, query_order, key_order, span
):
    rows, width = queries.shape
    full, kv_width = keys.shape
    kv_heads = kv_width // HEAD_DIM
    group = width // kv_width
    block = min(QUERY_BLOCK, span)
    half = HEAD_DIM // 2
    query_spec = pl.BlockSpec((block, group * HEAD_DIM), lambda g, i, *_: (i, g))
    key_spec = pl.BlockSpec((full, HEAD_DIM), lambda g, i, *_: (0, g))
    table_spec = pl.BlockSpec((half, block), lambda g, i, *_: (0, i))
    return pl.pallas_call(
        functools.partial(attend_back_kernel, group, span),
        grid_spec=pltpu.PrefetchScalarGridSpec(
            num_scalar_prefetch=2,
            grid=(kv_heads, rows // block),
            in_specs=[
                query_spec,
                query_spec,
                query_spec,
                pl.BlockSpec((1, group, block), lambda g, i, *_: (g, 0, i)),
                table_spec,
                table_spec,
                key_spec,
                key_spec,
                pl.BlockSpec((HEAD_DIM, full), lambda g, i, *_: (g, 0)),
            ],
            out_specs=[query_spec, key_spec, key_spec],
            scratch_shapes=[pltpu.VMEM((HEAD_DIM, group * block), F32)],
        ),
        out_shape=[
            jax.ShapeDtypeStruct((rows, width), BF16),
            jax.ShapeDtypeStruct((full, kv_width), F32),
            jax.ShapeDtypeStruct((full, kv_width), F32),
        ],
        compiler_params=pltpu.CompilerParams(vmem_limit_bytes=32 * 2**20),
        cost_estimate=pl.CostEstimate(
            flops=10 * rows * full * width,
            bytes_accessed=8 * rows * width + 14 * full * kv_width,
            transcendentals=rows * full * width // HEAD_DIM,
        ),
    )(
        query_order,
        key_order,
        queries,
        dmixed,
        mixed,
        logs,
        cosine.T,
        sine.T,
        keys,
        values,
        keys.T,
    )


LINE_CHUNK = 32
LINE_WINDOW = 2
LINE_SKEW = 2
MESH_AXES = ("dp", "ctx", "tensor")


def pair_steps(sizes):
    steps = []
    for axis, size in zip(MESH_AXES, sizes):
        bit = 1
        while bit < size:
            steps.append((axis, bit))
            bit *= 2
    return steps


def partner(axis, bit):
    index = lax.axis_index(axis)
    return jnp.where((index // bit) % 2 == 0, index + bit, index - bit)


def line_kernel(size, chunk, streams, owners, pairs, side_count, out_count, *refs):
    parts, refs = refs[:streams], refs[streams:]
    sides, refs = refs[:side_count], refs[side_count:]
    shared, refs = refs[:streams], refs[streams:]
    kept, refs = refs[:out_count], refs[out_count:]
    inbox, send_up, recv_up, send_back, recv_back = refs[:5]
    half = parts[0].shape[0] // 2
    count = half // chunk
    last = size - 1
    me = lax.axis_index("tensor")
    above, below = jnp.minimum(me + 1, last), jnp.maximum(me - 1, 0)
    flows = ((me, above, below), (last - me, below, above))

    barrier = pltpu.get_barrier_semaphore()

    def greet(axis, other):
        pl.semaphore_signal(
            barrier, inc=1, device_id={axis: other}, device_id_type=pl.DeviceIdType.MESH
        )

    if pairs:
        for axis, bit in pairs:
            greet(axis, partner(axis, bit))
        far_above = jnp.where(me % 2 == 0, 0, 1) * jnp.where(me < last, 1, 0)
        far_below = jnp.where(me % 2 == 0, 1, 0) * jnp.where(me > 0, 1, 0)
        pl.when(far_above == 1)(lambda: greet("tensor", above))
        pl.when(far_below == 1)(lambda: greet("tensor", below))
        pl.semaphore_wait(barrier, len(pairs) + far_above + far_below)
    else:
        pl.when(me < last)(lambda: greet("tensor", above))
        pl.when(me > 0)(lambda: greet("tensor", below))
        pl.semaphore_wait(barrier, jnp.where((me > 0) & (me < last), 2, 1))

    def place(f, i):
        return pl.ds(pl.multiple_of(f * half + i * chunk, chunk), chunk)

    def local(i):
        return pl.ds(pl.multiple_of(i * chunk, chunk), chunk)

    def onward(k, f, i, source):
        return pltpu.make_async_remote_copy(
            src_ref=source,
            dst_ref=inbox.at[k, f, local(i)],
            send_sem=send_up.at[k, f, i],
            recv_sem=recv_up.at[k, f, i],
            device_id={"tensor": flows[f][1]},
            device_id_type=pl.DeviceIdType.MESH,
        )

    def backward(k, f, i):
        block = shared[k].at[place(f, i)]
        return pltpu.make_async_remote_copy(
            src_ref=block,
            dst_ref=block,
            send_sem=send_back.at[k, f, i],
            recv_sem=recv_back.at[k, f, i],
            device_id={"tensor": flows[f][2]},
            device_id_type=pl.DeviceIdType.MESH,
        )

    def reduce_chunk(k, f, i):
        position = flows[f][0]
        mine = parts[k].at[place(f, i)]
        slot = inbox.at[k, f, local(i)]

        @pl.when(position == 0)
        def _():
            pl.when(i >= LINE_WINDOW)(lambda: onward(k, f, i - LINE_WINDOW, mine).wait_send())
            onward(k, f, i, mine).start()

        @pl.when(position > 0)
        def _():
            onward(k, f, i, slot).wait_recv()
            total = slot[...].astype(F32) + mine[...].astype(F32)

            @pl.when(position < last)
            def _():
                slot[...] = total.astype(BF16)
                onward(k, f, i, slot).start()

            @pl.when(position == last)
            def _():
                result = owners[k](total, place(f, i), local(i), sides, kept)
                shared[k][place(f, i), :] = result.astype(BF16)
                backward(k, f, i).start()

    def pass_back(k, f, i):
        position = flows[f][0]

        @pl.when((position < last) & (i >= 0) & (i < count))
        def _():
            backward(k, f, i).wait_recv()
            pl.when(position > 0)(lambda: backward(k, f, i).start())

    def step(s, carry):
        for k in range(streams):
            for f in range(2):
                i = s - LINE_SKEW * flows[f][0]
                pl.when((i >= 0) & (i < count))(lambda: reduce_chunk(k, f, i))
        for k in range(streams):
            for f in range(2):
                pass_back(k, f, s - LINE_SKEW * (2 * last - flows[f][0]))
        return carry

    if not pairs:
        for ref in kept[1:]:
            ref[...] = jnp.zeros_like(ref)
    else:
        gains = kept[0]
        gains[...] = jnp.zeros_like(gains)
        gains[1:2, :] = sides[-1][...]
    lax.fori_loop(0, count + 2 * LINE_SKEW * last, step, 0)

    def drain(i, carry):
        for k in range(streams):
            for f in range(2):
                position = flows[f][0]
                waited = (position == 0) & (i < count - LINE_WINDOW)
                pl.when((position < last) & ~waited)(
                    lambda: onward(k, f, i, inbox.at[k, f, local(i)]).wait_send()
                )
                pl.when(position > 0)(lambda: backward(k, f, i).wait_send())
        return carry

    lax.fori_loop(0, count, drain, 0)

    if pairs:
        slots, sums, send_pair, recv_pair = refs[5:]
        sums[0] = gains[...]
        for n, (axis, bit) in enumerate(pairs):
            copy = pltpu.make_async_remote_copy(
                src_ref=sums.at[n],
                dst_ref=slots.at[n],
                send_sem=send_pair.at[n],
                recv_sem=recv_pair.at[n],
                device_id={axis: partner(axis, bit)},
                device_id_type=pl.DeviceIdType.MESH,
            )
            copy.start()
            copy.wait()
            sums[n + 1] = sums[n] + slots[n]
        gains[...] = sums[len(pairs)]


def line_sum(parts, owners, sides, kept, collective_id, pairs=()):
    rows, width = parts[0].shape
    size = lax.axis_size("tensor")
    streams = len(parts)
    chunk = min(LINE_CHUNK, rows // 2)
    count = rows // 2 // chunk
    whole = pl.BlockSpec(memory_space=pltpu.VMEM)
    scalar = pl.BlockSpec(memory_space=pltpu.SMEM)
    sems = pltpu.SemaphoreType.DMA((streams, 2, count))
    outs = [jax.ShapeDtypeStruct((rows, width), BF16)] * streams + list(kept)
    extra = []
    if pairs:
        pair_sems = pltpu.SemaphoreType.DMA((len(pairs),))
        extra = [
            pltpu.VMEM((len(pairs), 8, width), F32),
            pltpu.VMEM((len(pairs) + 1, 8, width), F32),
            pair_sems,
            pair_sems,
        ]
    return pl.pallas_call(
        functools.partial(
            line_kernel, size, chunk, streams, owners, pairs, len(sides), len(kept)
        ),
        out_shape=outs,
        in_specs=[whole] * streams + [scalar if s.ndim == 1 else whole for s in sides],
        out_specs=[whole] * len(outs),
        scratch_shapes=[pltpu.VMEM((streams, 2, rows // 2, width), BF16)] + [sems] * 4 + extra,
        compiler_params=pltpu.CompilerParams(
            collective_id=collective_id, has_side_effects=True, vmem_limit_bytes=56 * 2**20
        ),
        cost_estimate=pl.CostEstimate(
            flops=streams * rows * width,
            bytes_accessed=streams * 300 * 2**20,
            transcendentals=0,
        ),
    )(*parts, *sides)


def unit_of(rows):
    inverse = lax.rsqrt(jnp.mean(rows * rows, axis=-1, keepdims=True) + EPSILON)
    return rows * inverse, inverse


def own_hidden(total, where, here, sides, kept):
    x_ref, gain_ref = sides
    hidden = x_ref[where, :].astype(F32) + total
    kept[0][here, :] = hidden
    return unit_of(hidden)[0] * gain_ref[...]


def own_dhidden(total, where, here, sides, kept):
    x_ref, hidden_ref, cot_ref, gain_ref, factor = sides
    unit, inverse = unit_of(hidden_ref[here, :])
    kept[1][...] += jnp.sum(total * unit, axis=0, keepdims=True)
    dhidden = norm_back(total, unit, inverse, gain_ref[...])
    kept[0][here, :] = dhidden
    return cot_ref[where, :].astype(F32) * factor[0] + dhidden


def own_output(total, where, here, sides, kept):
    x_ref, hidden_ref, cot_ref, gain_ref, factor = sides
    x = x_ref[where, :].astype(F32)
    return x + factor[1] * ((hidden_ref[here, :] - x) + total)


def own_dinput(total, where, here, sides, kept):
    x_ref, dhidden_ref, gain_ref, _ = sides
    unit, inverse = unit_of(x_ref[where, :].astype(F32))
    kept[0][0:1, :] += jnp.sum(total * unit, axis=0, keepdims=True)
    return dhidden_ref[here, :] + norm_back(total, unit, inverse, gain_ref[...])


def sequence_positions(order_row, length):
    spans = order_row.shape[0]
    stride = length // spans
    places = jnp.arange(length, dtype=jnp.int32)
    onehot = (places // stride)[:, None] == jnp.arange(spans, dtype=jnp.int32)[None, :]
    starts = jnp.sum(jnp.where(onehot, order_row[None, :], 0), axis=1)
    return starts * stride + places % stride


def rotary_tables(positions):
    inverse = 1.0 / 10000.0 ** (jnp.arange(0, HEAD_DIM, 2, dtype=F32) / HEAD_DIM)
    angle = positions.astype(F32)[:, None] * inverse[None, :]
    return (jnp.cos(angle), jnp.sin(angle))


def rotate(field, cosine, sine):
    half = field.shape[-1] // 2
    leading, trailing = (field[..., :half], field[..., half:])
    cosine, sine = (cosine[:, None, :], sine[:, None, :])
    return jnp.concatenate(
        [leading * cosine - trailing * sine, trailing * cosine + leading * sine], axis=-1
    )


def rotate_back(grad, cosine, sine):
    return rotate(grad, cosine, -sine)


def contract_rows(left, right):
    return jnp.einsum("rd,rf->df", left, right, preferred_element_type=F32)


def contract_cols(left, right):
    return jnp.einsum("rc,dc->rd", left, right, preferred_element_type=F32)


def norm_back(dnormed, unit, inverse, gain):
    scaled = dnormed * gain
    return inverse * (scaled - unit * jnp.mean(scaled * unit, axis=-1, keepdims=True))


def swap_ctx(part, ctx_size):
    return [
        lax.ppermute(part, "ctx", [(i, (i + s) % ctx_size) for i in range(ctx_size)])
        for s in range(1, ctx_size)
    ]


def per_device(
    inputs,
    cotangent,
    skip_mask,
    group_ids,
    span_order,
    exit_scale,
    attn_gain,
    ffn_gain,
    w_query,
    w_key,
    w_value,
    w_output,
    w_gate,
    w_up,
    w_down,
):
    _, rows, width = inputs.shape
    dp_size, ctx_size = lax.axis_size("dp"), lax.axis_size("ctx")
    full_len = rows * ctx_size
    spans = span_order.shape[1]
    span = full_len // spans
    kv_local = w_key.shape[1] // HEAD_DIM
    ctx = lax.axis_index("ctx")
    offset = ctx * rows
    positions = lax.dynamic_slice_in_dim(sequence_positions(span_order[0], full_len), offset, rows)
    cosine, sine = rotary_tables(positions)
    keep = skip_mask[0].astype(F32)
    scale = jnp.where(group_ids[0] == 1, exit_scale[1], exit_scale[0])

    own_spans = spans // ctx_size
    orders = [
        lax.dynamic_slice_in_dim(span_order[0], ((ctx - s) % ctx_size) * own_spans, own_spans)
        for s in range(ctx_size)
    ]
    query_order, key_order = orders[0], jnp.concatenate(orders)

    x_low = inputs[0]
    flat = x_low.astype(F32)
    inv_one = lax.rsqrt(jnp.mean(flat * flat, axis=-1, keepdims=True) + EPSILON)
    normed_one = (flat * inv_one * attn_gain).astype(BF16)
    k_proj = nn_dot(normed_one, w_key).reshape(rows, kv_local, HEAD_DIM)
    keys_own = rotate(k_proj, cosine, sine).astype(BF16).reshape(rows, -1)
    values_own = nn_dot(normed_one, w_value).astype(BF16)
    keys = jnp.concatenate([keys_own] + swap_ctx(keys_own, ctx_size), 0)
    values = jnp.concatenate([values_own] + swap_ctx(values_own, ctx_size), 0)
    q_proj = nn_dot(normed_one, w_query).reshape(rows, -1, HEAD_DIM)
    queries = rotate(q_proj, cosine, sine).astype(BF16).reshape(rows, -1)
    mixed, logs = attend(queries, keys, values, query_order, key_order, span)

    half_rows = jax.ShapeDtypeStruct((rows // 2, width), F32)
    gain_row = jax.ShapeDtypeStruct((1, width), F32)
    ffn_row, attn_row = ffn_gain[None, :], attn_gain[None, :]
    attn_part = nn_dot(mixed, w_output).astype(BF16)
    normed_two, hidden = line_sum(
        [attn_part], [own_hidden], [x_low, ffn_row], [half_rows], 1
    )

    dscaled = cotangent[0].astype(F32) * scale
    dffn = (keep * dscaled).astype(BF16)
    dacted = contract_cols(dffn, w_down)
    gate = nn_dot(normed_two, w_gate)
    upward = nn_dot(normed_two, w_up)
    sigmoid_gate = jax.nn.sigmoid(gate)
    silu_gate = gate * sigmoid_gate
    acted = (silu_gate * upward).astype(BF16)
    dgate = (dacted * upward * sigmoid_gate * (1.0 + gate * (1.0 - sigmoid_gate))).astype(BF16)
    dupward = (dacted * silu_gate).astype(BF16)
    dnormed_part = (contract_cols(dgate, w_gate) + contract_cols(dupward, w_up)).astype(BF16)
    ffn_part = nn_dot(acted, w_down).astype(BF16)
    total = lambda g, *axes: lax.psum(g, axes)
    ffn_grads = (
        contract_rows(acted, dffn).astype(BF16),
        contract_rows(normed_two, dgate).astype(BF16),
        contract_rows(normed_two, dupward).astype(BF16),
    )
    dnormed_part, ffn_part, ffn_grads = lax.optimization_barrier(
        (dnormed_part, ffn_part, ffn_grads)
    )
    ffn_grads = total(ffn_grads, "dp", "ctx")
    dattn, output, dhidden, ffn_gain_part = line_sum(
        [dnormed_part, ffn_part],
        [own_dhidden, own_output],
        [x_low, hidden, cotangent[0], ffn_row, jnp.stack([keep * scale, keep])],
        [half_rows, gain_row],
        2,
    )
    grad_output = contract_rows(mixed, dattn)
    dmixed = contract_cols(dattn, w_output).astype(BF16)

    dq_proj, dkeys, dvalues = attend_back(
        queries, dmixed, mixed, logs, cosine, sine, keys, values, query_order, key_order, span
    )

    def collect(grad):
        parts = grad.reshape(ctx_size, rows, -1)
        summed = parts[0]
        for s in range(1, ctx_size):
            back = [(i, (i - s) % ctx_size) for i in range(ctx_size)]
            summed = summed + lax.ppermute(parts[s].astype(BF16), "ctx", back).astype(F32)
        return summed

    dk_own = collect(dkeys).reshape(rows, kv_local, HEAD_DIM)
    dk_proj = rotate_back(dk_own, cosine, sine).reshape(rows, -1).astype(BF16)
    dv_proj = collect(dvalues).astype(BF16)
    dnormed_one = (
        contract_cols(dq_proj, w_query)
        + contract_cols(dk_proj, w_key)
        + contract_cols(dv_proj, w_value)
    ).astype(BF16)
    attn_grads = (
        contract_rows(normed_one, dq_proj).astype(BF16),
        contract_rows(normed_one, dk_proj).astype(BF16),
        contract_rows(normed_one, dv_proj).astype(BF16),
        grad_output.astype(BF16),
    )
    dnormed_one, attn_grads = lax.optimization_barrier((dnormed_one, attn_grads))
    attn_grads, ffn_grads = lax.optimization_barrier((attn_grads, ffn_grads))
    attn_grads = total(attn_grads, "ctx", "dp")
    pairs = pair_steps((dp_size, ctx_size, lax.axis_size("tensor")))
    through, gains = line_sum(
        [dnormed_one],
        [own_dinput],
        [x_low, dhidden, attn_row, ffn_gain_part],
        [jax.ShapeDtypeStruct((8, width), F32)],
        3,
        tuple(pairs),
    )
    grad_attn_gain, grad_ffn_gain = gains[0], gains[1]
    grad_down, grad_gate, grad_up = (g.astype(F32) for g in ffn_grads)
    grad_query, grad_key, grad_value, grad_output = (g.astype(F32) for g in attn_grads)
    input_grad = dscaled + through.astype(F32)
    return (
        output.reshape(inputs.shape),
        input_grad.reshape(inputs.shape),
        grad_attn_gain,
        grad_ffn_gain,
        grad_query,
        grad_key,
        grad_value,
        grad_output,
        grad_gate,
        grad_up,
        grad_down,
    )


def solution(mesh):
    rows = P("dp", "ctx", None)
    by_column, by_row = P(None, "tensor"), P("tensor", None)
    in_specs = (rows, rows, P("dp"), P("dp"), P("dp", None), P(), P(), P())
    in_specs += (by_column,) * 3 + (by_row,) + (by_column,) * 2 + (by_row,)
    out_specs = (rows, rows, P(), P()) + (by_column,) * 3 + (by_row,) + (by_column,) * 2 + (by_row,)
    return jax.shard_map(
        per_device, mesh=mesh, in_specs=in_specs, out_specs=out_specs, check_vma=False
    )
```

```python
import functools

import jax
import jax.numpy as jnp
from jax import lax
from jax.experimental import pallas as pl
from jax.experimental.pallas import tpu as pltpu
from jax.sharding import PartitionSpec as P

HEAD_DIM = 128
EPSILON = 1e-05
NEG_BIG = -1e30
FACTOR = HEAD_DIM ** (-0.5)
LOG2E = 1.4426950408889634
QUERY_BLOCK = 256
BF16 = jnp.bfloat16
F32 = jnp.float32

NT = (((1,), (1,)), ((), ()))


def nt_dot(left, right):
    return lax.dot_general(left, right, NT, preferred_element_type=F32)


def nn_dot(left, right):
    return jnp.dot(left, right, preferred_element_type=F32)


def stack_heads(block, group):
    return jnp.concatenate(
        [block[:, h * HEAD_DIM : (h + 1) * HEAD_DIM] for h in range(group)], axis=0
    )


def hide_later(scores, first_row, rows, fill):
    key_row = lax.broadcasted_iota(jnp.int32, scores.shape, 0)
    query_row = lax.broadcasted_iota(jnp.int32, scores.shape, 1) % rows + first_row
    return jnp.where(key_row <= query_row, scores, fill)


def attend_kernel(
    group, span, query_order, key_order, q_ref, k_ref, vt_ref, o_ref, lse_ref, top, total, acc
):
    rows = q_ref.shape[0]
    step = pl.program_id(1)
    first = step * rows
    order = query_order[first // span]
    queries = stack_heads(q_ref[...], group)
    top[...] = jnp.full_like(top, NEG_BIG)
    total[...] = jnp.zeros_like(total)
    acc[...] = jnp.zeros_like(acc)

    def visit(place, diagonal):
        keys = k_ref[pl.ds(place, span), :]
        scores = nt_dot(keys, queries) * (FACTOR * LOG2E)
        if diagonal:
            scores = hide_later(scores, first % span, rows, NEG_BIG)
        before = top[...]
        now = jnp.maximum(before, jnp.max(scores, axis=0, keepdims=True))
        weights = jnp.exp2(scores - now)
        shrink = jnp.exp2(before - now)
        top[...] = now
        total[...] = total[...] * shrink + jnp.sum(weights, axis=0, keepdims=True)
        acc[...] = acc[...] * shrink + nn_dot(
            vt_ref[:, pl.ds(place, span)], weights.astype(BF16)
        )

    def one_span(j, carry):
        place = pl.multiple_of(j * span, span)
        pl.when(key_order[j] < order)(lambda: visit(place, False))
        pl.when(key_order[j] == order)(lambda: visit(place, True))
        return carry

    lax.fori_loop(0, k_ref.shape[0] // span, one_span, 0)
    mixed = acc[...] / total[...]
    logs = top[...] + jnp.log2(total[...])
    for h in range(group):
        part = slice(h * rows, (h + 1) * rows)
        o_ref[:, h * HEAD_DIM : (h + 1) * HEAD_DIM] = mixed[:, part].T.astype(BF16)
        lse_ref[0, h : h + 1, :] = logs[:, part]


def attend(queries, keys, values, query_order, key_order, span):
    rows, width = queries.shape
    full, kv_width = keys.shape
    kv_heads = kv_width // HEAD_DIM
    group = width // kv_width
    block = min(QUERY_BLOCK, span)
    query_spec = pl.BlockSpec((block, group * HEAD_DIM), lambda g, i, *_: (i, g))
    return pl.pallas_call(
        functools.partial(attend_kernel, group, span),
        grid_spec=pltpu.PrefetchScalarGridSpec(
            num_scalar_prefetch=2,
            grid=(kv_heads, rows // block),
            in_specs=[
                query_spec,
                pl.BlockSpec((full, HEAD_DIM), lambda g, i, *_: (0, g)),
                pl.BlockSpec((HEAD_DIM, full), lambda g, i, *_: (g, 0)),
            ],
            out_specs=[
                query_spec,
                pl.BlockSpec((1, group, block), lambda g, i, *_: (g, 0, i)),
            ],
            scratch_shapes=[
                pltpu.VMEM((1, group * block), F32),
                pltpu.VMEM((1, group * block), F32),
                pltpu.VMEM((HEAD_DIM, group * block), F32),
            ],
        ),
        out_shape=[
            jax.ShapeDtypeStruct((rows, width), BF16),
            jax.ShapeDtypeStruct((kv_heads, group, rows), F32),
        ],
        compiler_params=pltpu.CompilerParams(vmem_limit_bytes=32 * 2**20),
        cost_estimate=pl.CostEstimate(
            flops=4 * rows * full * width,
            bytes_accessed=4 * rows * width + 4 * full * kv_width,
            transcendentals=rows * full * width // HEAD_DIM,
        ),
    )(query_order, key_order, queries, keys, values.T)


def attend_back_kernel(
    group,
    span,
    query_order,
    key_order,
    q_ref,
    do_ref,
    o_ref,
    lse_ref,
    cos_ref,
    sin_ref,
    k_ref,
    v_ref,
    kt_ref,
    dq_ref,
    dk_ref,
    dv_ref,
    acc,
):
    rows = q_ref.shape[0]
    step = pl.program_id(1)
    first = step * rows
    order = query_order[first // span]
    queries = stack_heads(q_ref[...], group)
    dmixed = stack_heads(do_ref[...], group)
    mixed = stack_heads(o_ref[...], group)
    product = dmixed.astype(F32) * mixed.astype(F32)
    delta = jnp.sum(product.T, axis=0, keepdims=True)
    logs = jnp.concatenate([lse_ref[0, h : h + 1, :] for h in range(group)], axis=1)
    acc[...] = jnp.zeros_like(acc)

    @pl.when(step == 0)
    def _():
        dk_ref[...] = jnp.zeros_like(dk_ref)
        dv_ref[...] = jnp.zeros_like(dv_ref)

    def visit(place, diagonal):
        here = pl.ds(place, span)
        scores = nt_dot(k_ref[here, :], queries) * (FACTOR * LOG2E)
        probs = jnp.exp2(scores - logs)
        if diagonal:
            probs = hide_later(probs, first % span, rows, 0.0)
        dprobs = nt_dot(v_ref[here, :], dmixed)
        dscore = (probs * (dprobs - delta)).astype(BF16)
        dv_ref[here, :] += nn_dot(probs.astype(BF16), dmixed)
        dk_ref[here, :] += nn_dot(dscore, queries)
        acc[...] += nn_dot(kt_ref[:, here], dscore)

    def one_span(j, carry):
        place = pl.multiple_of(j * span, span)
        pl.when(key_order[j] < order)(lambda: visit(place, False))
        pl.when(key_order[j] == order)(lambda: visit(place, True))
        return carry

    lax.fori_loop(0, k_ref.shape[0] // span, one_span, 0)
    half = HEAD_DIM // 2
    cosine, sine = cos_ref[...], sin_ref[...]
    for h in range(group):
        grad = acc[:, h * rows : (h + 1) * rows] * FACTOR
        leading, trailing = grad[:half], grad[half:]
        turned = jnp.concatenate(
            [leading * cosine + trailing * sine, trailing * cosine - leading * sine], axis=0
        )
        dq_ref[:, h * HEAD_DIM : (h + 1) * HEAD_DIM] = turned.T.astype(BF16)

    @pl.when(step == pl.num_programs(1) - 1)
    def _():
        dk_ref[...] = dk_ref[...] * FACTOR


def attend_back(
    queries, dmixed, mixed, logs, cosine, sine, keys, values, query_order, key_order, span
):
    rows, width = queries.shape
    full, kv_width = keys.shape
    kv_heads = kv_width // HEAD_DIM
    group = width // kv_width
    block = min(QUERY_BLOCK, span)
    half = HEAD_DIM // 2
    query_spec = pl.BlockSpec((block, group * HEAD_DIM), lambda g, i, *_: (i, g))
    key_spec = pl.BlockSpec((full, HEAD_DIM), lambda g, i, *_: (0, g))
    table_spec = pl.BlockSpec((half, block), lambda g, i, *_: (0, i))
    return pl.pallas_call(
        functools.partial(attend_back_kernel, group, span),
        grid_spec=pltpu.PrefetchScalarGridSpec(
            num_scalar_prefetch=2,
            grid=(kv_heads, rows // block),
            in_specs=[
                query_spec,
                query_spec,
                query_spec,
                pl.BlockSpec((1, group, block), lambda g, i, *_: (g, 0, i)),
                table_spec,
                table_spec,
                key_spec,
                key_spec,
                pl.BlockSpec((HEAD_DIM, full), lambda g, i, *_: (g, 0)),
            ],
            out_specs=[query_spec, key_spec, key_spec],
            scratch_shapes=[pltpu.VMEM((HEAD_DIM, group * block), F32)],
        ),
        out_shape=[
            jax.ShapeDtypeStruct((rows, width), BF16),
            jax.ShapeDtypeStruct((full, kv_width), F32),
            jax.ShapeDtypeStruct((full, kv_width), F32),
        ],
        compiler_params=pltpu.CompilerParams(vmem_limit_bytes=32 * 2**20),
        cost_estimate=pl.CostEstimate(
            flops=10 * rows * full * width,
            bytes_accessed=8 * rows * width + 14 * full * kv_width,
            transcendentals=rows * full * width // HEAD_DIM,
        ),
    )(
        query_order,
        key_order,
        queries,
        dmixed,
        mixed,
        logs,
        cosine.T,
        sine.T,
        keys,
        values,
        keys.T,
    )


LINE_CHUNK = 32
LINE_WINDOW = 2
LINE_SKEW = 2
MESH_AXES = ("dp", "ctx", "tensor")
SPREAD_PIECES = 4


def pair_steps(sizes):
    steps = []
    for axis, size in zip(MESH_AXES, sizes):
        bit = 1
        while bit < size:
            steps.append((axis, bit))
            bit *= 2
    return steps


def partner(axis, bit):
    index = lax.axis_index(axis)
    return jnp.where((index // bit) % 2 == 0, index + bit, index - bit)


def line_kernel(size, chunk, returns, owners, pairs, side_count, out_count, *refs):
    streams = len(returns)
    returned = [k for k in range(streams) if returns[k]]
    parts, refs = refs[:streams], refs[streams:]
    sides, refs = refs[:side_count], refs[side_count:]
    shared, refs = dict(zip(returned, refs)), refs[len(returned) :]
    kept, refs = refs[:out_count], refs[out_count:]
    inbox, send_up, recv_up, send_back, recv_back = refs[:5]
    half = parts[0].shape[0] // 2
    count = half // chunk
    last = size - 1
    me = lax.axis_index("tensor")
    above, below = jnp.minimum(me + 1, last), jnp.maximum(me - 1, 0)
    flows = ((me, above, below), (last - me, below, above))

    barrier = pltpu.get_barrier_semaphore()

    def greet(axis, other):
        pl.semaphore_signal(
            barrier, inc=1, device_id={axis: other}, device_id_type=pl.DeviceIdType.MESH
        )

    if pairs:
        for axis, bit in pairs:
            greet(axis, partner(axis, bit))
        far_above = jnp.where(me % 2 == 0, 0, 1) * jnp.where(me < last, 1, 0)
        far_below = jnp.where(me % 2 == 0, 1, 0) * jnp.where(me > 0, 1, 0)
        pl.when(far_above == 1)(lambda: greet("tensor", above))
        pl.when(far_below == 1)(lambda: greet("tensor", below))
        pl.semaphore_wait(barrier, len(pairs) + far_above + far_below)
    else:
        pl.when(me < last)(lambda: greet("tensor", above))
        pl.when(me > 0)(lambda: greet("tensor", below))
        pl.semaphore_wait(barrier, jnp.where((me > 0) & (me < last), 2, 1))

    def place(f, i):
        return pl.ds(pl.multiple_of(f * half + i * chunk, chunk), chunk)

    def local(i):
        return pl.ds(pl.multiple_of(i * chunk, chunk), chunk)

    def onward(k, f, i, source):
        return pltpu.make_async_remote_copy(
            src_ref=source,
            dst_ref=inbox.at[k, f, local(i)],
            send_sem=send_up.at[k, f, i],
            recv_sem=recv_up.at[k, f, i],
            device_id={"tensor": flows[f][1]},
            device_id_type=pl.DeviceIdType.MESH,
        )

    def backward(k, f, i):
        block = shared[k].at[place(f, i)]
        return pltpu.make_async_remote_copy(
            src_ref=block,
            dst_ref=block,
            send_sem=send_back.at[k, f, i],
            recv_sem=recv_back.at[k, f, i],
            device_id={"tensor": flows[f][2]},
            device_id_type=pl.DeviceIdType.MESH,
        )

    def reduce_chunk(k, f, i):
        position = flows[f][0]
        mine = parts[k].at[place(f, i)]
        slot = inbox.at[k, f, local(i)]

        @pl.when(position == 0)
        def _():
            pl.when(i >= LINE_WINDOW)(lambda: onward(k, f, i - LINE_WINDOW, mine).wait_send())
            onward(k, f, i, mine).start()

        @pl.when(position > 0)
        def _():
            onward(k, f, i, slot).wait_recv()
            total = slot[...].astype(F32) + mine[...].astype(F32)

            @pl.when(position < last)
            def _():
                slot[...] = total.astype(BF16)
                onward(k, f, i, slot).start()

            @pl.when(position == last)
            def _():
                result = owners[k](total, place(f, i), local(i), sides, kept)
                if returns[k]:
                    shared[k][place(f, i), :] = result.astype(BF16)
                    backward(k, f, i).start()

    def pass_back(k, f, i):
        position = flows[f][0]

        @pl.when((position < last) & (i >= 0) & (i < count))
        def _():
            backward(k, f, i).wait_recv()
            pl.when(position > 0)(lambda: backward(k, f, i).start())

    def step(s, carry):
        for k in range(streams):
            for f in range(2):
                i = s - LINE_SKEW * flows[f][0]
                pl.when((i >= 0) & (i < count))(lambda: reduce_chunk(k, f, i))
        for k in returned:
            for f in range(2):
                pass_back(k, f, s - LINE_SKEW * (2 * last - flows[f][0]))
        for n in range(len(pairs) + 1 if pairs else 0):
            pl.when(s == n * gap)(lambda: advance_gains(n))
        return carry

    steps = count + 2 * LINE_SKEW * last
    gap = steps // (len(pairs) + 1)
    if pairs:
        slots, sums, send_pair, recv_pair = refs[5:]
        sums[0] = sides[-1][...]
    elif len(kept) > 1:
        kept[1][...] = jnp.zeros_like(kept[1])

    def swap_gains(n):
        return pltpu.make_async_remote_copy(
            src_ref=sums.at[n],
            dst_ref=slots.at[n],
            send_sem=send_pair.at[n],
            recv_sem=recv_pair.at[n],
            device_id={pairs[n][0]: partner(*pairs[n])},
            device_id_type=pl.DeviceIdType.MESH,
        )

    def advance_gains(n):
        if n > 0:
            swap_gains(n - 1).wait()
            sums[n] = sums[n - 1] + slots[n - 1]
        if n < len(pairs):
            swap_gains(n).start()
        else:
            kept[0][...] = sums[n]

    lax.fori_loop(0, steps, step, 0)

    def drain(i, carry):
        for k in range(streams):
            for f in range(2):
                position = flows[f][0]
                waited = (position == 0) & (i < count - LINE_WINDOW)
                pl.when((position < last) & ~waited)(
                    lambda: onward(k, f, i, inbox.at[k, f, local(i)]).wait_send()
                )
                if returns[k]:
                    pl.when(position > 0)(lambda: backward(k, f, i).wait_send())
        return carry

    lax.fori_loop(0, count, drain, 0)


def line_sum(parts, owners, sides, kept, collective_id, returns=(True,), pairs=()):
    rows, width = parts[0].shape
    size = lax.axis_size("tensor")
    streams = len(parts)
    chunk = max(16, min(LINE_CHUNK, rows // 32))
    count = rows // 2 // chunk
    whole = pl.BlockSpec(memory_space=pltpu.VMEM)
    scalar = pl.BlockSpec(memory_space=pltpu.SMEM)
    sems = pltpu.SemaphoreType.DMA((streams, 2, count))
    outs = [jax.ShapeDtypeStruct((rows, width), BF16)] * sum(returns) + list(kept)
    extra = []
    if pairs:
        pair_sems = pltpu.SemaphoreType.DMA((len(pairs),))
        extra = [
            pltpu.VMEM((len(pairs), 8, width), F32),
            pltpu.VMEM((len(pairs) + 1, 8, width), F32),
            pair_sems,
            pair_sems,
        ]
    return pl.pallas_call(
        functools.partial(
            line_kernel, size, chunk, returns, owners, pairs, len(sides), len(kept)
        ),
        out_shape=outs,
        in_specs=[whole] * streams + [scalar if s.ndim == 1 else whole for s in sides],
        out_specs=[whole] * len(outs),
        scratch_shapes=[pltpu.VMEM((streams, 2, rows // 2, width), BF16)] + [sems] * 4 + extra,
        compiler_params=pltpu.CompilerParams(
            collective_id=collective_id, has_side_effects=True, vmem_limit_bytes=56 * 2**20
        ),
        cost_estimate=pl.CostEstimate(
            flops=streams * rows * width,
            bytes_accessed=streams * 300 * 2**20,
            transcendentals=0,
        ),
    )(*parts, *sides)


def unit_of(rows):
    inverse = lax.rsqrt(jnp.mean(rows * rows, axis=-1, keepdims=True) + EPSILON)
    return rows * inverse, inverse


def own_hidden(total, where, here, sides, kept):
    x_ref, gain_ref = sides
    hidden = x_ref[where, :].astype(F32) + total
    kept[0][here, :] = hidden
    return unit_of(hidden)[0] * gain_ref[...]


def own_dhidden(total, where, here, sides, kept):
    x_ref, hidden_ref, cot_ref, gain_ref, factor = sides
    unit, inverse = unit_of(hidden_ref[here, :])
    kept[1][...] += jnp.sum(total * unit, axis=0, keepdims=True)
    dhidden = norm_back(total, unit, inverse, gain_ref[...])
    kept[0][here, :] = dhidden
    return cot_ref[where, :].astype(F32) * factor[0] + dhidden


def own_output(total, where, here, sides, kept):
    x_ref, hidden_ref, cot_ref, gain_ref, factor = sides
    x = x_ref[where, :].astype(F32)
    result = x + factor[1] * ((hidden_ref[here, :] - x) + total)
    kept[2][here, :] = result.astype(BF16)


def own_dinput(total, where, here, sides, kept):
    x_ref, dhidden_ref, gain_ref, _ = sides
    unit, inverse = unit_of(x_ref[where, :].astype(F32))
    return dhidden_ref[here, :] + norm_back(total, unit, inverse, gain_ref[...])


def spread_halves(own):
    size = lax.axis_size("tensor")
    me = lax.axis_index("tensor")
    pieces = []
    step = own.shape[0] // SPREAD_PIECES
    for p in range(SPREAD_PIECES):
        hops = [own[p * step : (p + 1) * step]]
        for h in range(size - 1):
            perm = [(size - 1 - h, size - 2 - h), (h, h + 1)]
            hops.append(lax.ppermute(hops[-1], "tensor", perm))
        first = lax.select_n(size - 1 - me, *hops) if size > 2 else jnp.where(me == 1, *hops)
        second = lax.select_n(me, *hops) if size > 2 else jnp.where(me == 0, *hops)
        pieces.append((first, second))
    return jnp.concatenate([a for a, _ in pieces] + [b for _, b in pieces], 0)


def rotary_tables(positions):
    inverse = 1.0 / 10000.0 ** (jnp.arange(0, HEAD_DIM, 2, dtype=F32) / HEAD_DIM)
    angle = positions.astype(F32)[:, None] * inverse[None, :]
    return (jnp.cos(angle), jnp.sin(angle))


def rotate(field, cosine, sine):
    half = field.shape[-1] // 2
    leading, trailing = (field[..., :half], field[..., half:])
    cosine, sine = (cosine[:, None, :], sine[:, None, :])
    return jnp.concatenate(
        [leading * cosine - trailing * sine, trailing * cosine + leading * sine], axis=-1
    )


def rotate_back(grad, cosine, sine):
    return rotate(grad, cosine, -sine)


def contract_rows(left, right):
    return jnp.einsum("rd,rf->df", left, right, preferred_element_type=F32)


def contract_cols(left, right):
    return jnp.einsum("rc,dc->rd", left, right, preferred_element_type=F32)


def norm_back(dnormed, unit, inverse, gain):
    scaled = dnormed * gain
    return inverse * (scaled - unit * jnp.mean(scaled * unit, axis=-1, keepdims=True))


def flags_kernel(size, mine, everyone, send_sem, recv_sem):
    me = lax.axis_index("dp")
    barrier = pltpu.get_barrier_semaphore()
    others = [lax.rem(me + s, size) for s in range(1, size)]
    for other in others:
        pl.semaphore_signal(
            barrier, inc=1, device_id={"dp": other}, device_id_type=pl.DeviceIdType.MESH
        )
    pl.semaphore_wait(barrier, size - 1)

    def send(s, slot):
        return pltpu.make_async_remote_copy(
            src_ref=mine,
            dst_ref=everyone.at[slot],
            send_sem=send_sem.at[s],
            recv_sem=recv_sem.at[s],
            device_id={"dp": others[s]},
            device_id_type=pl.DeviceIdType.MESH,
        )

    for s in range(size - 1):
        send(s, me).start()
    everyone[me] = mine[...]
    for s in range(size - 1):
        send(s, me).wait_send()
        send(s, lax.rem(me + 2 * size - 1 - s, size)).wait_recv()


def share_flags(row):
    size = lax.axis_size("dp")
    tile = jnp.zeros((8, 128), jnp.int32).at[0, : row.shape[0]].set(row)
    sems = pltpu.SemaphoreType.DMA((size - 1,))
    whole = pl.BlockSpec(memory_space=pltpu.VMEM)
    shared = pl.pallas_call(
        functools.partial(flags_kernel, size),
        out_shape=jax.ShapeDtypeStruct((size, 8, 128), jnp.int32),
        in_specs=[whole],
        out_specs=whole,
        scratch_shapes=[sems, sems],
        compiler_params=pltpu.CompilerParams(collective_id=1, has_side_effects=True),
    )(tile)
    return shared[:, 0, : row.shape[0]]


def shift_ctx(part, s):
    size = lax.axis_size("ctx")
    return lax.ppermute(part, "ctx", [(i, (i + s) % size) for i in range(size)])


def swap_core(part):
    return lax.ppermute(part, "dp", [(i, i ^ 1) for i in range(lax.axis_size("dp"))])


def gather_parts(own, paired):
    parts = []
    for s in range(lax.axis_size("ctx")):
        here = own if s == 0 else shift_ctx(own, s)
        parts += [here, swap_core(here)] if paired else [here]
    return parts


def collect_parts(parts, paired):
    total = None
    for s in range(lax.axis_size("ctx")):
        if paired:
            near, far = parts[2 * s], parts[2 * s + 1]
            near = near + swap_core(far.astype(BF16)).astype(F32)
        else:
            near = parts[s]
        total = near if s == 0 else total + shift_ctx(near.astype(BF16), -s).astype(F32)
    return total


def block_pass(
    paired,
    first_id,
    span,
    x_low,
    cot_low,
    keep,
    scale,
    order_row,
    attn_gain,
    ffn_gain,
    w_query,
    w_key,
    w_value,
    w_output,
    w_gate,
    w_up,
    w_down,
):
    rows, width = x_low.shape
    dp_size, ctx_size = lax.axis_size("dp"), lax.axis_size("ctx")
    spans = order_row.shape[0]
    kv_local = w_key.shape[1] // HEAD_DIM
    ctx = lax.axis_index("ctx")
    core = lax.axis_index("dp") % 2
    per_part = rows // span
    order_parts = []
    for s in range(ctx_size):
        group = (ctx + ctx_size - s) % ctx_size
        places = [group * 2 + core, group * 2 + 1 - core] if paired else [group]
        order_parts += [
            lax.dynamic_slice_in_dim(order_row, place * per_part, per_part) for place in places
        ]
    query_order, key_order = order_parts[0], jnp.concatenate(order_parts)
    row_index = jnp.arange(rows, dtype=jnp.int32)
    starts = jnp.sum(
        jnp.where(
            (row_index // span)[:, None] == jnp.arange(per_part, dtype=jnp.int32)[None, :],
            query_order[None, :],
            0,
        ),
        axis=1,
    )
    cosine, sine = rotary_tables(starts * span + row_index % span)

    flat = x_low.astype(F32)
    inv_one = lax.rsqrt(jnp.mean(flat * flat, axis=-1, keepdims=True) + EPSILON)
    normed_one = (flat * inv_one * attn_gain).astype(BF16)
    k_proj = nn_dot(normed_one, w_key).reshape(rows, kv_local, HEAD_DIM)
    keys_own = rotate(k_proj, cosine, sine).astype(BF16).reshape(rows, -1)
    values_own = nn_dot(normed_one, w_value).astype(BF16)
    keys = jnp.concatenate(gather_parts(keys_own, paired), 0)
    values = jnp.concatenate(gather_parts(values_own, paired), 0)
    q_proj = nn_dot(normed_one, w_query).reshape(rows, -1, HEAD_DIM)
    queries = rotate(q_proj, cosine, sine).astype(BF16).reshape(rows, -1)
    mixed, logs = attend(queries, keys, values, query_order, key_order, span)

    half_rows = jax.ShapeDtypeStruct((rows // 2, width), F32)
    gain_row = jax.ShapeDtypeStruct((1, width), F32)
    ffn_row, attn_row = ffn_gain[None, :], attn_gain[None, :]
    attn_part = nn_dot(mixed, w_output).astype(BF16)
    normed_two, hidden = line_sum(
        [attn_part], [own_hidden], [x_low, ffn_row], [half_rows], first_id
    )

    dffn = (cot_low.astype(F32) * (keep * scale)).astype(BF16)
    dacted = contract_cols(dffn, w_down)
    gate = nn_dot(normed_two, w_gate)
    upward = nn_dot(normed_two, w_up)
    sigmoid_gate = jax.nn.sigmoid(gate)
    silu_gate = gate * sigmoid_gate
    acted = (silu_gate * upward).astype(BF16)
    dgate = (dacted * upward * sigmoid_gate * (1.0 + gate * (1.0 - sigmoid_gate))).astype(BF16)
    dupward = (dacted * silu_gate).astype(BF16)
    ffn_grads = (
        contract_rows(acted, dffn).astype(BF16),
        contract_rows(normed_two, dgate).astype(BF16),
        contract_rows(normed_two, dupward).astype(BF16),
    )
    acted, dgate, dupward, ffn_grads = lax.optimization_barrier((acted, dgate, dupward, ffn_grads))
    ffn_grads = lax.psum(ffn_grads, ("dp", "ctx"))
    dnormed_part = (contract_cols(dgate, w_gate) + contract_cols(dupward, w_up)).astype(BF16)
    ffn_part = nn_dot(acted, w_down).astype(BF16)
    dattn, dhidden, ffn_gain_part, output_half = line_sum(
        [dnormed_part, ffn_part],
        [own_dhidden, own_output],
        [x_low, hidden, cot_low, ffn_row, jnp.stack([keep * scale, keep])],
        [half_rows, gain_row, jax.ShapeDtypeStruct((rows // 2, width), BF16)],
        first_id + 1,
        (True, False),
    )
    output = spread_halves(output_half)
    grad_output = contract_rows(mixed, dattn)
    dmixed = contract_cols(dattn, w_output).astype(BF16)
    dq_proj, dkeys, dvalues = attend_back(
        queries, dmixed, mixed, logs, cosine, sine, keys, values, query_order, key_order, span
    )
    split = lambda grad: [grad[p * rows : (p + 1) * rows] for p in range(grad.shape[0] // rows)]
    dk_own = collect_parts(split(dkeys), paired).reshape(rows, kv_local, HEAD_DIM)
    dk_proj = rotate_back(dk_own, cosine, sine).reshape(rows, -1).astype(BF16)
    dv_proj = collect_parts(split(dvalues), paired).astype(BF16)
    dnormed_one = (
        contract_cols(dq_proj, w_query)
        + contract_cols(dk_proj, w_key)
        + contract_cols(dv_proj, w_value)
    )
    attn_gain_part = jnp.sum(dnormed_one * (flat * inv_one), axis=0, keepdims=True)
    gain_parts = jnp.concatenate(
        [attn_gain_part, ffn_gain_part, jnp.zeros((6, width), F32)], axis=0
    )
    dnormed_one = dnormed_one.astype(BF16)
    attn_grads = (
        contract_rows(normed_one, dq_proj).astype(BF16),
        contract_rows(normed_one, dk_proj).astype(BF16),
        contract_rows(normed_one, dv_proj).astype(BF16),
        grad_output.astype(BF16),
    )
    dnormed_one, attn_grads = lax.optimization_barrier((dnormed_one, attn_grads))
    attn_grads, ffn_grads = lax.optimization_barrier((attn_grads, ffn_grads))
    attn_grads = lax.psum(attn_grads, ("ctx", "dp"))
    pairs = pair_steps((dp_size, ctx_size, lax.axis_size("tensor")))
    through, gains = line_sum(
        [dnormed_one],
        [own_dinput],
        [x_low, dhidden, attn_row, gain_parts],
        [jax.ShapeDtypeStruct((8, width), F32)],
        first_id + 2,
        (True,),
        tuple(pairs),
    )
    return lax.optimization_barrier((output, through, gains, attn_grads, ffn_grads))


def per_device(
    inputs,
    cotangent,
    skip_mask,
    group_ids,
    span_order,
    exit_scale,
    attn_gain,
    ffn_gain,
    *weights,
):
    _, rows, width = inputs.shape
    spans = span_order.shape[1]
    own_spans = spans // lax.axis_size("ctx")
    span = rows // own_spans
    me = lax.axis_index("dp")
    core = me % 2
    x_low, cot_low = inputs[0], cotangent[0]
    flags = share_flags(jnp.concatenate([skip_mask, group_ids, span_order[0]]))
    runs, groups = flags[:, 0], flags[:, 1]
    scale_of = lambda group: jnp.where(group == 1, exit_scale[1], exit_scale[0])
    own_run, own_scale = skip_mask[0], scale_of(group_ids[0])
    gains = (attn_gain, ffn_gain)

    def alone():
        return block_pass(
            False,
            2,
            span,
            x_low,
            cot_low,
            own_run.astype(F32),
            own_scale,
            span_order[0],
            *gains,
            *weights,
        )

    def shared():
        half = rows // 2
        other = me + 1 - 2 * core
        take = lambda a, i: lax.dynamic_slice_in_dim(a, i * half, half, 0)
        pick = lambda a: lax.dynamic_index_in_dim(a, other, 0, keepdims=False)
        other_run = pick(runs)
        use_own = (own_run == 1) | ((other_run == 0) & (core == 0))
        choose = lambda mine, theirs: jnp.where(use_own, mine, theirs)
        work = lambda a: choose(take(a, core), swap_core(take(a, 1 - core)))
        output, through, *rest = block_pass(
            True,
            5,
            span,
            work(x_low),
            work(cot_low),
            choose(own_run, other_run).astype(F32),
            choose(own_scale, scale_of(pick(groups))),
            choose(span_order[0], pick(flags[:, 2:])),
            *gains,
            *weights,
        )

        def whole(part, idle):
            theirs = swap_core(part)
            first, second = jnp.where(core == 0, part, theirs), jnp.where(core == 0, theirs, part)
            return jnp.where(own_run == 1, jnp.concatenate([first, second], 0), idle)

        return whole(output, x_low), whole(through, jnp.zeros_like(x_low)), *rest

    if own_spans % 2 == 0 and lax.axis_size("dp") % 2 == 0:
        pairs = runs.reshape(-1, 2)
        output, through, sums, attn_grads, ffn_grads = lax.cond(
            jnp.all(pairs[:, 0] * pairs[:, 1] == 0), shared, alone
        )
    else:
        output, through, sums, attn_grads, ffn_grads = alone()
    grad_attn_gain, grad_ffn_gain = sums[0], sums[1]
    grad_down, grad_gate, grad_up = (g.astype(F32) for g in ffn_grads)
    grad_query, grad_key, grad_value, grad_output = (g.astype(F32) for g in attn_grads)
    input_grad = cot_low.astype(F32) * own_scale + through.astype(F32)
    return (
        output.reshape(inputs.shape),
        input_grad.reshape(inputs.shape),
        grad_attn_gain,
        grad_ffn_gain,
        grad_query,
        grad_key,
        grad_value,
        grad_output,
        grad_gate,
        grad_up,
        grad_down,
    )


def solution(mesh):
    rows = P("dp", "ctx", None)
    by_column, by_row = P(None, "tensor"), P("tensor", None)
    in_specs = (rows, rows, P("dp"), P("dp"), P("dp", None), P(), P(), P())
    in_specs += (by_column,) * 3 + (by_row,) + (by_column,) * 2 + (by_row,)
    out_specs = (rows, rows, P(), P()) + (by_column,) * 3 + (by_row,) + (by_column,) * 2 + (by_row,)
    return jax.shard_map(
        per_device, mesh=mesh, in_specs=in_specs, out_specs=out_specs, check_vma=False
    )
```

```python
import functools

import jax
import jax.numpy as jnp
from jax import lax
from jax.experimental import pallas as pl
from jax.experimental.pallas import tpu as pltpu
from jax.sharding import PartitionSpec as P

HEAD_DIM = 128
EPSILON = 1e-05
NEG_BIG = -1e30
FACTOR = HEAD_DIM ** (-0.5)
LOG2E = 1.4426950408889634
QUERY_BLOCK = 256
BF16 = jnp.bfloat16
F32 = jnp.float32

NT = (((1,), (1,)), ((), ()))


def nt_dot(left, right):
    return lax.dot_general(left, right, NT, preferred_element_type=F32)


def nn_dot(left, right):
    return jnp.dot(left, right, preferred_element_type=F32)


def stack_heads(block, group):
    return jnp.concatenate(
        [block[:, h * HEAD_DIM : (h + 1) * HEAD_DIM] for h in range(group)], axis=0
    )


def hide_later(scores, first_row, rows, fill):
    key_row = lax.broadcasted_iota(jnp.int32, scores.shape, 0)
    query_row = lax.broadcasted_iota(jnp.int32, scores.shape, 1) % rows + first_row
    return jnp.where(key_row <= query_row, scores, fill)


def attend_kernel(
    group, span, query_order, key_order, q_ref, k_ref, vt_ref, o_ref, lse_ref, top, total, acc
):
    rows = q_ref.shape[0]
    step = pl.program_id(1)
    first = step * rows
    order = query_order[first // span]
    queries = stack_heads(q_ref[...], group)
    top[...] = jnp.full_like(top, NEG_BIG)
    total[...] = jnp.zeros_like(total)
    acc[...] = jnp.zeros_like(acc)

    def visit(place, diagonal):
        keys = k_ref[pl.ds(place, span), :]
        scores = nt_dot(keys, queries) * (FACTOR * LOG2E)
        if diagonal:
            scores = hide_later(scores, first % span, rows, NEG_BIG)
        before = top[...]
        now = jnp.maximum(before, jnp.max(scores, axis=0, keepdims=True))
        weights = jnp.exp2(scores - now)
        shrink = jnp.exp2(before - now)
        top[...] = now
        total[...] = total[...] * shrink + jnp.sum(weights, axis=0, keepdims=True)
        acc[...] = acc[...] * shrink + nn_dot(
            vt_ref[:, pl.ds(place, span)], weights.astype(BF16)
        )

    def one_span(j, carry):
        place = pl.multiple_of(j * span, span)
        pl.when(key_order[j] < order)(lambda: visit(place, False))
        pl.when(key_order[j] == order)(lambda: visit(place, True))
        return carry

    lax.fori_loop(0, k_ref.shape[0] // span, one_span, 0)
    mixed = acc[...] / total[...]
    logs = top[...] + jnp.log2(total[...])
    for h in range(group):
        part = slice(h * rows, (h + 1) * rows)
        o_ref[:, h * HEAD_DIM : (h + 1) * HEAD_DIM] = mixed[:, part].T.astype(BF16)
        lse_ref[0, h : h + 1, :] = logs[:, part]


def attend(queries, keys, values, query_order, key_order, span):
    rows, width = queries.shape
    full, kv_width = keys.shape
    kv_heads = kv_width // HEAD_DIM
    group = width // kv_width
    block = min(QUERY_BLOCK, span)
    query_spec = pl.BlockSpec((block, group * HEAD_DIM), lambda g, i, *_: (i, g))
    return pl.pallas_call(
        functools.partial(attend_kernel, group, span),
        grid_spec=pltpu.PrefetchScalarGridSpec(
            num_scalar_prefetch=2,
            grid=(kv_heads, rows // block),
            in_specs=[
                query_spec,
                pl.BlockSpec((full, HEAD_DIM), lambda g, i, *_: (0, g)),
                pl.BlockSpec((HEAD_DIM, full), lambda g, i, *_: (g, 0)),
            ],
            out_specs=[
                query_spec,
                pl.BlockSpec((1, group, block), lambda g, i, *_: (g, 0, i)),
            ],
            scratch_shapes=[
                pltpu.VMEM((1, group * block), F32),
                pltpu.VMEM((1, group * block), F32),
                pltpu.VMEM((HEAD_DIM, group * block), F32),
            ],
        ),
        out_shape=[
            jax.ShapeDtypeStruct((rows, width), BF16),
            jax.ShapeDtypeStruct((kv_heads, group, rows), F32),
        ],
        compiler_params=pltpu.CompilerParams(vmem_limit_bytes=32 * 2**20),
        cost_estimate=pl.CostEstimate(
            flops=4 * rows * full * width,
            bytes_accessed=4 * rows * width + 4 * full * kv_width,
            transcendentals=rows * full * width // HEAD_DIM,
        ),
    )(query_order, key_order, queries, keys, values.T)


def attend_back_kernel(
    group,
    span,
    query_order,
    key_order,
    q_ref,
    do_ref,
    o_ref,
    lse_ref,
    cos_ref,
    sin_ref,
    k_ref,
    v_ref,
    kt_ref,
    dq_ref,
    dk_ref,
    dv_ref,
    acc,
):
    rows = q_ref.shape[0]
    step = pl.program_id(1)
    first = step * rows
    order = query_order[first // span]
    queries = stack_heads(q_ref[...], group)
    dmixed = stack_heads(do_ref[...], group)
    mixed = stack_heads(o_ref[...], group)
    product = dmixed.astype(F32) * mixed.astype(F32)
    delta = jnp.sum(product.T, axis=0, keepdims=True)
    logs = jnp.concatenate([lse_ref[0, h : h + 1, :] for h in range(group)], axis=1)
    acc[...] = jnp.zeros_like(acc)

    @pl.when(step == 0)
    def _():
        dk_ref[...] = jnp.zeros_like(dk_ref)
        dv_ref[...] = jnp.zeros_like(dv_ref)

    def visit(place, diagonal):
        here = pl.ds(place, span)
        scores = nt_dot(k_ref[here, :], queries) * (FACTOR * LOG2E)
        probs = jnp.exp2(scores - logs)
        if diagonal:
            probs = hide_later(probs, first % span, rows, 0.0)
        dprobs = nt_dot(v_ref[here, :], dmixed)
        dscore = (probs * (dprobs - delta)).astype(BF16)
        dv_ref[here, :] += nn_dot(probs.astype(BF16), dmixed)
        dk_ref[here, :] += nn_dot(dscore, queries)
        acc[...] += nn_dot(kt_ref[:, here], dscore)

    def one_span(j, carry):
        place = pl.multiple_of(j * span, span)
        pl.when(key_order[j] < order)(lambda: visit(place, False))
        pl.when(key_order[j] == order)(lambda: visit(place, True))
        return carry

    lax.fori_loop(0, k_ref.shape[0] // span, one_span, 0)
    half = HEAD_DIM // 2
    cosine, sine = cos_ref[...], sin_ref[...]
    for h in range(group):
        grad = acc[:, h * rows : (h + 1) * rows] * FACTOR
        leading, trailing = grad[:half], grad[half:]
        turned = jnp.concatenate(
            [leading * cosine + trailing * sine, trailing * cosine - leading * sine], axis=0
        )
        dq_ref[:, h * HEAD_DIM : (h + 1) * HEAD_DIM] = turned.T.astype(BF16)

    @pl.when(step == pl.num_programs(1) - 1)
    def _():
        dk_ref[...] = dk_ref[...] * FACTOR


def attend_back(
    queries, dmixed, mixed, logs, cosine, sine, keys, values, query_order, key_order, span
):
    rows, width = queries.shape
    full, kv_width = keys.shape
    kv_heads = kv_width // HEAD_DIM
    group = width // kv_width
    block = min(QUERY_BLOCK, span)
    half = HEAD_DIM // 2
    query_spec = pl.BlockSpec((block, group * HEAD_DIM), lambda g, i, *_: (i, g))
    key_spec = pl.BlockSpec((full, HEAD_DIM), lambda g, i, *_: (0, g))
    table_spec = pl.BlockSpec((half, block), lambda g, i, *_: (0, i))
    return pl.pallas_call(
        functools.partial(attend_back_kernel, group, span),
        grid_spec=pltpu.PrefetchScalarGridSpec(
            num_scalar_prefetch=2,
            grid=(kv_heads, rows // block),
            in_specs=[
                query_spec,
                query_spec,
                query_spec,
                pl.BlockSpec((1, group, block), lambda g, i, *_: (g, 0, i)),
                table_spec,
                table_spec,
                key_spec,
                key_spec,
                pl.BlockSpec((HEAD_DIM, full), lambda g, i, *_: (g, 0)),
            ],
            out_specs=[query_spec, key_spec, key_spec],
            scratch_shapes=[pltpu.VMEM((HEAD_DIM, group * block), F32)],
        ),
        out_shape=[
            jax.ShapeDtypeStruct((rows, width), BF16),
            jax.ShapeDtypeStruct((full, kv_width), F32),
            jax.ShapeDtypeStruct((full, kv_width), F32),
        ],
        compiler_params=pltpu.CompilerParams(vmem_limit_bytes=32 * 2**20),
        cost_estimate=pl.CostEstimate(
            flops=10 * rows * full * width,
            bytes_accessed=8 * rows * width + 14 * full * kv_width,
            transcendentals=rows * full * width // HEAD_DIM,
        ),
    )(
        query_order,
        key_order,
        queries,
        dmixed,
        mixed,
        logs,
        cosine.T,
        sine.T,
        keys,
        values,
        keys.T,
    )


LINE_CHUNK = 32
LINE_WINDOW = 2
LINE_SKEW = 2
MESH_AXES = ("dp", "ctx", "tensor")
SPREAD_PIECES = 2


def pair_steps(sizes):
    steps = []
    for axis, size in zip(MESH_AXES, sizes):
        bit = 1
        while bit < size:
            steps.append((axis, bit))
            bit *= 2
    return steps


def partner(axis, bit):
    index = lax.axis_index(axis)
    return jnp.where((index // bit) % 2 == 0, index + bit, index - bit)


def line_kernel(size, chunk, returns, owners, pairs, side_count, out_count, *refs):
    streams = len(returns)
    returned = [k for k in range(streams) if returns[k]]
    parts, refs = refs[:streams], refs[streams:]
    sides, refs = refs[:side_count], refs[side_count:]
    shared, refs = dict(zip(returned, refs)), refs[len(returned) :]
    kept, refs = refs[:out_count], refs[out_count:]
    inbox, send_up, recv_up, send_back, recv_back = refs[:5]
    half = parts[0].shape[0] // 2
    count = half // chunk
    last = size - 1
    me = lax.axis_index("tensor")
    above, below = jnp.minimum(me + 1, last), jnp.maximum(me - 1, 0)
    flows = ((me, above, below), (last - me, below, above))

    barrier = pltpu.get_barrier_semaphore()

    def greet(axis, other):
        pl.semaphore_signal(
            barrier, inc=1, device_id={axis: other}, device_id_type=pl.DeviceIdType.MESH
        )

    if pairs:
        for axis, bit in pairs:
            greet(axis, partner(axis, bit))
        far_above = jnp.where(me % 2 == 0, 0, 1) * jnp.where(me < last, 1, 0)
        far_below = jnp.where(me % 2 == 0, 1, 0) * jnp.where(me > 0, 1, 0)
        pl.when(far_above == 1)(lambda: greet("tensor", above))
        pl.when(far_below == 1)(lambda: greet("tensor", below))
        pl.semaphore_wait(barrier, len(pairs) + far_above + far_below)
    else:
        pl.when(me < last)(lambda: greet("tensor", above))
        pl.when(me > 0)(lambda: greet("tensor", below))
        pl.semaphore_wait(barrier, jnp.where((me > 0) & (me < last), 2, 1))

    def place(f, i):
        return pl.ds(pl.multiple_of(f * half + i * chunk, chunk), chunk)

    def local(i):
        return pl.ds(pl.multiple_of(i * chunk, chunk), chunk)

    def onward(k, f, i, source):
        return pltpu.make_async_remote_copy(
            src_ref=source,
            dst_ref=inbox.at[k, f, local(i)],
            send_sem=send_up.at[k, f, i],
            recv_sem=recv_up.at[k, f, i],
            device_id={"tensor": flows[f][1]},
            device_id_type=pl.DeviceIdType.MESH,
        )

    def backward(k, f, i):
        block = shared[k].at[place(f, i)]
        return pltpu.make_async_remote_copy(
            src_ref=block,
            dst_ref=block,
            send_sem=send_back.at[k, f, i],
            recv_sem=recv_back.at[k, f, i],
            device_id={"tensor": flows[f][2]},
            device_id_type=pl.DeviceIdType.MESH,
        )

    def reduce_chunk(k, f, i):
        position = flows[f][0]
        mine = parts[k].at[place(f, i)]
        slot = inbox.at[k, f, local(i)]

        @pl.when(position == 0)
        def _():
            pl.when(i >= LINE_WINDOW)(lambda: onward(k, f, i - LINE_WINDOW, mine).wait_send())
            onward(k, f, i, mine).start()

        @pl.when(position > 0)
        def _():
            onward(k, f, i, slot).wait_recv()
            total = slot[...].astype(F32) + mine[...].astype(F32)

            @pl.when(position < last)
            def _():
                slot[...] = total.astype(BF16)
                onward(k, f, i, slot).start()

            @pl.when(position == last)
            def _():
                result = owners[k](total, place(f, i), local(i), sides, kept)
                if returns[k]:
                    shared[k][place(f, i), :] = result.astype(BF16)
                    backward(k, f, i).start()

    def pass_back(k, f, i):
        position = flows[f][0]

        @pl.when((position < last) & (i >= 0) & (i < count))
        def _():
            backward(k, f, i).wait_recv()
            pl.when(position > 0)(lambda: backward(k, f, i).start())

    def step(s, carry):
        for k in range(streams):
            for f in range(2):
                i = s - LINE_SKEW * flows[f][0]
                pl.when((i >= 0) & (i < count))(lambda: reduce_chunk(k, f, i))
        for k in returned:
            for f in range(2):
                pass_back(k, f, s - LINE_SKEW * (2 * last - flows[f][0]))
        for n in range(len(pairs) + 1 if pairs else 0):
            pl.when(s == n * gap)(lambda: advance_gains(n))
        return carry

    steps = count + 2 * LINE_SKEW * last
    gap = steps // (len(pairs) + 1)
    if pairs:
        slots, sums, send_pair, recv_pair = refs[5:]
        sums[0] = sides[-1][...]
    elif len(kept) > 1:
        kept[1][...] = jnp.zeros_like(kept[1])

    def swap_gains(n):
        return pltpu.make_async_remote_copy(
            src_ref=sums.at[n],
            dst_ref=slots.at[n],
            send_sem=send_pair.at[n],
            recv_sem=recv_pair.at[n],
            device_id={pairs[n][0]: partner(*pairs[n])},
            device_id_type=pl.DeviceIdType.MESH,
        )

    def advance_gains(n):
        if n > 0:
            swap_gains(n - 1).wait()
            sums[n] = sums[n - 1] + slots[n - 1]
        if n < len(pairs):
            swap_gains(n).start()
        else:
            kept[0][...] = sums[n]

    lax.fori_loop(0, steps, step, 0)

    def drain(i, carry):
        for k in range(streams):
            for f in range(2):
                position = flows[f][0]
                waited = (position == 0) & (i < count - LINE_WINDOW)
                pl.when((position < last) & ~waited)(
                    lambda: onward(k, f, i, inbox.at[k, f, local(i)]).wait_send()
                )
                if returns[k]:
                    pl.when(position > 0)(lambda: backward(k, f, i).wait_send())
        return carry

    lax.fori_loop(0, count, drain, 0)


def line_sum(parts, owners, sides, kept, collective_id, returns=(True,), pairs=()):
    rows, width = parts[0].shape
    size = lax.axis_size("tensor")
    streams = len(parts)
    chunk = max(16, min(LINE_CHUNK, rows // 32))
    count = rows // 2 // chunk
    whole = pl.BlockSpec(memory_space=pltpu.VMEM)
    scalar = pl.BlockSpec(memory_space=pltpu.SMEM)
    sems = pltpu.SemaphoreType.DMA((streams, 2, count))
    outs = [jax.ShapeDtypeStruct((rows, width), BF16)] * sum(returns) + list(kept)
    extra = []
    if pairs:
        pair_sems = pltpu.SemaphoreType.DMA((len(pairs),))
        extra = [
            pltpu.VMEM((len(pairs), 8, width), F32),
            pltpu.VMEM((len(pairs) + 1, 8, width), F32),
            pair_sems,
            pair_sems,
        ]
    return pl.pallas_call(
        functools.partial(
            line_kernel, size, chunk, returns, owners, pairs, len(sides), len(kept)
        ),
        out_shape=outs,
        in_specs=[whole] * streams + [scalar if s.ndim == 1 else whole for s in sides],
        out_specs=[whole] * len(outs),
        scratch_shapes=[pltpu.VMEM((streams, 2, rows // 2, width), BF16)] + [sems] * 4 + extra,
        compiler_params=pltpu.CompilerParams(
            collective_id=collective_id, has_side_effects=True, vmem_limit_bytes=56 * 2**20
        ),
        cost_estimate=pl.CostEstimate(
            flops=streams * rows * width,
            bytes_accessed=streams * 300 * 2**20,
            transcendentals=0,
        ),
    )(*parts, *sides)


def unit_of(rows):
    inverse = lax.rsqrt(jnp.mean(rows * rows, axis=-1, keepdims=True) + EPSILON)
    return rows * inverse, inverse


def own_hidden(total, where, here, sides, kept):
    x_ref, gain_ref = sides
    hidden = x_ref[where, :].astype(F32) + total
    kept[0][here, :] = hidden
    return unit_of(hidden)[0] * gain_ref[...]


def own_dhidden(total, where, here, sides, kept):
    x_ref, hidden_ref, cot_ref, gain_ref, factor = sides
    unit, inverse = unit_of(hidden_ref[here, :])
    kept[1][...] += jnp.sum(total * unit, axis=0, keepdims=True)
    dhidden = norm_back(total, unit, inverse, gain_ref[...])
    kept[0][here, :] = dhidden
    return cot_ref[where, :].astype(F32) * factor[0] + dhidden


def own_output(total, where, here, sides, kept):
    x_ref, hidden_ref, cot_ref, gain_ref, factor = sides
    x = x_ref[where, :].astype(F32)
    result = x + factor[1] * ((hidden_ref[here, :] - x) + total)
    kept[2][here, :] = result.astype(BF16)


def own_dinput(total, where, here, sides, kept):
    x_ref, dhidden_ref, gain_ref, _ = sides
    unit, inverse = unit_of(x_ref[where, :].astype(F32))
    return dhidden_ref[here, :] + norm_back(total, unit, inverse, gain_ref[...])


def cut_half(own):
    step = own.shape[0] // SPREAD_PIECES
    return [[own[p * step : (p + 1) * step]] for p in range(SPREAD_PIECES)]


def send_wave(pieces, wave):
    size = lax.axis_size("tensor")
    for p, hops in enumerate(pieces):
        h = wave - p
        if 0 <= h < size - 1:
            perm = [(size - 1 - h, size - 2 - h), (h, h + 1)]
            hops.append(lax.ppermute(hops[-1], "tensor", perm))


def tie(pieces, others):
    heads, others = lax.optimization_barrier(([hops[-1] for hops in pieces], others))
    for hops, head in zip(pieces, heads):
        hops[-1] = head
    return others


def join_kernel(size, *refs):
    pieces, out, sems = refs[:-2], refs[-2], refs[-1]
    me = lax.axis_index("tensor")
    step = pieces[0].shape[0]
    half = out.shape[0] // 2

    def copies(act):
        for p in range(SPREAD_PIECES):
            for h in range(size):
                for f, wanted in enumerate((size - 1 - me, me)):
                    copy = pltpu.make_async_copy(
                        pieces[p * size + h],
                        out.at[pl.ds(f * half + p * step, step)],
                        sems.at[f, p],
                    )
                    pl.when(wanted == h)(functools.partial(act, copy))

    copies(lambda copy: copy.start())
    copies(lambda copy: copy.wait())


def join_halves(pieces):
    size = lax.axis_size("tensor")
    step, width = pieces[0].shape
    anywhere = pl.BlockSpec(memory_space=pl.ANY)
    return pl.pallas_call(
        functools.partial(join_kernel, size),
        out_shape=jax.ShapeDtypeStruct((2 * SPREAD_PIECES * step, width), BF16),
        in_specs=[anywhere] * len(pieces),
        out_specs=anywhere,
        scratch_shapes=[pltpu.SemaphoreType.DMA((2, SPREAD_PIECES))],
    )(*pieces)


def rotary_tables(positions):
    inverse = 1.0 / 10000.0 ** (jnp.arange(0, HEAD_DIM, 2, dtype=F32) / HEAD_DIM)
    angle = positions.astype(F32)[:, None] * inverse[None, :]
    return (jnp.cos(angle), jnp.sin(angle))


def rotate(field, cosine, sine):
    half = field.shape[-1] // 2
    leading, trailing = (field[..., :half], field[..., half:])
    cosine, sine = (cosine[:, None, :], sine[:, None, :])
    return jnp.concatenate(
        [leading * cosine - trailing * sine, trailing * cosine + leading * sine], axis=-1
    )


def rotate_back(grad, cosine, sine):
    return rotate(grad, cosine, -sine)


def contract_rows(left, right):
    return jnp.einsum("rd,rf->df", left, right, preferred_element_type=F32)


def contract_cols(left, right):
    return jnp.einsum("rc,dc->rd", left, right, preferred_element_type=F32)


def norm_back(dnormed, unit, inverse, gain):
    scaled = dnormed * gain
    return inverse * (scaled - unit * jnp.mean(scaled * unit, axis=-1, keepdims=True))


def flags_kernel(size, mine, everyone, send_sem, recv_sem):
    me = lax.axis_index("dp")
    barrier = pltpu.get_barrier_semaphore()
    others = [lax.rem(me + s, size) for s in range(1, size)]
    for other in others:
        pl.semaphore_signal(
            barrier, inc=1, device_id={"dp": other}, device_id_type=pl.DeviceIdType.MESH
        )
    pl.semaphore_wait(barrier, size - 1)

    def send(s, slot):
        return pltpu.make_async_remote_copy(
            src_ref=mine,
            dst_ref=everyone.at[slot],
            send_sem=send_sem.at[s],
            recv_sem=recv_sem.at[s],
            device_id={"dp": others[s]},
            device_id_type=pl.DeviceIdType.MESH,
        )

    for s in range(size - 1):
        send(s, me).start()
    everyone[me] = mine[...]
    for s in range(size - 1):
        send(s, me).wait_send()
        send(s, lax.rem(me + 2 * size - 1 - s, size)).wait_recv()


def share_flags(row):
    size = lax.axis_size("dp")
    tile = jnp.zeros((8, 128), jnp.int32).at[0, : row.shape[0]].set(row)
    sems = pltpu.SemaphoreType.DMA((size - 1,))
    whole = pl.BlockSpec(memory_space=pltpu.VMEM)
    shared = pl.pallas_call(
        functools.partial(flags_kernel, size),
        out_shape=jax.ShapeDtypeStruct((size, 8, 128), jnp.int32),
        in_specs=[whole],
        out_specs=whole,
        scratch_shapes=[sems, sems],
        compiler_params=pltpu.CompilerParams(collective_id=1, has_side_effects=True),
    )(tile)
    return shared[:, 0, : row.shape[0]]


def shift_ctx(part, s):
    size = lax.axis_size("ctx")
    return lax.ppermute(part, "ctx", [(i, (i + s) % size) for i in range(size)])


def swap_core(part):
    return lax.ppermute(part, "dp", [(i, i ^ 1) for i in range(lax.axis_size("dp"))])


def gather_parts(own, paired):
    parts = []
    for s in range(lax.axis_size("ctx")):
        here = own if s == 0 else shift_ctx(own, s)
        parts += [here, swap_core(here)] if paired else [here]
    return parts


def collect_parts(parts, paired):
    total = None
    for s in range(lax.axis_size("ctx")):
        if paired:
            near, far = parts[2 * s], parts[2 * s + 1]
            near = near + swap_core(far.astype(BF16)).astype(F32)
        else:
            near = parts[s]
        total = near if s == 0 else total + shift_ctx(near.astype(BF16), -s).astype(F32)
    return total


def block_pass(
    paired,
    first_id,
    span,
    x_low,
    cot_low,
    keep,
    scale,
    order_row,
    attn_gain,
    ffn_gain,
    w_query,
    w_key,
    w_value,
    w_output,
    w_gate,
    w_up,
    w_down,
):
    rows, width = x_low.shape
    dp_size, ctx_size = lax.axis_size("dp"), lax.axis_size("ctx")
    spans = order_row.shape[0]
    kv_local = w_key.shape[1] // HEAD_DIM
    ctx = lax.axis_index("ctx")
    core = lax.axis_index("dp") % 2
    per_part = rows // span
    order_parts = []
    for s in range(ctx_size):
        group = (ctx + ctx_size - s) % ctx_size
        places = [group * 2 + core, group * 2 + 1 - core] if paired else [group]
        order_parts += [
            lax.dynamic_slice_in_dim(order_row, place * per_part, per_part) for place in places
        ]
    query_order, key_order = order_parts[0], jnp.concatenate(order_parts)
    row_index = jnp.arange(rows, dtype=jnp.int32)
    starts = jnp.sum(
        jnp.where(
            (row_index // span)[:, None] == jnp.arange(per_part, dtype=jnp.int32)[None, :],
            query_order[None, :],
            0,
        ),
        axis=1,
    )
    cosine, sine = rotary_tables(starts * span + row_index % span)

    flat = x_low.astype(F32)
    inv_one = lax.rsqrt(jnp.mean(flat * flat, axis=-1, keepdims=True) + EPSILON)
    normed_one = (flat * inv_one * attn_gain).astype(BF16)
    k_proj = nn_dot(normed_one, w_key).reshape(rows, kv_local, HEAD_DIM)
    keys_own = rotate(k_proj, cosine, sine).astype(BF16).reshape(rows, -1)
    values_own = nn_dot(normed_one, w_value).astype(BF16)
    keys = jnp.concatenate(gather_parts(keys_own, paired), 0)
    values = jnp.concatenate(gather_parts(values_own, paired), 0)
    q_proj = nn_dot(normed_one, w_query).reshape(rows, -1, HEAD_DIM)
    queries = rotate(q_proj, cosine, sine).astype(BF16).reshape(rows, -1)
    mixed, logs = attend(queries, keys, values, query_order, key_order, span)

    half_rows = jax.ShapeDtypeStruct((rows // 2, width), F32)
    gain_row = jax.ShapeDtypeStruct((1, width), F32)
    ffn_row, attn_row = ffn_gain[None, :], attn_gain[None, :]
    attn_part = nn_dot(mixed, w_output).astype(BF16)
    normed_two, hidden = line_sum(
        [attn_part], [own_hidden], [x_low, ffn_row], [half_rows], first_id
    )

    dffn = (cot_low.astype(F32) * (keep * scale)).astype(BF16)
    dacted = contract_cols(dffn, w_down)
    gate = nn_dot(normed_two, w_gate)
    upward = nn_dot(normed_two, w_up)
    sigmoid_gate = jax.nn.sigmoid(gate)
    silu_gate = gate * sigmoid_gate
    acted = (silu_gate * upward).astype(BF16)
    dgate = (dacted * upward * sigmoid_gate * (1.0 + gate * (1.0 - sigmoid_gate))).astype(BF16)
    dupward = (dacted * silu_gate).astype(BF16)
    ffn_grads = (
        contract_rows(acted, dffn).astype(BF16),
        contract_rows(normed_two, dgate).astype(BF16),
        contract_rows(normed_two, dupward).astype(BF16),
    )
    acted, dgate, dupward, ffn_grads = lax.optimization_barrier((acted, dgate, dupward, ffn_grads))
    ffn_grads = lax.psum(ffn_grads, ("dp", "ctx"))
    dnormed_part = (contract_cols(dgate, w_gate) + contract_cols(dupward, w_up)).astype(BF16)
    ffn_part = nn_dot(acted, w_down).astype(BF16)
    dattn, dhidden, ffn_gain_part, output_half = line_sum(
        [dnormed_part, ffn_part],
        [own_dhidden, own_output],
        [x_low, hidden, cot_low, ffn_row, jnp.stack([keep * scale, keep])],
        [half_rows, gain_row, jax.ShapeDtypeStruct((rows // 2, width), BF16)],
        first_id + 1,
        (True, False),
    )
    pieces = cut_half(output_half)
    send_wave(pieces, 0)
    grad_output = contract_rows(mixed, dattn)
    dmixed = contract_cols(dattn, w_output).astype(BF16)
    dq_proj, dkeys, dvalues = attend_back(
        queries, dmixed, mixed, logs, cosine, sine, keys, values, query_order, key_order, span
    )
    dq_proj, dkeys, dvalues = tie(pieces, (dq_proj, dkeys, dvalues))
    send_wave(pieces, 1)
    split = lambda grad: [grad[p * rows : (p + 1) * rows] for p in range(grad.shape[0] // rows)]
    dk_own = collect_parts(split(dkeys), paired).reshape(rows, kv_local, HEAD_DIM)
    dk_proj = rotate_back(dk_own, cosine, sine).reshape(rows, -1).astype(BF16)
    dv_proj = collect_parts(split(dvalues), paired).astype(BF16)
    dk_proj, dv_proj = tie(pieces, (dk_proj, dv_proj))
    send_wave(pieces, 2)
    dnormed_one = (
        contract_cols(dq_proj, w_query)
        + contract_cols(dk_proj, w_key)
        + contract_cols(dv_proj, w_value)
    )
    attn_gain_part = jnp.sum(dnormed_one * (flat * inv_one), axis=0, keepdims=True)
    gain_parts = jnp.concatenate(
        [attn_gain_part, ffn_gain_part, jnp.zeros((6, width), F32)], axis=0
    )
    dnormed_one = dnormed_one.astype(BF16)
    attn_grads = (
        contract_rows(normed_one, dq_proj).astype(BF16),
        contract_rows(normed_one, dk_proj).astype(BF16),
        contract_rows(normed_one, dv_proj).astype(BF16),
        grad_output.astype(BF16),
    )
    dnormed_one, attn_grads, ffn_grads = tie(pieces, (dnormed_one, attn_grads, ffn_grads))
    for wave in range(3, lax.axis_size("tensor") + SPREAD_PIECES):
        send_wave(pieces, wave)
    attn_grads = lax.psum(attn_grads, ("ctx", "dp"))
    pairs = pair_steps((dp_size, ctx_size, lax.axis_size("tensor")))
    through, gains = line_sum(
        [dnormed_one],
        [own_dinput],
        [x_low, dhidden, attn_row, gain_parts],
        [jax.ShapeDtypeStruct((8, width), F32)],
        first_id + 2,
        (True,),
        tuple(pairs),
    )
    through, gains, attn_grads, ffn_grads, pieces = lax.optimization_barrier(
        (through, gains, attn_grads, ffn_grads, pieces)
    )
    return join_halves([hop for hops in pieces for hop in hops]), through, gains, attn_grads, ffn_grads


def per_device(
    inputs,
    cotangent,
    skip_mask,
    group_ids,
    span_order,
    exit_scale,
    attn_gain,
    ffn_gain,
    *weights,
):
    _, rows, width = inputs.shape
    spans = span_order.shape[1]
    own_spans = spans // lax.axis_size("ctx")
    span = rows // own_spans
    me = lax.axis_index("dp")
    core = me % 2
    x_low, cot_low = inputs[0], cotangent[0]
    flags = share_flags(jnp.concatenate([skip_mask, group_ids, span_order[0]]))
    runs, groups = flags[:, 0], flags[:, 1]
    scale_of = lambda group: jnp.where(group == 1, exit_scale[1], exit_scale[0])
    own_run, own_scale = skip_mask[0], scale_of(group_ids[0])
    gains = (attn_gain, ffn_gain)

    def alone():
        return block_pass(
            False,
            2,
            span,
            x_low,
            cot_low,
            own_run.astype(F32),
            own_scale,
            span_order[0],
            *gains,
            *weights,
        )

    def shared():
        half = rows // 2
        other = me + 1 - 2 * core
        take = lambda a, i: lax.dynamic_slice_in_dim(a, i * half, half, 0)
        pick = lambda a: lax.dynamic_index_in_dim(a, other, 0, keepdims=False)
        other_run = pick(runs)
        use_own = (own_run == 1) | ((other_run == 0) & (core == 0))
        choose = lambda mine, theirs: jnp.where(use_own, mine, theirs)
        work = lambda a: choose(take(a, core), swap_core(take(a, 1 - core)))
        output, through, *rest = block_pass(
            True,
            5,
            span,
            work(x_low),
            work(cot_low),
            choose(own_run, other_run).astype(F32),
            choose(own_scale, scale_of(pick(groups))),
            choose(span_order[0], pick(flags[:, 2:])),
            *gains,
            *weights,
        )

        def whole(part, idle):
            theirs = swap_core(part)
            first, second = jnp.where(core == 0, part, theirs), jnp.where(core == 0, theirs, part)
            return jnp.where(own_run == 1, jnp.concatenate([first, second], 0), idle)

        return whole(output, x_low), whole(through, jnp.zeros_like(x_low)), *rest

    if own_spans % 2 == 0 and lax.axis_size("dp") % 2 == 0:
        pairs = runs.reshape(-1, 2)
        output, through, sums, attn_grads, ffn_grads = lax.cond(
            jnp.all(pairs[:, 0] * pairs[:, 1] == 0), shared, alone
        )
    else:
        output, through, sums, attn_grads, ffn_grads = alone()
    grad_attn_gain, grad_ffn_gain = sums[0], sums[1]
    grad_down, grad_gate, grad_up = (g.astype(F32) for g in ffn_grads)
    grad_query, grad_key, grad_value, grad_output = (g.astype(F32) for g in attn_grads)
    input_grad = cot_low.astype(F32) * own_scale + through.astype(F32)
    return (
        output.reshape(inputs.shape),
        input_grad.reshape(inputs.shape),
        grad_attn_gain,
        grad_ffn_gain,
        grad_query,
        grad_key,
        grad_value,
        grad_output,
        grad_gate,
        grad_up,
        grad_down,
    )


def solution(mesh):
    rows = P("dp", "ctx", None)
    by_column, by_row = P(None, "tensor"), P("tensor", None)
    in_specs = (rows, rows, P("dp"), P("dp"), P("dp", None), P(), P(), P())
    in_specs += (by_column,) * 3 + (by_row,) + (by_column,) * 2 + (by_row,)
    out_specs = (rows, rows, P(), P()) + (by_column,) * 3 + (by_row,) + (by_column,) * 2 + (by_row,)
    return jax.shard_map(
        per_device, mesh=mesh, in_specs=in_specs, out_specs=out_specs, check_vma=False
    )
```

```python
import functools

import jax
import jax.numpy as jnp
from jax import lax
from jax.experimental import pallas as pl
from jax.experimental.pallas import tpu as pltpu
from jax.sharding import PartitionSpec as P

HEAD_DIM = 128
EPSILON = 1e-05
NEG_BIG = -1e30
FACTOR = HEAD_DIM ** (-0.5)
LOG2E = 1.4426950408889634
QUERY_BLOCK = 256
BF16 = jnp.bfloat16
F32 = jnp.float32

NT = (((1,), (1,)), ((), ()))


def nt_dot(left, right):
    return lax.dot_general(left, right, NT, preferred_element_type=F32)


def nn_dot(left, right):
    return jnp.dot(left, right, preferred_element_type=F32)


def stack_heads(block, group):
    return jnp.concatenate(
        [block[:, h * HEAD_DIM : (h + 1) * HEAD_DIM] for h in range(group)], axis=0
    )


def hide_later(scores, first_row, rows, fill):
    key_row = lax.broadcasted_iota(jnp.int32, scores.shape, 0)
    query_row = lax.broadcasted_iota(jnp.int32, scores.shape, 1) % rows + first_row
    return jnp.where(key_row <= query_row, scores, fill)


def attend_kernel(
    group, span, query_order, key_order, q_ref, k_ref, vt_ref, o_ref, lse_ref, top, total, acc
):
    rows = q_ref.shape[0]
    step = pl.program_id(1)
    first = step * rows
    order = query_order[first // span]
    queries = stack_heads(q_ref[...], group)
    top[...] = jnp.full_like(top, NEG_BIG)
    total[...] = jnp.zeros_like(total)
    acc[...] = jnp.zeros_like(acc)

    def visit(place, diagonal):
        keys = k_ref[pl.ds(place, span), :]
        scores = nt_dot(keys, queries) * (FACTOR * LOG2E)
        if diagonal:
            scores = hide_later(scores, first % span, rows, NEG_BIG)
        before = top[...]
        now = jnp.maximum(before, jnp.max(scores, axis=0, keepdims=True))
        weights = jnp.exp2(scores - now)
        shrink = jnp.exp2(before - now)
        top[...] = now
        total[...] = total[...] * shrink + jnp.sum(weights, axis=0, keepdims=True)
        acc[...] = acc[...] * shrink + nn_dot(
            vt_ref[:, pl.ds(place, span)], weights.astype(BF16)
        )

    def one_span(j, carry):
        place = pl.multiple_of(j * span, span)
        pl.when(key_order[j] < order)(lambda: visit(place, False))
        pl.when(key_order[j] == order)(lambda: visit(place, True))
        return carry

    lax.fori_loop(0, k_ref.shape[0] // span, one_span, 0)
    mixed = acc[...] / total[...]
    logs = top[...] + jnp.log2(total[...])
    for h in range(group):
        part = slice(h * rows, (h + 1) * rows)
        o_ref[:, h * HEAD_DIM : (h + 1) * HEAD_DIM] = mixed[:, part].T.astype(BF16)
        lse_ref[0, h : h + 1, :] = logs[:, part]


def attend(queries, keys, values, query_order, key_order, span):
    rows, width = queries.shape
    full, kv_width = keys.shape
    kv_heads = kv_width // HEAD_DIM
    group = width // kv_width
    block = min(QUERY_BLOCK, span)
    query_spec = pl.BlockSpec((block, group * HEAD_DIM), lambda g, i, *_: (i, g))
    return pl.pallas_call(
        functools.partial(attend_kernel, group, span),
        grid_spec=pltpu.PrefetchScalarGridSpec(
            num_scalar_prefetch=2,
            grid=(kv_heads, rows // block),
            in_specs=[
                query_spec,
                pl.BlockSpec((full, HEAD_DIM), lambda g, i, *_: (0, g)),
                pl.BlockSpec((HEAD_DIM, full), lambda g, i, *_: (g, 0)),
            ],
            out_specs=[
                query_spec,
                pl.BlockSpec((1, group, block), lambda g, i, *_: (g, 0, i)),
            ],
            scratch_shapes=[
                pltpu.VMEM((1, group * block), F32),
                pltpu.VMEM((1, group * block), F32),
                pltpu.VMEM((HEAD_DIM, group * block), F32),
            ],
        ),
        out_shape=[
            jax.ShapeDtypeStruct((rows, width), BF16),
            jax.ShapeDtypeStruct((kv_heads, group, rows), F32),
        ],
        compiler_params=pltpu.CompilerParams(vmem_limit_bytes=32 * 2**20),
        cost_estimate=pl.CostEstimate(
            flops=4 * rows * full * width,
            bytes_accessed=4 * rows * width + 4 * full * kv_width,
            transcendentals=rows * full * width // HEAD_DIM,
        ),
    )(query_order, key_order, queries, keys, values.T)


def attend_back_kernel(
    group,
    span,
    query_order,
    key_order,
    q_ref,
    do_ref,
    o_ref,
    lse_ref,
    cos_ref,
    sin_ref,
    k_ref,
    v_ref,
    kt_ref,
    dq_ref,
    dk_ref,
    dv_ref,
    acc,
):
    rows = q_ref.shape[0]
    step = pl.program_id(1)
    first = step * rows
    order = query_order[first // span]
    queries = stack_heads(q_ref[...], group)
    dmixed = stack_heads(do_ref[...], group)
    mixed = stack_heads(o_ref[...], group)
    product = dmixed.astype(F32) * mixed.astype(F32)
    delta = jnp.sum(product.T, axis=0, keepdims=True)
    logs = jnp.concatenate([lse_ref[0, h : h + 1, :] for h in range(group)], axis=1)
    acc[...] = jnp.zeros_like(acc)

    @pl.when(step == 0)
    def _():
        dk_ref[...] = jnp.zeros_like(dk_ref)
        dv_ref[...] = jnp.zeros_like(dv_ref)

    def visit(place, diagonal):
        here = pl.ds(place, span)
        scores = nt_dot(k_ref[here, :], queries) * (FACTOR * LOG2E)
        probs = jnp.exp2(scores - logs)
        if diagonal:
            probs = hide_later(probs, first % span, rows, 0.0)
        dprobs = nt_dot(v_ref[here, :], dmixed)
        dscore = (probs * (dprobs - delta)).astype(BF16)
        dv_ref[here, :] += nn_dot(probs.astype(BF16), dmixed)
        dk_ref[here, :] += nn_dot(dscore, queries)
        acc[...] += nn_dot(kt_ref[:, here], dscore)

    def one_span(j, carry):
        place = pl.multiple_of(j * span, span)
        pl.when(key_order[j] < order)(lambda: visit(place, False))
        pl.when(key_order[j] == order)(lambda: visit(place, True))
        return carry

    lax.fori_loop(0, k_ref.shape[0] // span, one_span, 0)
    half = HEAD_DIM // 2
    cosine, sine = cos_ref[...], sin_ref[...]
    for h in range(group):
        grad = acc[:, h * rows : (h + 1) * rows] * FACTOR
        leading, trailing = grad[:half], grad[half:]
        turned = jnp.concatenate(
            [leading * cosine + trailing * sine, trailing * cosine - leading * sine], axis=0
        )
        dq_ref[:, h * HEAD_DIM : (h + 1) * HEAD_DIM] = turned.T.astype(BF16)

    @pl.when(step == pl.num_programs(1) - 1)
    def _():
        dk_ref[...] = dk_ref[...] * FACTOR


def attend_back(
    queries, dmixed, mixed, logs, cosine, sine, keys, values, query_order, key_order, span
):
    rows, width = queries.shape
    full, kv_width = keys.shape
    kv_heads = kv_width // HEAD_DIM
    group = width // kv_width
    block = min(QUERY_BLOCK, span)
    half = HEAD_DIM // 2
    query_spec = pl.BlockSpec((block, group * HEAD_DIM), lambda g, i, *_: (i, g))
    key_spec = pl.BlockSpec((full, HEAD_DIM), lambda g, i, *_: (0, g))
    table_spec = pl.BlockSpec((half, block), lambda g, i, *_: (0, i))
    return pl.pallas_call(
        functools.partial(attend_back_kernel, group, span),
        grid_spec=pltpu.PrefetchScalarGridSpec(
            num_scalar_prefetch=2,
            grid=(kv_heads, rows // block),
            in_specs=[
                query_spec,
                query_spec,
                query_spec,
                pl.BlockSpec((1, group, block), lambda g, i, *_: (g, 0, i)),
                table_spec,
                table_spec,
                key_spec,
                key_spec,
                pl.BlockSpec((HEAD_DIM, full), lambda g, i, *_: (g, 0)),
            ],
            out_specs=[query_spec, key_spec, key_spec],
            scratch_shapes=[pltpu.VMEM((HEAD_DIM, group * block), F32)],
        ),
        out_shape=[
            jax.ShapeDtypeStruct((rows, width), BF16),
            jax.ShapeDtypeStruct((full, kv_width), F32),
            jax.ShapeDtypeStruct((full, kv_width), F32),
        ],
        compiler_params=pltpu.CompilerParams(vmem_limit_bytes=32 * 2**20),
        cost_estimate=pl.CostEstimate(
            flops=10 * rows * full * width,
            bytes_accessed=8 * rows * width + 14 * full * kv_width,
            transcendentals=rows * full * width // HEAD_DIM,
        ),
    )(
        query_order,
        key_order,
        queries,
        dmixed,
        mixed,
        logs,
        cosine.T,
        sine.T,
        keys,
        values,
        keys.T,
    )


LINE_CHUNK = 32
LINE_WINDOW = 2
LINE_SKEW = 2
MESH_AXES = ("dp", "ctx", "tensor")
SPREAD_PIECES = 2


def pair_steps(sizes):
    steps = []
    for axis, size in zip(MESH_AXES, sizes):
        bit = 1
        while bit < size:
            steps.append((axis, bit))
            bit *= 2
    return steps


def partner(axis, bit):
    index = lax.axis_index(axis)
    return jnp.where((index // bit) % 2 == 0, index + bit, index - bit)


def line_kernel(size, chunk, returns, owners, pairs, side_count, out_count, *refs):
    streams = len(returns)
    returned = [k for k in range(streams) if returns[k]]
    parts, refs = refs[:streams], refs[streams:]
    sides, refs = refs[:side_count], refs[side_count:]
    shared, refs = dict(zip(returned, refs)), refs[len(returned) :]
    kept, refs = refs[:out_count], refs[out_count:]
    inbox, send_up, recv_up, send_back, recv_back = refs[:5]
    half = parts[0].shape[0] // 2
    count = half // chunk
    last = size - 1
    me = lax.axis_index("tensor")
    above, below = jnp.minimum(me + 1, last), jnp.maximum(me - 1, 0)
    flows = ((me, above, below), (last - me, below, above))

    barrier = pltpu.get_barrier_semaphore()

    def greet(axis, other):
        pl.semaphore_signal(
            barrier, inc=1, device_id={axis: other}, device_id_type=pl.DeviceIdType.MESH
        )

    if pairs:
        for axis, bit in pairs:
            greet(axis, partner(axis, bit))
        far_above = jnp.where(me % 2 == 0, 0, 1) * jnp.where(me < last, 1, 0)
        far_below = jnp.where(me % 2 == 0, 1, 0) * jnp.where(me > 0, 1, 0)
        pl.when(far_above == 1)(lambda: greet("tensor", above))
        pl.when(far_below == 1)(lambda: greet("tensor", below))
        pl.semaphore_wait(barrier, len(pairs) + far_above + far_below)
    else:
        pl.when(me < last)(lambda: greet("tensor", above))
        pl.when(me > 0)(lambda: greet("tensor", below))
        pl.semaphore_wait(barrier, jnp.where((me > 0) & (me < last), 2, 1))

    def place(f, i):
        return pl.ds(pl.multiple_of(f * half + i * chunk, chunk), chunk)

    def local(i):
        return pl.ds(pl.multiple_of(i * chunk, chunk), chunk)

    def onward(k, f, i, source):
        return pltpu.make_async_remote_copy(
            src_ref=source,
            dst_ref=inbox.at[k, f, local(i)],
            send_sem=send_up.at[k, f, i],
            recv_sem=recv_up.at[k, f, i],
            device_id={"tensor": flows[f][1]},
            device_id_type=pl.DeviceIdType.MESH,
        )

    def backward(k, f, i):
        block = shared[k].at[place(f, i)]
        return pltpu.make_async_remote_copy(
            src_ref=block,
            dst_ref=block,
            send_sem=send_back.at[k, f, i],
            recv_sem=recv_back.at[k, f, i],
            device_id={"tensor": flows[f][2]},
            device_id_type=pl.DeviceIdType.MESH,
        )

    def reduce_chunk(k, f, i):
        position = flows[f][0]
        mine = parts[k].at[place(f, i)]
        slot = inbox.at[k, f, local(i)]

        @pl.when(position == 0)
        def _():
            pl.when(i >= LINE_WINDOW)(lambda: onward(k, f, i - LINE_WINDOW, mine).wait_send())
            onward(k, f, i, mine).start()

        @pl.when(position > 0)
        def _():
            onward(k, f, i, slot).wait_recv()
            total = slot[...].astype(F32) + mine[...].astype(F32)

            @pl.when(position < last)
            def _():
                slot[...] = total.astype(BF16)
                onward(k, f, i, slot).start()

            @pl.when(position == last)
            def _():
                result = owners[k](total, place(f, i), local(i), sides, kept)
                if returns[k]:
                    shared[k][place(f, i), :] = result.astype(BF16)
                    backward(k, f, i).start()

    def pass_back(k, f, i):
        position = flows[f][0]

        @pl.when((position < last) & (i >= 0) & (i < count))
        def _():
            backward(k, f, i).wait_recv()
            pl.when(position > 0)(lambda: backward(k, f, i).start())

    def step(s, carry):
        for k in range(streams):
            for f in range(2):
                i = s - LINE_SKEW * flows[f][0]
                pl.when((i >= 0) & (i < count))(lambda: reduce_chunk(k, f, i))
        for k in returned:
            for f in range(2):
                pass_back(k, f, s - LINE_SKEW * (2 * last - flows[f][0]))
        for n in range(len(pairs) + 1 if pairs else 0):
            pl.when(s == n * gap)(lambda: advance_gains(n))
        return carry

    steps = count + 2 * LINE_SKEW * last
    gap = steps // (len(pairs) + 1)
    if pairs:
        slots, sums, send_pair, recv_pair = refs[5:]
        sums[0] = sides[-1][...]
    elif len(kept) > 1:
        kept[1][...] = jnp.zeros_like(kept[1])

    def swap_gains(n):
        return pltpu.make_async_remote_copy(
            src_ref=sums.at[n],
            dst_ref=slots.at[n],
            send_sem=send_pair.at[n],
            recv_sem=recv_pair.at[n],
            device_id={pairs[n][0]: partner(*pairs[n])},
            device_id_type=pl.DeviceIdType.MESH,
        )

    def advance_gains(n):
        if n > 0:
            swap_gains(n - 1).wait()
            sums[n] = sums[n - 1] + slots[n - 1]
        if n < len(pairs):
            swap_gains(n).start()
        else:
            kept[0][...] = sums[n]

    lax.fori_loop(0, steps, step, 0)

    def drain(i, carry):
        for k in range(streams):
            for f in range(2):
                position = flows[f][0]
                waited = (position == 0) & (i < count - LINE_WINDOW)
                pl.when((position < last) & ~waited)(
                    lambda: onward(k, f, i, inbox.at[k, f, local(i)]).wait_send()
                )
                if returns[k]:
                    pl.when(position > 0)(lambda: backward(k, f, i).wait_send())
        return carry

    lax.fori_loop(0, count, drain, 0)


def line_sum(parts, owners, sides, kept, collective_id, returns=(True,), pairs=()):
    rows, width = parts[0].shape
    size = lax.axis_size("tensor")
    streams = len(parts)
    chunk = max(16, min(LINE_CHUNK, rows // 32))
    count = rows // 2 // chunk
    whole = pl.BlockSpec(memory_space=pltpu.VMEM)
    scalar = pl.BlockSpec(memory_space=pltpu.SMEM)
    sems = pltpu.SemaphoreType.DMA((streams, 2, count))
    outs = [jax.ShapeDtypeStruct((rows, width), BF16)] * sum(returns) + list(kept)
    extra = []
    if pairs:
        pair_sems = pltpu.SemaphoreType.DMA((len(pairs),))
        extra = [
            pltpu.VMEM((len(pairs), 8, width), F32),
            pltpu.VMEM((len(pairs) + 1, 8, width), F32),
            pair_sems,
            pair_sems,
        ]
    return pl.pallas_call(
        functools.partial(
            line_kernel, size, chunk, returns, owners, pairs, len(sides), len(kept)
        ),
        out_shape=outs,
        in_specs=[whole] * streams + [scalar if s.ndim == 1 else whole for s in sides],
        out_specs=[whole] * len(outs),
        scratch_shapes=[pltpu.VMEM((streams, 2, rows // 2, width), BF16)] + [sems] * 4 + extra,
        compiler_params=pltpu.CompilerParams(
            collective_id=collective_id, has_side_effects=True, vmem_limit_bytes=56 * 2**20
        ),
        cost_estimate=pl.CostEstimate(
            flops=streams * rows * width,
            bytes_accessed=streams * 300 * 2**20,
            transcendentals=0,
        ),
    )(*parts, *sides)


def unit_of(rows):
    inverse = lax.rsqrt(jnp.mean(rows * rows, axis=-1, keepdims=True) + EPSILON)
    return rows * inverse, inverse


def own_hidden(total, where, here, sides, kept):
    x_ref, gain_ref = sides
    hidden = x_ref[where, :].astype(F32) + total
    kept[0][here, :] = hidden
    return unit_of(hidden)[0] * gain_ref[...]


def own_dhidden(total, where, here, sides, kept):
    x_ref, hidden_ref, cot_ref, gain_ref, factor = sides
    unit, inverse = unit_of(hidden_ref[here, :])
    kept[1][...] += jnp.sum(total * unit, axis=0, keepdims=True)
    dhidden = norm_back(total, unit, inverse, gain_ref[...])
    kept[0][here, :] = dhidden
    return cot_ref[where, :].astype(F32) * factor[0] + dhidden


def own_output(total, where, here, sides, kept):
    x_ref, hidden_ref, cot_ref, gain_ref, factor = sides
    x = x_ref[where, :].astype(F32)
    result = x + factor[1] * ((hidden_ref[here, :] - x) + total)
    kept[2][here, :] = result.astype(BF16)


def own_dinput(total, where, here, sides, kept):
    x_ref, dhidden_ref, gain_ref, _ = sides
    unit, inverse = unit_of(x_ref[where, :].astype(F32))
    return dhidden_ref[here, :] + norm_back(total, unit, inverse, gain_ref[...])


def cut_half(own):
    step = own.shape[0] // SPREAD_PIECES
    return [[own[p * step : (p + 1) * step]] for p in range(SPREAD_PIECES)]


def send_wave(pieces, wave):
    size = lax.axis_size("tensor")
    for p, hops in enumerate(pieces):
        h = wave - p
        if 0 <= h < size - 1:
            perm = [(size - 1 - h, size - 2 - h), (h, h + 1)]
            hops.append(lax.ppermute(hops[-1], "tensor", perm))


def tie(pieces, others):
    heads, others = lax.optimization_barrier(([hops[-1] for hops in pieces], others))
    for hops, head in zip(pieces, heads):
        hops[-1] = head
    return others


def join_kernel(size, *refs):
    pieces, out = refs[:-1], refs[-1]
    me = lax.axis_index("tensor")
    step = pieces[0].shape[0]
    half = out.shape[0] // 2
    for p in range(SPREAD_PIECES):
        for h in range(size):
            for f, wanted in enumerate((size - 1 - me, me)):

                @pl.when(wanted == h)
                def _():
                    out[pl.ds(f * half + p * step, step), :] = pieces[p * size + h][...]


def join_halves(pieces):
    size = lax.axis_size("tensor")
    step, width = pieces[0].shape
    whole = pl.BlockSpec(memory_space=pltpu.VMEM)
    return pl.pallas_call(
        functools.partial(join_kernel, size),
        out_shape=jax.ShapeDtypeStruct((2 * SPREAD_PIECES * step, width), BF16),
        in_specs=[whole] * len(pieces),
        out_specs=whole,
        compiler_params=pltpu.CompilerParams(vmem_limit_bytes=40 * 2**20),
    )(*pieces)


def rotary_tables(positions):
    inverse = 1.0 / 10000.0 ** (jnp.arange(0, HEAD_DIM, 2, dtype=F32) / HEAD_DIM)
    angle = positions.astype(F32)[:, None] * inverse[None, :]
    return (jnp.cos(angle), jnp.sin(angle))


def rotate(field, cosine, sine):
    half = field.shape[-1] // 2
    leading, trailing = (field[..., :half], field[..., half:])
    cosine, sine = (cosine[:, None, :], sine[:, None, :])
    return jnp.concatenate(
        [leading * cosine - trailing * sine, trailing * cosine + leading * sine], axis=-1
    )


def rotate_back(grad, cosine, sine):
    return rotate(grad, cosine, -sine)


def contract_rows(left, right):
    return jnp.einsum("rd,rf->df", left, right, preferred_element_type=F32)


def contract_cols(left, right):
    return jnp.einsum("rc,dc->rd", left, right, preferred_element_type=F32)


def norm_back(dnormed, unit, inverse, gain):
    scaled = dnormed * gain
    return inverse * (scaled - unit * jnp.mean(scaled * unit, axis=-1, keepdims=True))


def flags_kernel(size, mine, everyone, send_sem, recv_sem):
    me = lax.axis_index("dp")
    barrier = pltpu.get_barrier_semaphore()
    others = [lax.rem(me + s, size) for s in range(1, size)]
    for other in others:
        pl.semaphore_signal(
            barrier, inc=1, device_id={"dp": other}, device_id_type=pl.DeviceIdType.MESH
        )
    pl.semaphore_wait(barrier, size - 1)

    def send(s, slot):
        return pltpu.make_async_remote_copy(
            src_ref=mine,
            dst_ref=everyone.at[slot],
            send_sem=send_sem.at[s],
            recv_sem=recv_sem.at[s],
            device_id={"dp": others[s]},
            device_id_type=pl.DeviceIdType.MESH,
        )

    for s in range(size - 1):
        send(s, me).start()
    everyone[me] = mine[...]
    for s in range(size - 1):
        send(s, me).wait_send()
        send(s, lax.rem(me + 2 * size - 1 - s, size)).wait_recv()


def share_flags(row):
    size = lax.axis_size("dp")
    tile = jnp.zeros((8, 128), jnp.int32).at[0, : row.shape[0]].set(row)
    sems = pltpu.SemaphoreType.DMA((size - 1,))
    whole = pl.BlockSpec(memory_space=pltpu.VMEM)
    shared = pl.pallas_call(
        functools.partial(flags_kernel, size),
        out_shape=jax.ShapeDtypeStruct((size, 8, 128), jnp.int32),
        in_specs=[whole],
        out_specs=whole,
        scratch_shapes=[sems, sems],
        compiler_params=pltpu.CompilerParams(collective_id=1, has_side_effects=True),
    )(tile)
    return shared[:, 0, : row.shape[0]]


def shift_ctx(part, s):
    size = lax.axis_size("ctx")
    return lax.ppermute(part, "ctx", [(i, (i + s) % size) for i in range(size)])


def swap_core(part):
    return lax.ppermute(part, "dp", [(i, i ^ 1) for i in range(lax.axis_size("dp"))])


def gather_parts(own, paired):
    parts = []
    for s in range(lax.axis_size("ctx")):
        here = own if s == 0 else shift_ctx(own, s)
        parts += [here, swap_core(here)] if paired else [here]
    return parts


def collect_parts(parts, paired):
    total = None
    for s in range(lax.axis_size("ctx")):
        if paired:
            near, far = parts[2 * s], parts[2 * s + 1]
            near = near + swap_core(far.astype(BF16)).astype(F32)
        else:
            near = parts[s]
        total = near if s == 0 else total + shift_ctx(near.astype(BF16), -s).astype(F32)
    return total


def block_pass(
    paired,
    first_id,
    span,
    x_low,
    cot_low,
    keep,
    scale,
    order_row,
    attn_gain,
    ffn_gain,
    w_query,
    w_key,
    w_value,
    w_output,
    w_gate,
    w_up,
    w_down,
):
    rows, width = x_low.shape
    dp_size, ctx_size = lax.axis_size("dp"), lax.axis_size("ctx")
    spans = order_row.shape[0]
    kv_local = w_key.shape[1] // HEAD_DIM
    ctx = lax.axis_index("ctx")
    core = lax.axis_index("dp") % 2
    per_part = rows // span
    order_parts = []
    for s in range(ctx_size):
        group = (ctx + ctx_size - s) % ctx_size
        places = [group * 2 + core, group * 2 + 1 - core] if paired else [group]
        order_parts += [
            lax.dynamic_slice_in_dim(order_row, place * per_part, per_part) for place in places
        ]
    query_order, key_order = order_parts[0], jnp.concatenate(order_parts)
    row_index = jnp.arange(rows, dtype=jnp.int32)
    starts = jnp.sum(
        jnp.where(
            (row_index // span)[:, None] == jnp.arange(per_part, dtype=jnp.int32)[None, :],
            query_order[None, :],
            0,
        ),
        axis=1,
    )
    cosine, sine = rotary_tables(starts * span + row_index % span)

    flat = x_low.astype(F32)
    inv_one = lax.rsqrt(jnp.mean(flat * flat, axis=-1, keepdims=True) + EPSILON)
    normed_one = (flat * inv_one * attn_gain).astype(BF16)
    k_proj = nn_dot(normed_one, w_key).reshape(rows, kv_local, HEAD_DIM)
    keys_own = rotate(k_proj, cosine, sine).astype(BF16).reshape(rows, -1)
    values_own = nn_dot(normed_one, w_value).astype(BF16)
    keys = jnp.concatenate(gather_parts(keys_own, paired), 0)
    values = jnp.concatenate(gather_parts(values_own, paired), 0)
    q_proj = nn_dot(normed_one, w_query).reshape(rows, -1, HEAD_DIM)
    queries = rotate(q_proj, cosine, sine).astype(BF16).reshape(rows, -1)
    mixed, logs = attend(queries, keys, values, query_order, key_order, span)

    half_rows = jax.ShapeDtypeStruct((rows // 2, width), F32)
    gain_row = jax.ShapeDtypeStruct((1, width), F32)
    ffn_row, attn_row = ffn_gain[None, :], attn_gain[None, :]
    attn_part = nn_dot(mixed, w_output).astype(BF16)
    normed_two, hidden = line_sum(
        [attn_part], [own_hidden], [x_low, ffn_row], [half_rows], first_id
    )

    dffn = (cot_low.astype(F32) * (keep * scale)).astype(BF16)
    dacted = contract_cols(dffn, w_down)
    gate = nn_dot(normed_two, w_gate)
    upward = nn_dot(normed_two, w_up)
    sigmoid_gate = jax.nn.sigmoid(gate)
    silu_gate = gate * sigmoid_gate
    acted = (silu_gate * upward).astype(BF16)
    dgate = (dacted * upward * sigmoid_gate * (1.0 + gate * (1.0 - sigmoid_gate))).astype(BF16)
    dupward = (dacted * silu_gate).astype(BF16)
    ffn_grads = (
        contract_rows(acted, dffn).astype(BF16),
        contract_rows(normed_two, dgate).astype(BF16),
        contract_rows(normed_two, dupward).astype(BF16),
    )
    acted, dgate, dupward, ffn_grads = lax.optimization_barrier((acted, dgate, dupward, ffn_grads))
    ffn_grads = lax.psum(ffn_grads, ("dp", "ctx"))
    dnormed_part = (contract_cols(dgate, w_gate) + contract_cols(dupward, w_up)).astype(BF16)
    ffn_part = nn_dot(acted, w_down).astype(BF16)
    dattn, dhidden, ffn_gain_part, output_half = line_sum(
        [dnormed_part, ffn_part],
        [own_dhidden, own_output],
        [x_low, hidden, cot_low, ffn_row, jnp.stack([keep * scale, keep])],
        [half_rows, gain_row, jax.ShapeDtypeStruct((rows // 2, width), BF16)],
        first_id + 1,
        (True, False),
    )
    pieces = cut_half(output_half)
    send_wave(pieces, 0)
    grad_output = contract_rows(mixed, dattn)
    dmixed = contract_cols(dattn, w_output).astype(BF16)
    dq_proj, dkeys, dvalues = attend_back(
        queries, dmixed, mixed, logs, cosine, sine, keys, values, query_order, key_order, span
    )
    dq_proj, dkeys, dvalues = tie(pieces, (dq_proj, dkeys, dvalues))
    send_wave(pieces, 1)
    split = lambda grad: [grad[p * rows : (p + 1) * rows] for p in range(grad.shape[0] // rows)]
    dk_own = collect_parts(split(dkeys), paired).reshape(rows, kv_local, HEAD_DIM)
    dk_proj = rotate_back(dk_own, cosine, sine).reshape(rows, -1).astype(BF16)
    dv_proj = collect_parts(split(dvalues), paired).astype(BF16)
    dk_proj, dv_proj = tie(pieces, (dk_proj, dv_proj))
    send_wave(pieces, 2)
    dnormed_one = (
        contract_cols(dq_proj, w_query)
        + contract_cols(dk_proj, w_key)
        + contract_cols(dv_proj, w_value)
    )
    attn_gain_part = jnp.sum(dnormed_one * (flat * inv_one), axis=0, keepdims=True)
    gain_parts = jnp.concatenate(
        [attn_gain_part, ffn_gain_part, jnp.zeros((6, width), F32)], axis=0
    )
    dnormed_one = dnormed_one.astype(BF16)
    attn_grads = (
        contract_rows(normed_one, dq_proj).astype(BF16),
        contract_rows(normed_one, dk_proj).astype(BF16),
        contract_rows(normed_one, dv_proj).astype(BF16),
        grad_output.astype(BF16),
    )
    dnormed_one, attn_grads, ffn_grads = tie(pieces, (dnormed_one, attn_grads, ffn_grads))
    for wave in range(3, lax.axis_size("tensor") + SPREAD_PIECES):
        send_wave(pieces, wave)
    attn_grads = lax.psum(attn_grads, ("ctx", "dp"))
    pairs = pair_steps((dp_size, ctx_size, lax.axis_size("tensor")))
    through, gains = line_sum(
        [dnormed_one],
        [own_dinput],
        [x_low, dhidden, attn_row, gain_parts],
        [jax.ShapeDtypeStruct((8, width), F32)],
        first_id + 2,
        (True,),
        tuple(pairs),
    )
    through, gains, attn_grads, ffn_grads, pieces = lax.optimization_barrier(
        (through, gains, attn_grads, ffn_grads, pieces)
    )
    return join_halves([hop for hops in pieces for hop in hops]), through, gains, attn_grads, ffn_grads


def per_device(
    inputs,
    cotangent,
    skip_mask,
    group_ids,
    span_order,
    exit_scale,
    attn_gain,
    ffn_gain,
    *weights,
):
    _, rows, width = inputs.shape
    spans = span_order.shape[1]
    own_spans = spans // lax.axis_size("ctx")
    span = rows // own_spans
    me = lax.axis_index("dp")
    core = me % 2
    x_low, cot_low = inputs[0], cotangent[0]
    flags = share_flags(jnp.concatenate([skip_mask, group_ids, span_order[0]]))
    runs, groups = flags[:, 0], flags[:, 1]
    scale_of = lambda group: jnp.where(group == 1, exit_scale[1], exit_scale[0])
    own_run, own_scale = skip_mask[0], scale_of(group_ids[0])
    gains = (attn_gain, ffn_gain)

    def alone():
        return block_pass(
            False,
            2,
            span,
            x_low,
            cot_low,
            own_run.astype(F32),
            own_scale,
            span_order[0],
            *gains,
            *weights,
        )

    def shared():
        half = rows // 2
        other = me + 1 - 2 * core
        take = lambda a, i: lax.dynamic_slice_in_dim(a, i * half, half, 0)
        pick = lambda a: lax.dynamic_index_in_dim(a, other, 0, keepdims=False)
        other_run = pick(runs)
        use_own = (own_run == 1) | ((other_run == 0) & (core == 0))
        choose = lambda mine, theirs: jnp.where(use_own, mine, theirs)
        work = lambda a: choose(take(a, core), swap_core(take(a, 1 - core)))
        output, through, *rest = block_pass(
            True,
            5,
            span,
            work(x_low),
            work(cot_low),
            choose(own_run, other_run).astype(F32),
            choose(own_scale, scale_of(pick(groups))),
            choose(span_order[0], pick(flags[:, 2:])),
            *gains,
            *weights,
        )

        def whole(part, idle):
            theirs = swap_core(part)
            first, second = jnp.where(core == 0, part, theirs), jnp.where(core == 0, theirs, part)
            return jnp.where(own_run == 1, jnp.concatenate([first, second], 0), idle)

        return whole(output, x_low), whole(through, jnp.zeros_like(x_low)), *rest

    def finish(output, through, sums, attn_grads, ffn_grads):
        input_grad = cot_low.astype(F32) * own_scale + through.astype(F32)
        grads = [g.astype(F32) for g in attn_grads + ffn_grads]
        return lax.optimization_barrier((output, input_grad, sums[0], sums[1], *grads))

    if own_spans % 2 == 0 and lax.axis_size("dp") % 2 == 0:
        pairs = runs.reshape(-1, 2)
        results = lax.cond(
            jnp.all(pairs[:, 0] * pairs[:, 1] == 0),
            lambda: finish(*shared()),
            lambda: finish(*alone()),
        )
    else:
        results = finish(*alone())
    output, input_grad, grad_attn_gain, grad_ffn_gain = results[:4]
    grad_query, grad_key, grad_value, grad_output, grad_down, grad_gate, grad_up = results[4:]
    return (
        output.reshape(inputs.shape),
        input_grad.reshape(inputs.shape),
        grad_attn_gain,
        grad_ffn_gain,
        grad_query,
        grad_key,
        grad_value,
        grad_output,
        grad_gate,
        grad_up,
        grad_down,
    )


def solution(mesh):
    rows = P("dp", "ctx", None)
    by_column, by_row = P(None, "tensor"), P("tensor", None)
    in_specs = (rows, rows, P("dp"), P("dp"), P("dp", None), P(), P(), P())
    in_specs += (by_column,) * 3 + (by_row,) + (by_column,) * 2 + (by_row,)
    out_specs = (rows, rows, P(), P()) + (by_column,) * 3 + (by_row,) + (by_column,) * 2 + (by_row,)
    return jax.shard_map(
        per_device, mesh=mesh, in_specs=in_specs, out_specs=out_specs, check_vma=False
    )
```

```python
import functools

import jax
import jax.numpy as jnp
from jax import lax
from jax.experimental import pallas as pl
from jax.experimental.pallas import tpu as pltpu
from jax.sharding import PartitionSpec as P

HEAD_DIM = 128
EPSILON = 1e-05
NEG_BIG = -1e30
FACTOR = HEAD_DIM ** (-0.5)
LOG2E = 1.4426950408889634
QUERY_BLOCK = 256
BF16 = jnp.bfloat16
F32 = jnp.float32

NT = (((1,), (1,)), ((), ()))


def nt_dot(left, right):
    return lax.dot_general(left, right, NT, preferred_element_type=F32)


def nn_dot(left, right):
    return jnp.dot(left, right, preferred_element_type=F32)


def stack_heads(block, group):
    return jnp.concatenate(
        [block[:, h * HEAD_DIM : (h + 1) * HEAD_DIM] for h in range(group)], axis=0
    )


def hide_later(scores, first_row, rows, fill):
    key_row = lax.broadcasted_iota(jnp.int32, scores.shape, 0)
    query_row = lax.broadcasted_iota(jnp.int32, scores.shape, 1) % rows + first_row
    return jnp.where(key_row <= query_row, scores, fill)


def over_spans(kv_refs, span, visit, query_order, key_order, first):
    order = query_order[first // span]
    seen = 0
    for part, kv_ref in enumerate(kv_refs):
        count = kv_ref.shape[1] // span

        def one_span(j, carry, part=part, seen=seen):
            place = pl.multiple_of(j * span, span)
            column = pl.multiple_of((seen + j) * span, span)
            pl.when(key_order[seen + j] < order)(lambda: visit(part, place, column, False))
            pl.when(key_order[seen + j] == order)(lambda: visit(part, place, column, True))
            return carry

        lax.fori_loop(0, count, one_span, 0)
        seen += count


def attend_kernel(group, span, parts, query_order, key_order, q_ref, *refs):
    kv_refs, (o_ref, lse_ref, vt_ref, top, total, acc) = refs[:parts], refs[parts:]
    rows = q_ref.shape[0]
    step = pl.program_id(1)
    first = step * rows

    @pl.when(step == 0)
    def _():
        for part, kv_ref in enumerate(kv_refs):
            size = kv_ref.shape[1]
            vt_ref[:, part * size : (part + 1) * size] = kv_ref[1].T

    queries = stack_heads(q_ref[...], group)
    top[...] = jnp.full_like(top, NEG_BIG)
    total[...] = jnp.zeros_like(total)
    acc[...] = jnp.zeros_like(acc)

    def visit(part, place, column, diagonal):
        keys = kv_refs[part][0, pl.ds(place, span), :]
        scores = nt_dot(keys, queries) * (FACTOR * LOG2E)
        if diagonal:
            scores = hide_later(scores, first % span, rows, NEG_BIG)
        before = top[...]
        now = jnp.maximum(before, jnp.max(scores, axis=0, keepdims=True))
        weights = jnp.exp2(scores - now)
        shrink = jnp.exp2(before - now)
        top[...] = now
        total[...] = total[...] * shrink + jnp.sum(weights, axis=0, keepdims=True)
        acc[...] = acc[...] * shrink + nn_dot(
            vt_ref[:, pl.ds(column, span)], weights.astype(BF16)
        )

    over_spans(kv_refs, span, visit, query_order, key_order, first)
    mixed = acc[...] / total[...]
    logs = top[...] + jnp.log2(total[...])
    for h in range(group):
        part = slice(h * rows, (h + 1) * rows)
        o_ref[:, h * HEAD_DIM : (h + 1) * HEAD_DIM] = mixed[:, part].T.astype(BF16)
        lse_ref[0, h : h + 1, :] = logs[:, part]


def attend(queries, kv_parts, query_order, key_order, span):
    rows, width = queries.shape
    part_rows, kv_width = kv_parts[0].shape[1:]
    full = part_rows * len(kv_parts)
    kv_heads = kv_width // HEAD_DIM
    group = width // kv_width
    block = min(QUERY_BLOCK, span)
    query_spec = pl.BlockSpec((block, group * HEAD_DIM), lambda g, i, *_: (i, g))
    kv_spec = pl.BlockSpec((2, part_rows, HEAD_DIM), lambda g, i, *_: (0, 0, g))
    return pl.pallas_call(
        functools.partial(attend_kernel, group, span, len(kv_parts)),
        grid_spec=pltpu.PrefetchScalarGridSpec(
            num_scalar_prefetch=2,
            grid=(kv_heads, rows // block),
            in_specs=[query_spec] + [kv_spec] * len(kv_parts),
            out_specs=[
                query_spec,
                pl.BlockSpec((1, group, block), lambda g, i, *_: (g, 0, i)),
            ],
            scratch_shapes=[
                pltpu.VMEM((HEAD_DIM, full), BF16),
                pltpu.VMEM((1, group * block), F32),
                pltpu.VMEM((1, group * block), F32),
                pltpu.VMEM((HEAD_DIM, group * block), F32),
            ],
        ),
        out_shape=[
            jax.ShapeDtypeStruct((rows, width), BF16),
            jax.ShapeDtypeStruct((kv_heads, group, rows), F32),
        ],
        compiler_params=pltpu.CompilerParams(vmem_limit_bytes=32 * 2**20),
        cost_estimate=pl.CostEstimate(
            flops=4 * rows * full * width,
            bytes_accessed=4 * rows * width + 4 * full * kv_width,
            transcendentals=rows * full * width // HEAD_DIM,
        ),
    )(query_order, key_order, queries, *kv_parts)


def attend_back_kernel(
    group,
    span,
    parts,
    query_order,
    key_order,
    q_ref,
    do_ref,
    o_ref,
    lse_ref,
    cos_ref,
    sin_ref,
    *refs,
):
    kv_refs, dq_ref, dkv_refs = refs[:parts], refs[parts], refs[parts + 1 : 2 * parts + 1]
    kt_ref, acc, sums = refs[2 * parts + 1 :]
    rows = q_ref.shape[0]
    step = pl.program_id(1)
    first = step * rows
    queries = stack_heads(q_ref[...], group)
    dmixed = stack_heads(do_ref[...], group)
    mixed = stack_heads(o_ref[...], group)
    product = dmixed.astype(F32) * mixed.astype(F32)
    delta = jnp.sum(product.T, axis=0, keepdims=True)
    logs = jnp.concatenate([lse_ref[0, h : h + 1, :] for h in range(group)], axis=1)
    acc[...] = jnp.zeros_like(acc)

    @pl.when(step == 0)
    def _():
        sums[...] = jnp.zeros_like(sums)
        for part, kv_ref in enumerate(kv_refs):
            size = kv_ref.shape[1]
            kt_ref[:, part * size : (part + 1) * size] = kv_ref[0].T

    def visit(part, place, column, diagonal):
        here = pl.ds(place, span)
        scores = nt_dot(kv_refs[part][0, here, :], queries) * (FACTOR * LOG2E)
        probs = jnp.exp2(scores - logs)
        if diagonal:
            probs = hide_later(probs, first % span, rows, 0.0)
        dprobs = nt_dot(kv_refs[part][1, here, :], dmixed)
        dscore = (probs * (dprobs - delta)).astype(BF16)
        sums[part, 1, here, :] += nn_dot(probs.astype(BF16), dmixed)
        sums[part, 0, here, :] += nn_dot(dscore, queries)
        acc[...] += nn_dot(kt_ref[:, pl.ds(column, span)], dscore)

    over_spans(kv_refs, span, visit, query_order, key_order, first)
    for h in range(group):
        grad = acc[:, h * rows : (h + 1) * rows] * FACTOR
        half = HEAD_DIM // 2
        leading, trailing = grad[:half], grad[half:]
        cosine, sine = cos_ref[...], sin_ref[...]
        turned = jnp.concatenate(
            [leading * cosine + trailing * sine, trailing * cosine - leading * sine], axis=0
        )
        dq_ref[:, h * HEAD_DIM : (h + 1) * HEAD_DIM] = turned.T.astype(BF16)

    @pl.when(step == pl.num_programs(1) - 1)
    def _():
        for part, dkv_ref in enumerate(dkv_refs):
            dkv_ref[0] = (sums[part, 0] * FACTOR).astype(dkv_ref.dtype)
            dkv_ref[1] = sums[part, 1].astype(dkv_ref.dtype)


def attend_back(
    queries, dmixed, mixed, logs, cosine, sine, kv_parts, query_order, key_order, span
):
    rows, width = queries.shape
    part_rows, kv_width = kv_parts[0].shape[1:]
    parts = len(kv_parts)
    full = part_rows * parts
    kv_heads = kv_width // HEAD_DIM
    group = width // kv_width
    block = min(QUERY_BLOCK, span)
    half = HEAD_DIM // 2
    query_spec = pl.BlockSpec((block, group * HEAD_DIM), lambda g, i, *_: (i, g))
    kv_spec = pl.BlockSpec((2, part_rows, HEAD_DIM), lambda g, i, *_: (0, 0, g))
    table_spec = pl.BlockSpec((half, block), lambda g, i, *_: (0, i))
    kinds = [F32] + [BF16] * (parts - 1)
    return pl.pallas_call(
        functools.partial(attend_back_kernel, group, span, parts),
        grid_spec=pltpu.PrefetchScalarGridSpec(
            num_scalar_prefetch=2,
            grid=(kv_heads, rows // block),
            in_specs=[
                query_spec,
                query_spec,
                query_spec,
                pl.BlockSpec((1, group, block), lambda g, i, *_: (g, 0, i)),
                table_spec,
                table_spec,
            ]
            + [kv_spec] * parts,
            out_specs=[query_spec] + [kv_spec] * parts,
            scratch_shapes=[
                pltpu.VMEM((HEAD_DIM, full), BF16),
                pltpu.VMEM((HEAD_DIM, group * block), F32),
                pltpu.VMEM((parts, 2, part_rows, HEAD_DIM), F32),
            ],
        ),
        out_shape=[jax.ShapeDtypeStruct((rows, width), BF16)]
        + [jax.ShapeDtypeStruct((2, part_rows, kv_width), kind) for kind in kinds],
        compiler_params=pltpu.CompilerParams(vmem_limit_bytes=40 * 2**20),
        cost_estimate=pl.CostEstimate(
            flops=10 * rows * full * width,
            bytes_accessed=8 * rows * width + 14 * full * kv_width,
            transcendentals=rows * full * width // HEAD_DIM,
        ),
    )(
        query_order,
        key_order,
        queries,
        dmixed,
        mixed,
        logs,
        cosine.T,
        sine.T,
        *kv_parts,
    )


ROW_BLOCK = 256


def by_rows(block, width):
    return pl.BlockSpec((block, width), lambda i: (i, 0))


def held(array):
    return pl.BlockSpec(
        array.shape, lambda i: (0,) * array.ndim, pipeline_mode=pl.Buffered(1)
    )


def column_cuts(width, size=512):
    return [slice(c, min(c + size, width)) for c in range(0, width, size)]


def turn(field, cosine, sine):
    return field * cosine + pltpu.roll(field, HEAD_DIM // 2, 1) * sine


def project_kernel(x_ref, gain_ref, cos_ref, sin_ref, wq, wk, wv, n_ref, q_ref, kv_ref):
    unit, _ = unit_of(x_ref[...].astype(F32))
    normed = (unit * gain_ref[...]).astype(BF16)
    n_ref[...] = normed
    cosine, sine = cos_ref[...], sin_ref[...]
    queries, keys = nn_dot(normed, wq[...]), nn_dot(normed, wk[...])
    for h in range(q_ref.shape[1] // HEAD_DIM):
        head = slice(h * HEAD_DIM, (h + 1) * HEAD_DIM)
        q_ref[:, head] = turn(queries[:, head], cosine, sine).astype(BF16)
    for h in range(kv_ref.shape[2] // HEAD_DIM):
        head = slice(h * HEAD_DIM, (h + 1) * HEAD_DIM)
        kv_ref[0, :, head] = turn(keys[:, head], cosine, sine).astype(BF16)
    kv_ref[1] = nn_dot(normed, wv[...]).astype(BF16)


def project(x_low, gain_row, cosine, sine, w_query, w_key, w_value):
    rows, width = x_low.shape
    block = min(ROW_BLOCK, rows)
    heads_width, kv_width = w_query.shape[1], w_key.shape[1]
    return pl.pallas_call(
        project_kernel,
        grid=(rows // block,),
        in_specs=[
            by_rows(block, width),
            held(gain_row),
            by_rows(block, HEAD_DIM),
            by_rows(block, HEAD_DIM),
            held(w_query),
            held(w_key),
            held(w_value),
        ],
        out_specs=[
            by_rows(block, width),
            by_rows(block, heads_width),
            pl.BlockSpec((2, block, kv_width), lambda i: (0, i, 0)),
        ],
        out_shape=[
            jax.ShapeDtypeStruct((rows, width), BF16),
            jax.ShapeDtypeStruct((rows, heads_width), BF16),
            jax.ShapeDtypeStruct((2, rows, kv_width), BF16),
        ],
        compiler_params=pltpu.CompilerParams(vmem_limit_bytes=40 * 2**20),
        cost_estimate=pl.CostEstimate(
            flops=2 * rows * width * (heads_width + 2 * kv_width),
            bytes_accessed=6 * rows * width + 2 * width * (heads_width + 2 * kv_width),
            transcendentals=rows,
        ),
    )(x_low, gain_row, cosine, sine, w_query, w_key, w_value)


def hidden_kernel(n_ref, cot_ref, factor, wg, wu, wd, df_ref, a_ref, dg_ref, du_ref):
    dffn = (cot_ref[...].astype(F32) * factor[0]).astype(BF16)
    df_ref[...] = dffn
    normed = n_ref[...]
    for cut in column_cuts(a_ref.shape[1]):
        gate, upward = nn_dot(normed, wg[:, cut]), nn_dot(normed, wu[:, cut])
        dacted = nt_dot(dffn, wd[cut, :])
        sigmoid = jax.nn.sigmoid(gate)
        silu = gate * sigmoid
        a_ref[:, cut] = (silu * upward).astype(BF16)
        slope = sigmoid * (1.0 + gate * (1.0 - sigmoid))
        dg_ref[:, cut] = (dacted * upward * slope).astype(BF16)
        du_ref[:, cut] = (dacted * silu).astype(BF16)


def hidden_units(normed, cot_low, factor, w_gate, w_up, w_down):
    rows, width = normed.shape
    units = w_gate.shape[1]
    block = min(ROW_BLOCK, rows)
    return pl.pallas_call(
        hidden_kernel,
        grid=(rows // block,),
        in_specs=[
            by_rows(block, width),
            by_rows(block, width),
            pl.BlockSpec(memory_space=pltpu.SMEM),
            held(w_gate),
            held(w_up),
            held(w_down),
        ],
        out_specs=[by_rows(block, width)] + [by_rows(block, units)] * 3,
        out_shape=[jax.ShapeDtypeStruct((rows, width), BF16)]
        + [jax.ShapeDtypeStruct((rows, units), BF16)] * 3,
        compiler_params=pltpu.CompilerParams(vmem_limit_bytes=50 * 2**20),
        cost_estimate=pl.CostEstimate(
            flops=6 * rows * width * units,
            bytes_accessed=6 * rows * width + 6 * width * units + 6 * rows * units,
            transcendentals=rows * units,
        ),
    )(normed, cot_low, factor, w_gate, w_up, w_down)


def parts_kernel(a_ref, dg_ref, du_ref, wg, wu, wd, dn_ref, f_ref):
    for cut in column_cuts(dn_ref.shape[1]):
        dnormed = nt_dot(dg_ref[...], wg[cut, :]) + nt_dot(du_ref[...], wu[cut, :])
        dn_ref[:, cut] = dnormed.astype(BF16)
        f_ref[:, cut] = nn_dot(a_ref[...], wd[:, cut]).astype(BF16)


def width_parts(acted, dgate, dupward, w_gate, w_up, w_down):
    rows, units = acted.shape
    width = w_gate.shape[0]
    block = min(ROW_BLOCK, rows)
    return pl.pallas_call(
        parts_kernel,
        grid=(rows // block,),
        in_specs=[by_rows(block, units)] * 3 + [held(w) for w in (w_gate, w_up, w_down)],
        out_specs=[by_rows(block, width)] * 2,
        out_shape=[jax.ShapeDtypeStruct((rows, width), BF16)] * 2,
        compiler_params=pltpu.CompilerParams(vmem_limit_bytes=50 * 2**20),
        cost_estimate=pl.CostEstimate(
            flops=6 * rows * width * units,
            bytes_accessed=4 * rows * width + 6 * width * units + 6 * rows * units,
            transcendentals=0,
        ),
    )(acted, dgate, dupward, w_gate, w_up, w_down)


def project_back_kernel(
    addends, x_ref, dq_ref, cos_ref, sin_ref, wq, wk, wv, *refs
):
    terms, (dqkv_ref, dn_ref, gain_ref) = refs[:addends], refs[addends:]
    heads_width, kv_width = dq_ref.shape[1], terms[0].shape[2]
    dqkv_ref[:, :heads_width] = dq_ref[...]
    cosine, sine = cos_ref[...], -sin_ref[...]
    dkeys, dvalues = terms[0][0], terms[0][1]
    for term in terms[1:]:
        dkeys, dvalues = dkeys + term[0].astype(F32), dvalues + term[1].astype(F32)
    for h in range(kv_width // HEAD_DIM):
        head = slice(h * HEAD_DIM, (h + 1) * HEAD_DIM)
        place = slice(heads_width + h * HEAD_DIM, heads_width + (h + 1) * HEAD_DIM)
        dqkv_ref[:, place] = turn(dkeys[:, head], cosine, sine).astype(BF16)
    dqkv_ref[:, heads_width + kv_width :] = dvalues.astype(BF16)
    dk = slice(heads_width, heads_width + kv_width)
    dv = slice(heads_width + kv_width, heads_width + 2 * kv_width)
    unit, _ = unit_of(x_ref[...].astype(F32))

    @pl.when(pl.program_id(0) == 0)
    def _():
        gain_ref[...] = jnp.zeros_like(gain_ref)

    for cut in column_cuts(dn_ref.shape[1]):
        dnormed = nt_dot(dq_ref[...], wq[cut, :])
        dnormed = dnormed + nt_dot(dqkv_ref[:, dk], wk[cut, :]) + nt_dot(dqkv_ref[:, dv], wv[cut, :])
        dn_ref[:, cut] = dnormed.astype(BF16)
        gain_ref[:, cut] += jnp.sum(dnormed * unit[:, cut], axis=0, keepdims=True)


def project_back(x_low, dq, terms, cosine, sine, w_query, w_key, w_value):
    rows, width = x_low.shape
    block = min(ROW_BLOCK, rows)
    heads_width, kv_width = w_query.shape[1], w_key.shape[1]
    kv_spec = pl.BlockSpec((2, block, kv_width), lambda i: (0, i, 0))
    return pl.pallas_call(
        functools.partial(project_back_kernel, len(terms)),
        grid=(rows // block,),
        in_specs=[
            by_rows(block, width),
            by_rows(block, heads_width),
            by_rows(block, HEAD_DIM),
            by_rows(block, HEAD_DIM),
            held(w_query),
            held(w_key),
            held(w_value),
        ]
        + [kv_spec] * len(terms),
        out_specs=[
            by_rows(block, heads_width + 2 * kv_width),
            by_rows(block, width),
            pl.BlockSpec((1, width), lambda i: (0, 0)),
        ],
        out_shape=[
            jax.ShapeDtypeStruct((rows, heads_width + 2 * kv_width), BF16),
            jax.ShapeDtypeStruct((rows, width), BF16),
            jax.ShapeDtypeStruct((1, width), F32),
        ],
        compiler_params=pltpu.CompilerParams(vmem_limit_bytes=40 * 2**20),
        cost_estimate=pl.CostEstimate(
            flops=2 * rows * width * (heads_width + 2 * kv_width),
            bytes_accessed=6 * rows * width + 2 * width * (heads_width + 2 * kv_width),
            transcendentals=rows,
        ),
    )(x_low, dq, cosine, sine, w_query, w_key, w_value, *terms)


LINE_CHUNK = 32
LINE_WINDOW = 2
LINE_SKEW = 2
MESH_AXES = ("dp", "ctx", "tensor")
SPREAD_PIECES = 2
PLANE_ROWS = 16
PLANE_SKEW = 2


def pair_steps(sizes):
    steps = []
    for axis, size in zip(MESH_AXES, sizes):
        bit = 1
        while bit < size:
            steps.append((axis, bit))
            bit *= 2
    return steps


def partner(axis, bit):
    index = lax.axis_index(axis)
    return jnp.where((index // bit) % 2 == 0, index + bit, index - bit)


def plane_steps(dp_size, ctx_size):
    across, along, bit = [], [], 1
    while bit < ctx_size:
        across.append(("ctx", bit))
        bit *= 2
    bit = 2
    while bit < dp_size:
        along.append(("dp", bit))
        bit *= 2
    first = [(("dp", 1), ("dp", 1))] if dp_size > 1 else []
    return tuple(first + list(zip(across + along, along + across)))


class PlaneSum:
    def __init__(self, stages, sources, out, inbox, send_sem, recv_sem):
        self.stages, self.sources, self.out, self.inbox = stages, sources, out, inbox
        self.send_sem, self.recv_sem = send_sem, recv_sem
        self.unit = 2 ** len(stages) * PLANE_ROWS
        self.count = out.shape[0] // self.unit
        odd = lax.axis_index("dp") % 2
        self.bits, self.peers = [], []
        for even_step, odd_step in stages:
            ids = {}
            for axis, bit, here in ((*even_step, odd == 0), (*odd_step, odd == 1)):
                index = ids.get(axis, lax.axis_index(axis))
                ids[axis] = jnp.where(here, partner(axis, bit), index)
            pick = lambda step: (lax.axis_index(step[0]) // step[1]) % 2
            self.bits.append(jnp.where(odd == 0, pick(even_step), pick(odd_step)))
            self.peers.append(ids)

    def start_row(self, c, k):
        row = c * self.unit
        for n in range(k):
            row = row + self.bits[n] * (self.unit >> (n + 1))
        return row

    def rows(self, start, size):
        return pl.ds(pl.multiple_of(start, PLANE_ROWS), size)

    def copy(self, slot, c, peer, source, target):
        return pltpu.make_async_remote_copy(
            src_ref=source,
            dst_ref=target,
            send_sem=self.send_sem.at[slot, c],
            recv_sem=self.recv_sem.at[slot, c],
            device_id=peer,
            device_id_type=pl.DeviceIdType.MESH,
        )

    def inward(self, k, c, source_ref, base):
        size = self.unit >> (k + 1)
        start = self.start_row(c, k) + (1 - self.bits[k]) * size - base
        target = self.inbox[k].at[self.rows(c * size, size)]
        return self.copy(k, c, self.peers[k], source_ref.at[self.rows(start, size)], target)

    def inward_wait(self, k, c):
        size = self.unit >> (k + 1)
        target = self.inbox[k].at[self.rows(c * size, size)]
        return self.copy(k, c, self.peers[k], target, target)

    def outward(self, k, c):
        size = self.unit >> (k + 1)
        block = self.out.at[self.rows(self.start_row(c, k + 1), size)]
        return self.copy(2 * len(self.stages) - 1 - k, c, self.peers[k], block, block)

    def at_source(self, c, act):
        base = 0
        for ref in self.sources:
            height = ref.shape[0]
            inside = (c * self.unit >= base) & (c * self.unit < base + height)
            pl.when(inside)(functools.partial(act, ref, base))
            base += height

    def stage(self, slot, c):
        total = len(self.stages)
        if slot == 0:
            self.at_source(c, lambda ref, base: self.inward(0, c, ref, base).start())
        elif slot <= total:
            k = slot - 1
            size = self.unit >> slot
            got = self.inbox[k].at[self.rows(c * size, size)]
            self.inward_wait(k, c).wait_recv()
            last = slot == total
            kept = self.out if last else self.inbox[k]
            place = self.rows(self.start_row(c, slot), size)
            where = place if last else self.rows(c * size, size)
            if k == 0:

                def add(ref, base):
                    mine = ref[self.rows(self.start_row(c, 1) - base, size), :]
                    kept[where, :] = (mine.astype(F32) + got[...].astype(F32)).astype(BF16)

                self.at_source(c, add)
            else:
                before = c * (2 * size) + self.bits[k] * size
                mine = self.inbox[k - 1][self.rows(before, size), :]
                kept[where, :] = (mine.astype(F32) + got[...].astype(F32)).astype(BF16)
            if last:
                self.outward(total - 1, c).start()
            else:
                base = self.start_row(c, slot) - c * size
                self.inward(slot, c, kept, base).start()
        else:
            k = 2 * total - slot
            self.outward(k, c).wait_recv()
            if k > 0:
                self.outward(k - 1, c).start()

    def steps(self):
        return self.count + PLANE_SKEW * 2 * len(self.stages)

    def step(self, s):
        for slot in range(2 * len(self.stages) + 1):
            c = s - PLANE_SKEW * slot
            pl.when((c >= 0) & (c < self.count))(functools.partial(self.stage, slot, c))

    def drain(self):
        def one(c, carry):
            for k in range(len(self.stages)):
                self.inward_wait(k, c).wait_send()
                self.outward(k, c).wait_send()
            return carry

        lax.fori_loop(0, self.count, one, 0)


def line_kernel(
    size, chunk, returns, owners, pairs, stages, source_count, side_count, out_count, *refs
):
    streams = len(returns)
    returned = [k for k in range(streams) if returns[k]]
    parts, refs = refs[:streams], refs[streams:]
    sides, refs = refs[:side_count], refs[side_count:]
    shared, refs = dict(zip(returned, refs)), refs[len(returned) :]
    kept, refs = refs[:out_count], refs[out_count:]
    inbox, send_up, recv_up, send_back, recv_back = refs[:5]
    plane = None
    if source_count:
        plane_inbox, plane_send, plane_recv = refs[9 : 9 + len(stages)], *refs[9 + len(stages) :]
        plane = PlaneSum(
            stages, sides[:source_count], kept[1], plane_inbox, plane_send, plane_recv
        )
        sides = sides[source_count:]
    half = parts[0].shape[0] // 2
    count = half // chunk
    last = size - 1
    me = lax.axis_index("tensor")
    above, below = jnp.minimum(me + 1, last), jnp.maximum(me - 1, 0)
    flows = ((me, above, below), (last - me, below, above))

    barrier = pltpu.get_barrier_semaphore()

    def greet(axis, other):
        pl.semaphore_signal(
            barrier, inc=1, device_id={axis: other}, device_id_type=pl.DeviceIdType.MESH
        )

    if pairs:
        for axis, bit in pairs:
            greet(axis, partner(axis, bit))
        far_above = jnp.where(me % 2 == 0, 0, 1) * jnp.where(me < last, 1, 0)
        far_below = jnp.where(me % 2 == 0, 1, 0) * jnp.where(me > 0, 1, 0)
        pl.when(far_above == 1)(lambda: greet("tensor", above))
        pl.when(far_below == 1)(lambda: greet("tensor", below))
        pl.semaphore_wait(barrier, len(pairs) + far_above + far_below)
    else:
        pl.when(me < last)(lambda: greet("tensor", above))
        pl.when(me > 0)(lambda: greet("tensor", below))
        pl.semaphore_wait(barrier, jnp.where((me > 0) & (me < last), 2, 1))

    def place(f, i):
        return pl.ds(pl.multiple_of(f * half + i * chunk, chunk), chunk)

    def local(i):
        return pl.ds(pl.multiple_of(i * chunk, chunk), chunk)

    def onward(k, f, i, source):
        return pltpu.make_async_remote_copy(
            src_ref=source,
            dst_ref=inbox.at[k, f, local(i)],
            send_sem=send_up.at[k, f, i],
            recv_sem=recv_up.at[k, f, i],
            device_id={"tensor": flows[f][1]},
            device_id_type=pl.DeviceIdType.MESH,
        )

    def backward(k, f, i):
        block = shared[k].at[place(f, i)]
        return pltpu.make_async_remote_copy(
            src_ref=block,
            dst_ref=block,
            send_sem=send_back.at[k, f, i],
            recv_sem=recv_back.at[k, f, i],
            device_id={"tensor": flows[f][2]},
            device_id_type=pl.DeviceIdType.MESH,
        )

    def reduce_chunk(k, f, i):
        position = flows[f][0]
        mine = parts[k].at[place(f, i)]
        slot = inbox.at[k, f, local(i)]

        @pl.when(position == 0)
        def _():
            pl.when(i >= LINE_WINDOW)(lambda: onward(k, f, i - LINE_WINDOW, mine).wait_send())
            onward(k, f, i, mine).start()

        @pl.when(position > 0)
        def _():
            onward(k, f, i, slot).wait_recv()
            total = slot[...].astype(F32) + mine[...].astype(F32)

            @pl.when(position < last)
            def _():
                slot[...] = total.astype(BF16)
                onward(k, f, i, slot).start()

            @pl.when(position == last)
            def _():
                result = owners[k](total, place(f, i), local(i), sides, kept)
                if returns[k]:
                    shared[k][place(f, i), :] = result.astype(BF16)
                    backward(k, f, i).start()

    def pass_back(k, f, i):
        position = flows[f][0]

        @pl.when((position < last) & (i >= 0) & (i < count))
        def _():
            backward(k, f, i).wait_recv()
            pl.when(position > 0)(lambda: backward(k, f, i).start())

    def step(s, carry):
        for k in range(streams):
            for f in range(2):
                i = s - LINE_SKEW * flows[f][0]
                pl.when((i >= 0) & (i < count))(lambda: reduce_chunk(k, f, i))
        for k in returned:
            for f in range(2):
                pass_back(k, f, s - LINE_SKEW * (2 * last - flows[f][0]))
        if plane:
            plane.step(s)
        for n in range(len(pairs) + 1 if pairs else 0):
            pl.when(s == n * gap)(lambda: advance_gains(n))
        return carry

    steps = count + 2 * LINE_SKEW * last
    if plane:
        steps = max(steps, plane.steps())
    gap = steps // (len(pairs) + 1)
    if pairs:
        slots, sums, send_pair, recv_pair = refs[5:9]
        sums[0] = sides[-1][...]
    elif len(kept) > 1:
        kept[1][...] = jnp.zeros_like(kept[1])

    def swap_gains(n):
        return pltpu.make_async_remote_copy(
            src_ref=sums.at[n],
            dst_ref=slots.at[n],
            send_sem=send_pair.at[n],
            recv_sem=recv_pair.at[n],
            device_id={pairs[n][0]: partner(*pairs[n])},
            device_id_type=pl.DeviceIdType.MESH,
        )

    def advance_gains(n):
        if n > 0:
            swap_gains(n - 1).wait()
            sums[n] = sums[n - 1] + slots[n - 1]
        if n < len(pairs):
            swap_gains(n).start()
        else:
            kept[0][...] = sums[n]

    lax.fori_loop(0, steps, step, 0)

    def drain(i, carry):
        for k in range(streams):
            for f in range(2):
                position = flows[f][0]
                waited = (position == 0) & (i < count - LINE_WINDOW)
                pl.when((position < last) & ~waited)(
                    lambda: onward(k, f, i, inbox.at[k, f, local(i)]).wait_send()
                )
                if returns[k]:
                    pl.when(position > 0)(lambda: backward(k, f, i).wait_send())
        return carry

    lax.fori_loop(0, count, drain, 0)
    if plane:
        plane.drain()


def line_sum(
    parts, owners, sides, kept, collective_id, returns=(True,), pairs=(), stages=(), sources=()
):
    rows, width = parts[0].shape
    size = lax.axis_size("tensor")
    streams = len(parts)
    chunk = max(16, min(LINE_CHUNK, rows // 32))
    count = rows // 2 // chunk
    whole = pl.BlockSpec(memory_space=pltpu.VMEM)
    scalar = pl.BlockSpec(memory_space=pltpu.SMEM)
    sems = pltpu.SemaphoreType.DMA((streams, 2, count))
    outs = [jax.ShapeDtypeStruct((rows, width), BF16)] * sum(returns) + list(kept)
    extra = []
    if pairs:
        pair_sems = pltpu.SemaphoreType.DMA((len(pairs),))
        extra = [
            pltpu.VMEM((len(pairs), 8, width), F32),
            pltpu.VMEM((len(pairs) + 1, 8, width), F32),
            pair_sems,
            pair_sems,
        ]
    if sources:
        plane_rows = sum(source.shape[0] for source in sources)
        unit = 2 ** len(stages) * PLANE_ROWS
        kept = [*kept, jax.ShapeDtypeStruct((plane_rows, width), BF16)]
        outs.append(kept[-1])
        extra += [pltpu.VMEM((plane_rows >> (k + 1), width), BF16) for k in range(len(stages))]
        extra += [pltpu.SemaphoreType.DMA((2 * len(stages), plane_rows // unit))] * 2
        sides = [*sources, *sides]
    return pl.pallas_call(
        functools.partial(
            line_kernel,
            size,
            chunk,
            returns,
            owners,
            pairs,
            stages,
            len(sources),
            len(sides),
            len(kept),
        ),
        out_shape=outs,
        in_specs=[whole] * streams + [scalar if s.ndim == 1 else whole for s in sides],
        out_specs=[whole] * len(outs),
        scratch_shapes=[pltpu.VMEM((streams, 2, rows // 2, width), BF16)] + [sems] * 4 + extra,
        compiler_params=pltpu.CompilerParams(
            collective_id=collective_id, has_side_effects=True, vmem_limit_bytes=56 * 2**20
        ),
        cost_estimate=pl.CostEstimate(
            flops=streams * rows * width,
            bytes_accessed=streams * 300 * 2**20,
            transcendentals=0,
        ),
    )(*parts, *sides)


def unit_of(rows):
    inverse = lax.rsqrt(jnp.mean(rows * rows, axis=-1, keepdims=True) + EPSILON)
    return rows * inverse, inverse


def own_hidden(total, where, here, sides, kept):
    x_ref, gain_ref = sides
    hidden = x_ref[where, :].astype(F32) + total
    kept[0][here, :] = hidden
    return unit_of(hidden)[0] * gain_ref[...]


def own_dhidden(total, where, here, sides, kept):
    x_ref, hidden_ref, cot_ref, gain_ref, factor = sides
    unit, inverse = unit_of(hidden_ref[here, :])
    kept[1][...] += jnp.sum(total * unit, axis=0, keepdims=True)
    dhidden = norm_back(total, unit, inverse, gain_ref[...])
    kept[0][here, :] = dhidden
    return cot_ref[where, :].astype(F32) * factor[0] + dhidden


def own_output(total, where, here, sides, kept):
    x_ref, hidden_ref, cot_ref, gain_ref, factor = sides
    x = x_ref[where, :].astype(F32)
    result = x + factor[1] * ((hidden_ref[here, :] - x) + total)
    kept[2][here, :] = result.astype(BF16)


def own_dinput(total, where, here, sides, kept):
    x_ref, dhidden_ref, gain_ref, _ = sides
    unit, inverse = unit_of(x_ref[where, :].astype(F32))
    return dhidden_ref[here, :] + norm_back(total, unit, inverse, gain_ref[...])


def cut_half(own):
    step = own.shape[0] // SPREAD_PIECES
    return [[own[p * step : (p + 1) * step]] for p in range(SPREAD_PIECES)]


def send_wave(pieces, wave):
    size = lax.axis_size("tensor")
    for p, hops in enumerate(pieces):
        h = wave - p
        if 0 <= h < size - 1:
            perm = [(size - 1 - h, size - 2 - h), (h, h + 1)]
            hops.append(lax.ppermute(hops[-1], "tensor", perm))


def tie(pieces, others):
    heads, others = lax.optimization_barrier(([hops[-1] for hops in pieces], others))
    for hops, head in zip(pieces, heads):
        hops[-1] = head
    return others


def join_kernel(size, *refs):
    pieces, out = refs[:-1], refs[-1]
    me = lax.axis_index("tensor")
    step = pieces[0].shape[0]
    half = out.shape[0] // 2
    for p in range(SPREAD_PIECES):
        for h in range(size):
            for f, wanted in enumerate((size - 1 - me, me)):

                @pl.when(wanted == h)
                def _():
                    out[pl.ds(f * half + p * step, step), :] = pieces[p * size + h][...]


def join_halves(pieces):
    size = lax.axis_size("tensor")
    step, width = pieces[0].shape
    whole = pl.BlockSpec(memory_space=pltpu.VMEM)
    return pl.pallas_call(
        functools.partial(join_kernel, size),
        out_shape=jax.ShapeDtypeStruct((2 * SPREAD_PIECES * step, width), BF16),
        in_specs=[whole] * len(pieces),
        out_specs=whole,
        compiler_params=pltpu.CompilerParams(vmem_limit_bytes=40 * 2**20),
    )(*pieces)


def rotary_tables(positions):
    inverse = 1.0 / 10000.0 ** (jnp.arange(0, HEAD_DIM, 2, dtype=F32) / HEAD_DIM)
    angle = positions.astype(F32)[:, None] * inverse[None, :]
    return (jnp.cos(angle), jnp.sin(angle))


def contract_rows(left, right):
    return jnp.einsum("rd,rf->df", left, right, preferred_element_type=F32)


def contract_cols(left, right):
    return jnp.einsum("rc,dc->rd", left, right, preferred_element_type=F32)


def norm_back(dnormed, unit, inverse, gain):
    scaled = dnormed * gain
    return inverse * (scaled - unit * jnp.mean(scaled * unit, axis=-1, keepdims=True))


def flags_kernel(size, mine, everyone, send_sem, recv_sem):
    me = lax.axis_index("dp")
    barrier = pltpu.get_barrier_semaphore()
    others = [lax.rem(me + s, size) for s in range(1, size)]
    for other in others:
        pl.semaphore_signal(
            barrier, inc=1, device_id={"dp": other}, device_id_type=pl.DeviceIdType.MESH
        )
    pl.semaphore_wait(barrier, size - 1)

    def send(s, slot):
        return pltpu.make_async_remote_copy(
            src_ref=mine,
            dst_ref=everyone.at[slot],
            send_sem=send_sem.at[s],
            recv_sem=recv_sem.at[s],
            device_id={"dp": others[s]},
            device_id_type=pl.DeviceIdType.MESH,
        )

    for s in range(size - 1):
        send(s, me).start()
    everyone[me] = mine[...]
    for s in range(size - 1):
        send(s, me).wait_send()
        send(s, lax.rem(me + 2 * size - 1 - s, size)).wait_recv()


def share_flags(row):
    size = lax.axis_size("dp")
    tile = jnp.zeros((8, 128), jnp.int32).at[0, : row.shape[0]].set(row)
    sems = pltpu.SemaphoreType.DMA((size - 1,))
    whole = pl.BlockSpec(memory_space=pltpu.VMEM)
    shared = pl.pallas_call(
        functools.partial(flags_kernel, size),
        out_shape=jax.ShapeDtypeStruct((size, 8, 128), jnp.int32),
        in_specs=[whole],
        out_specs=whole,
        scratch_shapes=[sems, sems],
        compiler_params=pltpu.CompilerParams(collective_id=1, has_side_effects=True),
    )(tile)
    return shared[:, 0, : row.shape[0]]


def shift_ctx(part, s):
    size = lax.axis_size("ctx")
    return lax.ppermute(part, "ctx", [(i, (i + s) % size) for i in range(size)])


def swap_core(part):
    return lax.ppermute(part, "dp", [(i, i ^ 1) for i in range(lax.axis_size("dp"))])


def gather_parts(own, paired):
    parts = []
    for s in range(lax.axis_size("ctx")):
        here = own if s == 0 else shift_ctx(own, s)
        parts += [here, swap_core(here)] if paired else [here]
    return parts


def collect_parts(parts, paired):
    terms = [parts[0]]
    if paired:
        terms.append(swap_core(parts[1]))
    per = 2 if paired else 1
    for s in range(1, lax.axis_size("ctx")):
        near = parts[per * s]
        if paired:
            near = (near.astype(F32) + swap_core(parts[per * s + 1]).astype(F32)).astype(BF16)
        terms.append(shift_ctx(near, -s))
    return terms


def block_pass(
    paired,
    first_id,
    span,
    x_low,
    cot_low,
    keep,
    scale,
    order_row,
    attn_gain,
    ffn_gain,
    w_query,
    w_key,
    w_value,
    w_output,
    w_gate,
    w_up,
    w_down,
):
    rows, width = x_low.shape
    dp_size, ctx_size = lax.axis_size("dp"), lax.axis_size("ctx")
    spans = order_row.shape[0]
    ctx = lax.axis_index("ctx")
    core = lax.axis_index("dp") % 2
    per_part = rows // span
    order_parts = []
    for s in range(ctx_size):
        group = (ctx + ctx_size - s) % ctx_size
        places = [group * 2 + core, group * 2 + 1 - core] if paired else [group]
        order_parts += [
            lax.dynamic_slice_in_dim(order_row, place * per_part, per_part) for place in places
        ]
    query_order, key_order = order_parts[0], jnp.concatenate(order_parts)
    row_index = jnp.arange(rows, dtype=jnp.int32)
    starts = jnp.sum(
        jnp.where(
            (row_index // span)[:, None] == jnp.arange(per_part, dtype=jnp.int32)[None, :],
            query_order[None, :],
            0,
        ),
        axis=1,
    )
    cosine, sine = rotary_tables(starts * span + row_index % span)

    wide_cosine = jnp.concatenate([cosine, cosine], axis=1)
    wide_sine = jnp.concatenate([-sine, sine], axis=1)
    attn_row, ffn_row = attn_gain[None, :], ffn_gain[None, :]
    normed_one, queries, kv_own = project(
        x_low, attn_row, wide_cosine, wide_sine, w_query, w_key, w_value
    )
    kv_parts = gather_parts(kv_own, paired)
    mixed, logs = attend(queries, kv_parts, query_order, key_order, span)

    half_rows = jax.ShapeDtypeStruct((rows // 2, width), F32)
    gain_row = jax.ShapeDtypeStruct((1, width), F32)
    attn_part = nn_dot(mixed, w_output).astype(BF16)
    normed_two, hidden = line_sum(
        [attn_part], [own_hidden], [x_low, ffn_row], [half_rows], first_id
    )

    factors = jnp.stack([keep * scale, keep])
    dffn, acted, dgate, dupward = hidden_units(
        normed_two, cot_low, factors, w_gate, w_up, w_down
    )
    early_grads = (
        contract_rows(acted, dffn).astype(BF16),
        contract_rows(normed_two, dgate).astype(BF16),
    )
    late_grads = contract_rows(normed_two, dupward).astype(BF16)
    acted, dgate, dupward, early_grads, late_grads = lax.optimization_barrier(
        (acted, dgate, dupward, early_grads, late_grads)
    )
    early_grads = lax.psum(early_grads, ("dp", "ctx"))
    dnormed_part, ffn_part = width_parts(acted, dgate, dupward, w_gate, w_up, w_down)
    dattn, dhidden, ffn_gain_part, output_half = line_sum(
        [dnormed_part, ffn_part],
        [own_dhidden, own_output],
        [x_low, hidden, cot_low, ffn_row, factors],
        [half_rows, gain_row, jax.ShapeDtypeStruct((rows // 2, width), BF16)],
        first_id + 1,
        (True, False),
    )
    pieces = cut_half(output_half)
    send_wave(pieces, 0)
    grad_output = contract_rows(mixed, dattn)
    dmixed = contract_cols(dattn, w_output).astype(BF16)
    dq_proj, *dkv_parts = attend_back(
        queries, dmixed, mixed, logs, cosine, sine, kv_parts, query_order, key_order, span
    )
    dq_proj, dkv_parts = tie(pieces, (dq_proj, dkv_parts))
    send_wave(pieces, 1)
    terms = tie(pieces, collect_parts(dkv_parts, paired))
    send_wave(pieces, 2)
    dqkv_proj, dnormed_one, attn_gain_part = project_back(
        x_low, dq_proj, terms, wide_cosine, wide_sine, w_query, w_key, w_value
    )
    gain_parts = jnp.concatenate(
        [attn_gain_part, ffn_gain_part, jnp.zeros((6, width), F32)], axis=0
    )
    grad_qkv = contract_rows(dqkv_proj, normed_one).astype(BF16)
    dnormed_one, early_grads, late_grads = tie(pieces, (dnormed_one, early_grads, late_grads))
    late_grads = lax.psum(late_grads, ("ctx", "dp"))
    for wave in range(3, lax.axis_size("tensor") + SPREAD_PIECES):
        send_wave(pieces, wave)
    through, gains, attn_grads = line_sum(
        [dnormed_one],
        [own_dinput],
        [x_low, dhidden, attn_row, gain_parts],
        [jax.ShapeDtypeStruct((8, width), F32)],
        first_id + 2,
        (True,),
        tuple(pair_steps((dp_size, ctx_size, lax.axis_size("tensor")))),
        plane_steps(dp_size, ctx_size),
        [grad_qkv, grad_output.astype(BF16)],
    )
    through, gains, attn_grads, early_grads, late_grads, pieces = lax.optimization_barrier(
        (through, gains, attn_grads, early_grads, late_grads, pieces)
    )
    output = join_halves([hop for hops in pieces for hop in hops])
    cuts = (w_query.shape[1], w_query.shape[1] + w_key.shape[1], dqkv_proj.shape[1])
    grad_query, grad_key, grad_value, grad_output = jnp.split(attn_grads, cuts, axis=0)
    grads = (grad_query.T, grad_key.T, grad_value.T, grad_output, *early_grads, late_grads)
    return output, through, gains, grads


def per_device(
    inputs,
    cotangent,
    skip_mask,
    group_ids,
    span_order,
    exit_scale,
    attn_gain,
    ffn_gain,
    *weights,
):
    _, rows, width = inputs.shape
    spans = span_order.shape[1]
    own_spans = spans // lax.axis_size("ctx")
    span = rows // own_spans
    me = lax.axis_index("dp")
    core = me % 2
    x_low, cot_low = inputs[0], cotangent[0]
    flags = share_flags(jnp.concatenate([skip_mask, group_ids, span_order[0]]))
    runs, groups = flags[:, 0], flags[:, 1]
    scale_of = lambda group: jnp.where(group == 1, exit_scale[1], exit_scale[0])
    own_run, own_scale = skip_mask[0], scale_of(group_ids[0])
    gains = (attn_gain, ffn_gain)

    def alone():
        return block_pass(
            False,
            2,
            span,
            x_low,
            cot_low,
            own_run.astype(F32),
            own_scale,
            span_order[0],
            *gains,
            *weights,
        )

    def shared():
        half = rows // 2
        other = me + 1 - 2 * core
        take = lambda a, i: lax.dynamic_slice_in_dim(a, i * half, half, 0)
        pick = lambda a: lax.dynamic_index_in_dim(a, other, 0, keepdims=False)
        other_run = pick(runs)
        use_own = (own_run == 1) | ((other_run == 0) & (core == 0))
        choose = lambda mine, theirs: jnp.where(use_own, mine, theirs)
        work = lambda a: choose(take(a, core), swap_core(take(a, 1 - core)))
        output, through, *rest = block_pass(
            True,
            5,
            span,
            work(x_low),
            work(cot_low),
            choose(own_run, other_run).astype(F32),
            choose(own_scale, scale_of(pick(groups))),
            choose(span_order[0], pick(flags[:, 2:])),
            *gains,
            *weights,
        )

        def whole(part):
            theirs = swap_core(part)
            first, second = jnp.where(core == 0, part, theirs), jnp.where(core == 0, theirs, part)
            return jnp.concatenate([first, second], 0)

        through = jnp.where(own_run == 1, whole(through), 0)
        return whole(output), through, *rest

    def finish(output, through, sums, grads):
        output = jnp.where(own_run == 1, output, x_low)
        input_grad = cot_low.astype(F32) * own_scale + through.astype(F32)
        grads = [g.astype(F32) for g in grads]
        return lax.optimization_barrier((output, input_grad, sums[0], sums[1], *grads))

    if own_spans % 2 == 0 and lax.axis_size("dp") % 2 == 0:
        pairs = runs.reshape(-1, 2)
        results = lax.cond(
            jnp.all(pairs[:, 0] * pairs[:, 1] == 0),
            lambda: finish(*shared()),
            lambda: finish(*alone()),
        )
    else:
        results = finish(*alone())
    output, input_grad, grad_attn_gain, grad_ffn_gain = results[:4]
    grad_query, grad_key, grad_value, grad_output, grad_down, grad_gate, grad_up = results[4:]
    return (
        output.reshape(inputs.shape),
        input_grad.reshape(inputs.shape),
        grad_attn_gain,
        grad_ffn_gain,
        grad_query,
        grad_key,
        grad_value,
        grad_output,
        grad_gate,
        grad_up,
        grad_down,
    )


def solution(mesh):
    rows = P("dp", "ctx", None)
    by_column, by_row = P(None, "tensor"), P("tensor", None)
    in_specs = (rows, rows, P("dp"), P("dp"), P("dp", None), P(), P(), P())
    in_specs += (by_column,) * 3 + (by_row,) + (by_column,) * 2 + (by_row,)
    out_specs = (rows, rows, P(), P()) + (by_column,) * 3 + (by_row,) + (by_column,) * 2 + (by_row,)
    return jax.shard_map(
        per_device, mesh=mesh, in_specs=in_specs, out_specs=out_specs, check_vma=False
    )
```

```python
import functools

import jax
import jax.numpy as jnp
from jax import lax
from jax.experimental import pallas as pl
from jax.experimental.pallas import tpu as pltpu
from jax.sharding import PartitionSpec as P

HEAD_DIM = 128
EPSILON = 1e-05
NEG_BIG = -1e30
FACTOR = HEAD_DIM ** (-0.5)
LOG2E = 1.4426950408889634
QUERY_BLOCK = 256
BF16 = jnp.bfloat16
F32 = jnp.float32

NT = (((1,), (1,)), ((), ()))


def nt_dot(left, right):
    return lax.dot_general(left, right, NT, preferred_element_type=F32)


def nn_dot(left, right):
    return jnp.dot(left, right, preferred_element_type=F32)


def stack_heads(block, group):
    return jnp.concatenate(
        [block[:, h * HEAD_DIM : (h + 1) * HEAD_DIM] for h in range(group)], axis=0
    )


def hide_later(scores, first_row, rows, fill):
    key_row = lax.broadcasted_iota(jnp.int32, scores.shape, 0)
    query_row = lax.broadcasted_iota(jnp.int32, scores.shape, 1) % rows + first_row
    return jnp.where(key_row <= query_row, scores, fill)


def over_spans(kv_refs, span, visit, query_order, key_order, first):
    order = query_order[first // span]
    seen = 0
    for part, kv_ref in enumerate(kv_refs):
        count = kv_ref.shape[1] // span

        def one_span(j, carry, part=part, seen=seen):
            place = pl.multiple_of(j * span, span)
            column = pl.multiple_of((seen + j) * span, span)
            pl.when(key_order[seen + j] < order)(lambda: visit(part, place, column, False))
            pl.when(key_order[seen + j] == order)(lambda: visit(part, place, column, True))
            return carry

        lax.fori_loop(0, count, one_span, 0)
        seen += count


def attend_kernel(group, span, parts, query_order, key_order, q_ref, *refs):
    kv_refs, (o_ref, lse_ref, vt_ref, top, total, acc) = refs[:parts], refs[parts:]
    rows = q_ref.shape[0]
    step = pl.program_id(1)
    first = step * rows

    @pl.when(step == 0)
    def _():
        for part, kv_ref in enumerate(kv_refs):
            size = kv_ref.shape[1]
            vt_ref[:, part * size : (part + 1) * size] = kv_ref[1].T

    queries = stack_heads(q_ref[...], group)
    top[...] = jnp.full_like(top, NEG_BIG)
    total[...] = jnp.zeros_like(total)
    acc[...] = jnp.zeros_like(acc)

    def visit(part, place, column, diagonal):
        keys = kv_refs[part][0, pl.ds(place, span), :]
        scores = nt_dot(keys, queries) * (FACTOR * LOG2E)
        if diagonal:
            scores = hide_later(scores, first % span, rows, NEG_BIG)
        before = top[...]
        now = jnp.maximum(before, jnp.max(scores, axis=0, keepdims=True))
        weights = jnp.exp2(scores - now)
        shrink = jnp.exp2(before - now)
        top[...] = now
        total[...] = total[...] * shrink + jnp.sum(weights, axis=0, keepdims=True)
        acc[...] = acc[...] * shrink + nn_dot(
            vt_ref[:, pl.ds(column, span)], weights.astype(BF16)
        )

    over_spans(kv_refs, span, visit, query_order, key_order, first)
    mixed = acc[...] / total[...]
    logs = top[...] + jnp.log2(total[...])
    for h in range(group):
        part = slice(h * rows, (h + 1) * rows)
        o_ref[:, h * HEAD_DIM : (h + 1) * HEAD_DIM] = mixed[:, part].T.astype(BF16)
        lse_ref[0, h : h + 1, :] = logs[:, part]


def attend(queries, kv_parts, query_order, key_order, span):
    rows, width = queries.shape
    part_rows, kv_width = kv_parts[0].shape[1:]
    full = part_rows * len(kv_parts)
    kv_heads = kv_width // HEAD_DIM
    group = width // kv_width
    block = min(QUERY_BLOCK, span)
    query_spec = pl.BlockSpec((block, group * HEAD_DIM), lambda g, i, *_: (i, g))
    kv_spec = pl.BlockSpec((2, part_rows, HEAD_DIM), lambda g, i, *_: (0, 0, g))
    return pl.pallas_call(
        functools.partial(attend_kernel, group, span, len(kv_parts)),
        grid_spec=pltpu.PrefetchScalarGridSpec(
            num_scalar_prefetch=2,
            grid=(kv_heads, rows // block),
            in_specs=[query_spec] + [kv_spec] * len(kv_parts),
            out_specs=[
                query_spec,
                pl.BlockSpec((1, group, block), lambda g, i, *_: (g, 0, i)),
            ],
            scratch_shapes=[
                pltpu.VMEM((HEAD_DIM, full), BF16),
                pltpu.VMEM((1, group * block), F32),
                pltpu.VMEM((1, group * block), F32),
                pltpu.VMEM((HEAD_DIM, group * block), F32),
            ],
        ),
        out_shape=[
            jax.ShapeDtypeStruct((rows, width), BF16),
            jax.ShapeDtypeStruct((kv_heads, group, rows), F32),
        ],
        compiler_params=pltpu.CompilerParams(vmem_limit_bytes=32 * 2**20),
        cost_estimate=pl.CostEstimate(
            flops=4 * rows * full * width,
            bytes_accessed=4 * rows * width + 4 * full * kv_width,
            transcendentals=rows * full * width // HEAD_DIM,
        ),
    )(query_order, key_order, queries, *kv_parts)


def attend_back_kernel(
    group,
    span,
    parts,
    query_order,
    key_order,
    q_ref,
    do_ref,
    o_ref,
    lse_ref,
    cos_ref,
    sin_ref,
    *refs,
):
    kv_refs, dq_ref, dkv_refs = refs[:parts], refs[parts], refs[parts + 1 : 2 * parts + 1]
    kt_ref, acc, sums = refs[2 * parts + 1 :]
    rows = q_ref.shape[0]
    step = pl.program_id(1)
    first = step * rows
    queries = stack_heads(q_ref[...], group)
    dmixed = stack_heads(do_ref[...], group)
    mixed = stack_heads(o_ref[...], group)
    product = dmixed.astype(F32) * mixed.astype(F32)
    delta = jnp.sum(product.T, axis=0, keepdims=True)
    logs = jnp.concatenate([lse_ref[0, h : h + 1, :] for h in range(group)], axis=1)
    acc[...] = jnp.zeros_like(acc)

    @pl.when(step == 0)
    def _():
        sums[...] = jnp.zeros_like(sums)
        for part, kv_ref in enumerate(kv_refs):
            size = kv_ref.shape[1]
            kt_ref[:, part * size : (part + 1) * size] = kv_ref[0].T

    def visit(part, place, column, diagonal):
        here = pl.ds(place, span)
        scores = nt_dot(kv_refs[part][0, here, :], queries) * (FACTOR * LOG2E)
        probs = jnp.exp2(scores - logs)
        if diagonal:
            probs = hide_later(probs, first % span, rows, 0.0)
        dprobs = nt_dot(kv_refs[part][1, here, :], dmixed)
        dscore = (probs * (dprobs - delta)).astype(BF16)
        sums[part, 1, here, :] += nn_dot(probs.astype(BF16), dmixed)
        sums[part, 0, here, :] += nn_dot(dscore, queries)
        acc[...] += nn_dot(kt_ref[:, pl.ds(column, span)], dscore)

    over_spans(kv_refs, span, visit, query_order, key_order, first)
    for h in range(group):
        grad = acc[:, h * rows : (h + 1) * rows] * FACTOR
        half = HEAD_DIM // 2
        leading, trailing = grad[:half], grad[half:]
        cosine, sine = cos_ref[...], sin_ref[...]
        turned = jnp.concatenate(
            [leading * cosine + trailing * sine, trailing * cosine - leading * sine], axis=0
        )
        dq_ref[:, h * HEAD_DIM : (h + 1) * HEAD_DIM] = turned.T.astype(BF16)

    @pl.when(step == pl.num_programs(1) - 1)
    def _():
        for part, dkv_ref in enumerate(dkv_refs):
            dkv_ref[0] = (sums[part, 0] * FACTOR).astype(dkv_ref.dtype)
            dkv_ref[1] = sums[part, 1].astype(dkv_ref.dtype)


def attend_back(
    queries, dmixed, mixed, logs, cosine, sine, kv_parts, query_order, key_order, span
):
    rows, width = queries.shape
    part_rows, kv_width = kv_parts[0].shape[1:]
    parts = len(kv_parts)
    full = part_rows * parts
    kv_heads = kv_width // HEAD_DIM
    group = width // kv_width
    block = min(QUERY_BLOCK, span)
    half = HEAD_DIM // 2
    query_spec = pl.BlockSpec((block, group * HEAD_DIM), lambda g, i, *_: (i, g))
    kv_spec = pl.BlockSpec((2, part_rows, HEAD_DIM), lambda g, i, *_: (0, 0, g))
    table_spec = pl.BlockSpec((half, block), lambda g, i, *_: (0, i))
    kinds = [F32] + [BF16] * (parts - 1)
    return pl.pallas_call(
        functools.partial(attend_back_kernel, group, span, parts),
        grid_spec=pltpu.PrefetchScalarGridSpec(
            num_scalar_prefetch=2,
            grid=(kv_heads, rows // block),
            in_specs=[
                query_spec,
                query_spec,
                query_spec,
                pl.BlockSpec((1, group, block), lambda g, i, *_: (g, 0, i)),
                table_spec,
                table_spec,
            ]
            + [kv_spec] * parts,
            out_specs=[query_spec] + [kv_spec] * parts,
            scratch_shapes=[
                pltpu.VMEM((HEAD_DIM, full), BF16),
                pltpu.VMEM((HEAD_DIM, group * block), F32),
                pltpu.VMEM((parts, 2, part_rows, HEAD_DIM), F32),
            ],
        ),
        out_shape=[jax.ShapeDtypeStruct((rows, width), BF16)]
        + [jax.ShapeDtypeStruct((2, part_rows, kv_width), kind) for kind in kinds],
        compiler_params=pltpu.CompilerParams(vmem_limit_bytes=40 * 2**20),
        cost_estimate=pl.CostEstimate(
            flops=10 * rows * full * width,
            bytes_accessed=8 * rows * width + 14 * full * kv_width,
            transcendentals=rows * full * width // HEAD_DIM,
        ),
    )(
        query_order,
        key_order,
        queries,
        dmixed,
        mixed,
        logs,
        cosine.T,
        sine.T,
        *kv_parts,
    )


ROW_BLOCK = 256


def by_rows(block, width):
    return pl.BlockSpec((block, width), lambda i: (i, 0))


def held(array):
    return pl.BlockSpec(
        array.shape, lambda i: (0,) * array.ndim, pipeline_mode=pl.Buffered(1)
    )


def column_cuts(width, size=512):
    return [slice(c, min(c + size, width)) for c in range(0, width, size)]


def turn(field, cosine, sine):
    return field * cosine + pltpu.roll(field, HEAD_DIM // 2, 1) * sine


def project_kernel(x_ref, gain_ref, cos_ref, sin_ref, wq, wk, wv, n_ref, q_ref, kv_ref):
    unit, _ = unit_of(x_ref[...].astype(F32))
    normed = (unit * gain_ref[...]).astype(BF16)
    n_ref[...] = normed
    cosine, sine = cos_ref[...], sin_ref[...]
    queries, keys = nn_dot(normed, wq[...]), nn_dot(normed, wk[...])
    for h in range(q_ref.shape[1] // HEAD_DIM):
        head = slice(h * HEAD_DIM, (h + 1) * HEAD_DIM)
        q_ref[:, head] = turn(queries[:, head], cosine, sine).astype(BF16)
    for h in range(kv_ref.shape[2] // HEAD_DIM):
        head = slice(h * HEAD_DIM, (h + 1) * HEAD_DIM)
        kv_ref[0, :, head] = turn(keys[:, head], cosine, sine).astype(BF16)
    kv_ref[1] = nn_dot(normed, wv[...]).astype(BF16)


def project(x_low, gain_row, cosine, sine, w_query, w_key, w_value):
    rows, width = x_low.shape
    block = min(ROW_BLOCK, rows)
    heads_width, kv_width = w_query.shape[1], w_key.shape[1]
    return pl.pallas_call(
        project_kernel,
        grid=(rows // block,),
        in_specs=[
            by_rows(block, width),
            held(gain_row),
            by_rows(block, HEAD_DIM),
            by_rows(block, HEAD_DIM),
            held(w_query),
            held(w_key),
            held(w_value),
        ],
        out_specs=[
            by_rows(block, width),
            by_rows(block, heads_width),
            pl.BlockSpec((2, block, kv_width), lambda i: (0, i, 0)),
        ],
        out_shape=[
            jax.ShapeDtypeStruct((rows, width), BF16),
            jax.ShapeDtypeStruct((rows, heads_width), BF16),
            jax.ShapeDtypeStruct((2, rows, kv_width), BF16),
        ],
        compiler_params=pltpu.CompilerParams(vmem_limit_bytes=40 * 2**20),
        cost_estimate=pl.CostEstimate(
            flops=2 * rows * width * (heads_width + 2 * kv_width),
            bytes_accessed=6 * rows * width + 2 * width * (heads_width + 2 * kv_width),
            transcendentals=rows,
        ),
    )(x_low, gain_row, cosine, sine, w_query, w_key, w_value)


def stream_cuts(sources, targets, sems, cuts):
    first = pl.program_id(0) == 0

    def copies(n):
        out = []
        for w, (source, target, by_column) in enumerate(zip(sources, targets, cuts[1])):
            start, size = cuts[0][n].start, cuts[0][n].stop - cuts[0][n].start
            place = (slice(None), pl.ds(start, size)) if by_column else (pl.ds(start, size),)
            out.append(
                pltpu.make_async_copy(source.at[place], target.at[place], sems.at[w, n])
            )
        return out

    @pl.when(first)
    def _():
        for n in range(len(cuts[0])):
            for copy in copies(n):
                copy.start()

    def ready(n):
        @pl.when(first)
        def _():
            for copy in copies(n):
                copy.wait()

    return ready


def hidden_kernel(n_ref, da_ref, wg_ref, wu_ref, a_ref, dg_ref, du_ref, wg, wu, sems):
    cuts = column_cuts(a_ref.shape[1])
    ready = stream_cuts((wg_ref, wu_ref), (wg, wu), sems, (cuts, (True, True)))
    normed = n_ref[...]
    for n, cut in enumerate(cuts):
        ready(n)
        gate, upward = nn_dot(normed, wg[:, cut]), nn_dot(normed, wu[:, cut])
        dacted = da_ref[:, cut]
        sigmoid = jax.nn.sigmoid(gate)
        silu = gate * sigmoid
        a_ref[:, cut] = (silu * upward).astype(BF16)
        slope = sigmoid * (1.0 + gate * (1.0 - sigmoid))
        dg_ref[:, cut] = (dacted * upward * slope).astype(BF16)
        du_ref[:, cut] = (dacted * silu).astype(BF16)


def hidden_units(normed, dacted, w_gate, w_up):
    rows, width = normed.shape
    units = w_gate.shape[1]
    block = min(ROW_BLOCK, rows)
    anywhere = pl.BlockSpec(memory_space=pl.ANY)
    return pl.pallas_call(
        hidden_kernel,
        grid=(rows // block,),
        in_specs=[by_rows(block, width), by_rows(block, units), anywhere, anywhere],
        out_specs=[by_rows(block, units)] * 3,
        out_shape=[jax.ShapeDtypeStruct((rows, units), BF16)] * 3,
        scratch_shapes=[pltpu.VMEM(w.shape, BF16) for w in (w_gate, w_up)]
        + [pltpu.SemaphoreType.DMA((2, len(column_cuts(units))))],
        compiler_params=pltpu.CompilerParams(vmem_limit_bytes=44 * 2**20),
        cost_estimate=pl.CostEstimate(
            flops=4 * rows * width * units,
            bytes_accessed=2 * rows * width + 4 * width * units + 10 * rows * units,
            transcendentals=rows * units,
        ),
    )(normed, dacted, w_gate, w_up)


def parts_kernel(
    a_ref, dg_ref, du_ref, wg_ref, wu_ref, wd_ref, dn_ref, f_ref, wg, wu, wd, sems
):
    cuts = column_cuts(dn_ref.shape[1])
    weights = (wg_ref, wu_ref, wd_ref), (wg, wu, wd)
    ready = stream_cuts(*weights, sems, (cuts, (False, False, True)))
    for n, cut in enumerate(cuts):
        ready(n)
        dnormed = nt_dot(dg_ref[...], wg[cut, :]) + nt_dot(du_ref[...], wu[cut, :])
        dn_ref[:, cut] = dnormed.astype(BF16)
        f_ref[:, cut] = nn_dot(a_ref[...], wd[:, cut]).astype(BF16)


def width_parts(acted, dgate, dupward, w_gate, w_up, w_down):
    rows, units = acted.shape
    width = w_gate.shape[0]
    block = min(ROW_BLOCK, rows)
    weights = (w_gate, w_up, w_down)
    return pl.pallas_call(
        parts_kernel,
        grid=(rows // block,),
        in_specs=[by_rows(block, units)] * 3 + [pl.BlockSpec(memory_space=pl.ANY)] * 3,
        out_specs=[by_rows(block, width)] * 2,
        out_shape=[jax.ShapeDtypeStruct((rows, width), BF16)] * 2,
        scratch_shapes=[pltpu.VMEM(w.shape, BF16) for w in weights]
        + [pltpu.SemaphoreType.DMA((3, len(column_cuts(width))))],
        compiler_params=pltpu.CompilerParams(vmem_limit_bytes=44 * 2**20),
        cost_estimate=pl.CostEstimate(
            flops=6 * rows * width * units,
            bytes_accessed=4 * rows * width + 6 * width * units + 6 * rows * units,
            transcendentals=0,
        ),
    )(acted, dgate, dupward, *weights)


def project_back_kernel(
    addends, x_ref, dq_ref, cos_ref, sin_ref, wq, wk, wv, *refs
):
    terms, (dkv_ref, dn_ref, gain_ref) = refs[:addends], refs[addends:]
    kv_width = terms[0].shape[2]
    cosine, sine = cos_ref[...], -sin_ref[...]
    dkeys, dvalues = terms[0][0], terms[0][1]
    for term in terms[1:]:
        dkeys, dvalues = dkeys + term[0].astype(F32), dvalues + term[1].astype(F32)
    for h in range(kv_width // HEAD_DIM):
        head = slice(h * HEAD_DIM, (h + 1) * HEAD_DIM)
        dkv_ref[:, head] = turn(dkeys[:, head], cosine, sine).astype(BF16)
    dkv_ref[:, kv_width:] = dvalues.astype(BF16)
    unit, _ = unit_of(x_ref[...].astype(F32))

    @pl.when(pl.program_id(0) == 0)
    def _():
        gain_ref[...] = jnp.zeros_like(gain_ref)

    for cut in column_cuts(dn_ref.shape[1]):
        dnormed = nt_dot(dq_ref[...], wq[cut, :])
        dnormed = dnormed + nt_dot(dkv_ref[:, :kv_width], wk[cut, :])
        dnormed = dnormed + nt_dot(dkv_ref[:, kv_width:], wv[cut, :])
        dn_ref[:, cut] = dnormed.astype(BF16)
        gain_ref[:, cut] += jnp.sum(dnormed * unit[:, cut], axis=0, keepdims=True)


def project_back(x_low, dq, terms, cosine, sine, w_query, w_key, w_value):
    rows, width = x_low.shape
    block = min(ROW_BLOCK, rows)
    heads_width, kv_width = w_query.shape[1], w_key.shape[1]
    kv_spec = pl.BlockSpec((2, block, kv_width), lambda i: (0, i, 0))
    return pl.pallas_call(
        functools.partial(project_back_kernel, len(terms)),
        grid=(rows // block,),
        in_specs=[
            by_rows(block, width),
            by_rows(block, heads_width),
            by_rows(block, HEAD_DIM),
            by_rows(block, HEAD_DIM),
            held(w_query),
            held(w_key),
            held(w_value),
        ]
        + [kv_spec] * len(terms),
        out_specs=[
            by_rows(block, 2 * kv_width),
            by_rows(block, width),
            pl.BlockSpec((1, width), lambda i: (0, 0)),
        ],
        out_shape=[
            jax.ShapeDtypeStruct((rows, 2 * kv_width), BF16),
            jax.ShapeDtypeStruct((rows, width), BF16),
            jax.ShapeDtypeStruct((1, width), F32),
        ],
        compiler_params=pltpu.CompilerParams(vmem_limit_bytes=40 * 2**20),
        cost_estimate=pl.CostEstimate(
            flops=2 * rows * width * (heads_width + 2 * kv_width),
            bytes_accessed=6 * rows * width + 2 * width * (heads_width + 2 * kv_width),
            transcendentals=rows,
        ),
    )(x_low, dq, cosine, sine, w_query, w_key, w_value, *terms)


def unpack_kernel(packed, *outs):
    row = 0
    for out in outs[:-1]:
        height = out.shape[1]
        out[...] = packed[row : row + height, :].astype(F32).T
        row += height
    outs[-1][...] = packed[row:, :].astype(F32)


def unpack(packed, *widths):
    total, width = packed.shape
    last = total - sum(widths)
    block = min(ROW_BLOCK, width)
    return pl.pallas_call(
        unpack_kernel,
        grid=(width // block,),
        in_specs=[pl.BlockSpec((total, block), lambda i: (0, i))],
        out_specs=[by_rows(block, w) for w in widths]
        + [pl.BlockSpec((last, block), lambda i: (0, i))],
        out_shape=[jax.ShapeDtypeStruct((width, w), F32) for w in widths]
        + [jax.ShapeDtypeStruct((last, width), F32)],
        compiler_params=pltpu.CompilerParams(vmem_limit_bytes=32 * 2**20),
    )(packed)


LINE_CHUNK = 32
LINE_WINDOW = 2
LINE_SKEW = 2
MESH_AXES = ("dp", "ctx", "tensor")
SPREAD_PIECES = 2
PLANE_ROWS = 16
PLANE_SKEW = 2


def pair_steps(sizes):
    steps = []
    for axis, size in zip(MESH_AXES, sizes):
        bit = 1
        while bit < size:
            steps.append((axis, bit))
            bit *= 2
    return steps


def partner(axis, bit):
    index = lax.axis_index(axis)
    return jnp.where((index // bit) % 2 == 0, index + bit, index - bit)


def plane_steps(dp_size, ctx_size):
    across, along, bit = [], [], 1
    while bit < ctx_size:
        across.append(("ctx", bit))
        bit *= 2
    bit = 2
    while bit < dp_size:
        along.append(("dp", bit))
        bit *= 2
    first = [(("dp", 1), ("dp", 1))] if dp_size > 1 else []
    return tuple(first + list(zip(across + along, along + across)))


class PlaneSum:
    def __init__(self, stages, sources, out, inbox, send_sem, recv_sem):
        self.stages, self.sources, self.out, self.inbox = stages, sources, out, inbox
        self.send_sem, self.recv_sem = send_sem, recv_sem
        self.unit = 2 ** len(stages) * PLANE_ROWS
        self.count = out.shape[0] // self.unit
        odd = lax.axis_index("dp") % 2
        self.bits, self.peers = [], []
        for even_step, odd_step in stages:
            ids = {}
            for axis, bit, here in ((*even_step, odd == 0), (*odd_step, odd == 1)):
                index = ids.get(axis, lax.axis_index(axis))
                ids[axis] = jnp.where(here, partner(axis, bit), index)
            pick = lambda step: (lax.axis_index(step[0]) // step[1]) % 2
            self.bits.append(jnp.where(odd == 0, pick(even_step), pick(odd_step)))
            self.peers.append(ids)

    def start_row(self, c, k):
        row = c * self.unit
        for n in range(k):
            row = row + self.bits[n] * (self.unit >> (n + 1))
        return row

    def rows(self, start, size):
        return pl.ds(pl.multiple_of(start, PLANE_ROWS), size)

    def copy(self, slot, c, peer, source, target):
        return pltpu.make_async_remote_copy(
            src_ref=source,
            dst_ref=target,
            send_sem=self.send_sem.at[slot, c],
            recv_sem=self.recv_sem.at[slot, c],
            device_id=peer,
            device_id_type=pl.DeviceIdType.MESH,
        )

    def inward(self, k, c, source_ref, base):
        size = self.unit >> (k + 1)
        start = self.start_row(c, k) + (1 - self.bits[k]) * size - base
        target = self.inbox[k].at[self.rows(c * size, size)]
        return self.copy(k, c, self.peers[k], source_ref.at[self.rows(start, size)], target)

    def inward_wait(self, k, c):
        size = self.unit >> (k + 1)
        target = self.inbox[k].at[self.rows(c * size, size)]
        return self.copy(k, c, self.peers[k], target, target)

    def outward(self, k, c):
        size = self.unit >> (k + 1)
        block = self.out.at[self.rows(self.start_row(c, k + 1), size)]
        return self.copy(2 * len(self.stages) - 1 - k, c, self.peers[k], block, block)

    def at_source(self, c, act):
        base = 0
        for ref in self.sources:
            height = ref.shape[0]
            inside = (c * self.unit >= base) & (c * self.unit < base + height)
            pl.when(inside)(functools.partial(act, ref, base))
            base += height

    def stage(self, slot, c):
        total = len(self.stages)
        if slot == 0:
            self.at_source(c, lambda ref, base: self.inward(0, c, ref, base).start())
        elif slot <= total:
            k = slot - 1
            size = self.unit >> slot
            got = self.inbox[k].at[self.rows(c * size, size)]
            self.inward_wait(k, c).wait_recv()
            last = slot == total
            kept = self.out if last else self.inbox[k]
            place = self.rows(self.start_row(c, slot), size)
            where = place if last else self.rows(c * size, size)
            if k == 0:

                def add(ref, base):
                    mine = ref[self.rows(self.start_row(c, 1) - base, size), :]
                    kept[where, :] = (mine.astype(F32) + got[...].astype(F32)).astype(BF16)

                self.at_source(c, add)
            else:
                before = c * (2 * size) + self.bits[k] * size
                mine = self.inbox[k - 1][self.rows(before, size), :]
                kept[where, :] = (mine.astype(F32) + got[...].astype(F32)).astype(BF16)
            if last:
                self.outward(total - 1, c).start()
            else:
                base = self.start_row(c, slot) - c * size
                self.inward(slot, c, kept, base).start()
        else:
            k = 2 * total - slot
            self.outward(k, c).wait_recv()
            if k > 0:
                self.outward(k - 1, c).start()

    def steps(self):
        return self.count + PLANE_SKEW * 2 * len(self.stages)

    def step(self, s):
        for slot in range(2 * len(self.stages) + 1):
            c = s - PLANE_SKEW * slot
            pl.when((c >= 0) & (c < self.count))(functools.partial(self.stage, slot, c))

    def drain(self):
        def one(c, carry):
            for k in range(len(self.stages)):
                self.inward_wait(k, c).wait_send()
                self.outward(k, c).wait_send()
            return carry

        lax.fori_loop(0, self.count, one, 0)


def line_kernel(
    size, chunk, returns, owners, pairs, stages, source_count, side_count, out_count, *refs
):
    streams = len(returns)
    returned = [k for k in range(streams) if returns[k]]
    parts, refs = refs[:streams], refs[streams:]
    sides, refs = refs[:side_count], refs[side_count:]
    shared, refs = dict(zip(returned, refs)), refs[len(returned) :]
    kept, refs = refs[:out_count], refs[out_count:]
    inbox, send_up, recv_up, send_back, recv_back = refs[:5]
    plane = None
    if source_count:
        plane_inbox, plane_send, plane_recv = refs[9 : 9 + len(stages)], *refs[9 + len(stages) :]
        plane = PlaneSum(
            stages, sides[:source_count], kept[1], plane_inbox, plane_send, plane_recv
        )
        sides = sides[source_count:]
    half = parts[0].shape[0] // 2
    count = half // chunk
    last = size - 1
    me = lax.axis_index("tensor")
    above, below = jnp.minimum(me + 1, last), jnp.maximum(me - 1, 0)
    flows = ((me, above, below), (last - me, below, above))

    barrier = pltpu.get_barrier_semaphore()

    def greet(axis, other):
        pl.semaphore_signal(
            barrier, inc=1, device_id={axis: other}, device_id_type=pl.DeviceIdType.MESH
        )

    if pairs:
        for axis, bit in pairs:
            greet(axis, partner(axis, bit))
        far_above = jnp.where(me % 2 == 0, 0, 1) * jnp.where(me < last, 1, 0)
        far_below = jnp.where(me % 2 == 0, 1, 0) * jnp.where(me > 0, 1, 0)
        pl.when(far_above == 1)(lambda: greet("tensor", above))
        pl.when(far_below == 1)(lambda: greet("tensor", below))
        pl.semaphore_wait(barrier, len(pairs) + far_above + far_below)
    else:
        pl.when(me < last)(lambda: greet("tensor", above))
        pl.when(me > 0)(lambda: greet("tensor", below))
        pl.semaphore_wait(barrier, jnp.where((me > 0) & (me < last), 2, 1))

    def place(f, i):
        return pl.ds(pl.multiple_of(f * half + i * chunk, chunk), chunk)

    def local(i):
        return pl.ds(pl.multiple_of(i * chunk, chunk), chunk)

    def onward(k, f, i, source):
        return pltpu.make_async_remote_copy(
            src_ref=source,
            dst_ref=inbox.at[k, f, local(i)],
            send_sem=send_up.at[k, f, i],
            recv_sem=recv_up.at[k, f, i],
            device_id={"tensor": flows[f][1]},
            device_id_type=pl.DeviceIdType.MESH,
        )

    def backward(k, f, i):
        block = shared[k].at[place(f, i)]
        return pltpu.make_async_remote_copy(
            src_ref=block,
            dst_ref=block,
            send_sem=send_back.at[k, f, i],
            recv_sem=recv_back.at[k, f, i],
            device_id={"tensor": flows[f][2]},
            device_id_type=pl.DeviceIdType.MESH,
        )

    def reduce_chunk(k, f, i):
        position = flows[f][0]
        mine = parts[k].at[place(f, i)]
        slot = inbox.at[k, f, local(i)]

        @pl.when(position == 0)
        def _():
            pl.when(i >= LINE_WINDOW)(lambda: onward(k, f, i - LINE_WINDOW, mine).wait_send())
            onward(k, f, i, mine).start()

        @pl.when(position > 0)
        def _():
            onward(k, f, i, slot).wait_recv()
            total = slot[...].astype(F32) + mine[...].astype(F32)

            @pl.when(position < last)
            def _():
                slot[...] = total.astype(BF16)
                onward(k, f, i, slot).start()

            @pl.when(position == last)
            def _():
                result = owners[k](total, place(f, i), local(i), sides, kept)
                if returns[k]:
                    shared[k][place(f, i), :] = result.astype(BF16)
                    backward(k, f, i).start()

    def pass_back(k, f, i):
        position = flows[f][0]

        @pl.when((position < last) & (i >= 0) & (i < count))
        def _():
            backward(k, f, i).wait_recv()
            pl.when(position > 0)(lambda: backward(k, f, i).start())

    def step(s, carry):
        for k in range(streams):
            for f in range(2):
                i = s - LINE_SKEW * flows[f][0]
                pl.when((i >= 0) & (i < count))(lambda: reduce_chunk(k, f, i))
        for k in returned:
            for f in range(2):
                pass_back(k, f, s - LINE_SKEW * (2 * last - flows[f][0]))
        if plane:
            plane.step(s)
        for n in range(len(pairs) + 1 if pairs else 0):
            pl.when(s == n * gap)(lambda: advance_gains(n))
        return carry

    steps = count + 2 * LINE_SKEW * last
    if plane:
        steps = max(steps, plane.steps())
    gap = steps // (len(pairs) + 1)
    if pairs:
        slots, sums, send_pair, recv_pair = refs[5:9]
        sums[0] = sides[-1][...]
    elif len(kept) > 1:
        kept[1][...] = jnp.zeros_like(kept[1])

    def swap_gains(n):
        return pltpu.make_async_remote_copy(
            src_ref=sums.at[n],
            dst_ref=slots.at[n],
            send_sem=send_pair.at[n],
            recv_sem=recv_pair.at[n],
            device_id={pairs[n][0]: partner(*pairs[n])},
            device_id_type=pl.DeviceIdType.MESH,
        )

    def advance_gains(n):
        if n > 0:
            swap_gains(n - 1).wait()
            sums[n] = sums[n - 1] + slots[n - 1]
        if n < len(pairs):
            swap_gains(n).start()
        else:
            kept[0][...] = sums[n]

    lax.fori_loop(0, steps, step, 0)

    def drain(i, carry):
        for k in range(streams):
            for f in range(2):
                position = flows[f][0]
                waited = (position == 0) & (i < count - LINE_WINDOW)
                pl.when((position < last) & ~waited)(
                    lambda: onward(k, f, i, inbox.at[k, f, local(i)]).wait_send()
                )
                if returns[k]:
                    pl.when(position > 0)(lambda: backward(k, f, i).wait_send())
        return carry

    lax.fori_loop(0, count, drain, 0)
    if plane:
        plane.drain()


def line_sum(
    parts, owners, sides, kept, collective_id, returns=(True,), pairs=(), stages=(), sources=()
):
    rows, width = parts[0].shape
    size = lax.axis_size("tensor")
    streams = len(parts)
    chunk = max(16, min(LINE_CHUNK, rows // 32))
    count = rows // 2 // chunk
    whole = pl.BlockSpec(memory_space=pltpu.VMEM)
    scalar = pl.BlockSpec(memory_space=pltpu.SMEM)
    sems = pltpu.SemaphoreType.DMA((streams, 2, count))
    outs = [jax.ShapeDtypeStruct((rows, width), BF16)] * sum(returns) + list(kept)
    extra = []
    if pairs:
        pair_sems = pltpu.SemaphoreType.DMA((len(pairs),))
        extra = [
            pltpu.VMEM((len(pairs), 8, width), F32),
            pltpu.VMEM((len(pairs) + 1, 8, width), F32),
            pair_sems,
            pair_sems,
        ]
    if sources:
        plane_rows = sum(source.shape[0] for source in sources)
        unit = 2 ** len(stages) * PLANE_ROWS
        kept = [*kept, jax.ShapeDtypeStruct((plane_rows, width), BF16)]
        outs.append(kept[-1])
        extra += [pltpu.VMEM((plane_rows >> (k + 1), width), BF16) for k in range(len(stages))]
        extra += [pltpu.SemaphoreType.DMA((2 * len(stages), plane_rows // unit))] * 2
        sides = [*sources, *sides]
    return pl.pallas_call(
        functools.partial(
            line_kernel,
            size,
            chunk,
            returns,
            owners,
            pairs,
            stages,
            len(sources),
            len(sides),
            len(kept),
        ),
        out_shape=outs,
        in_specs=[whole] * streams + [scalar if s.ndim == 1 else whole for s in sides],
        out_specs=[whole] * len(outs),
        scratch_shapes=[pltpu.VMEM((streams, 2, rows // 2, width), BF16)] + [sems] * 4 + extra,
        compiler_params=pltpu.CompilerParams(
            collective_id=collective_id, has_side_effects=True, vmem_limit_bytes=56 * 2**20
        ),
        cost_estimate=pl.CostEstimate(
            flops=streams * rows * width,
            bytes_accessed=streams * 300 * 2**20,
            transcendentals=0,
        ),
    )(*parts, *sides)


def unit_of(rows):
    inverse = lax.rsqrt(jnp.mean(rows * rows, axis=-1, keepdims=True) + EPSILON)
    return rows * inverse, inverse


def own_hidden(total, where, here, sides, kept):
    x_ref, gain_ref = sides
    hidden = x_ref[where, :].astype(F32) + total
    kept[0][here, :] = hidden
    return unit_of(hidden)[0] * gain_ref[...]


def own_dhidden(total, where, here, sides, kept):
    x_ref, hidden_ref, cot_ref, gain_ref, factor = sides
    unit, inverse = unit_of(hidden_ref[here, :])
    kept[1][...] += jnp.sum(total * unit, axis=0, keepdims=True)
    dhidden = norm_back(total, unit, inverse, gain_ref[...])
    kept[0][here, :] = dhidden
    return cot_ref[where, :].astype(F32) * factor[0] + dhidden


def own_output(total, where, here, sides, kept):
    x_ref, hidden_ref, cot_ref, gain_ref, factor = sides
    x = x_ref[where, :].astype(F32)
    result = x + factor[1] * ((hidden_ref[here, :] - x) + total)
    kept[2][here, :] = result.astype(BF16)


def own_dinput(total, where, here, sides, kept):
    x_ref, dhidden_ref, gain_ref, _ = sides
    unit, inverse = unit_of(x_ref[where, :].astype(F32))
    return dhidden_ref[here, :] + norm_back(total, unit, inverse, gain_ref[...])


def cut_half(own):
    step = own.shape[0] // SPREAD_PIECES
    return [[own[p * step : (p + 1) * step]] for p in range(SPREAD_PIECES)]


def send_wave(pieces, wave):
    size = lax.axis_size("tensor")
    for p, hops in enumerate(pieces):
        h = wave - p
        if 0 <= h < size - 1:
            perm = [(size - 1 - h, size - 2 - h), (h, h + 1)]
            hops.append(lax.ppermute(hops[-1], "tensor", perm))


def tie(pieces, others):
    heads, others = lax.optimization_barrier(([hops[-1] for hops in pieces], others))
    for hops, head in zip(pieces, heads):
        hops[-1] = head
    return others


def join_kernel(size, *refs):
    pieces, out = refs[:-1], refs[-1]
    me = lax.axis_index("tensor")
    step = pieces[0].shape[0]
    half = out.shape[0] // 2
    for p in range(SPREAD_PIECES):
        for h in range(size):
            for f, wanted in enumerate((size - 1 - me, me)):

                @pl.when(wanted == h)
                def _():
                    out[pl.ds(f * half + p * step, step), :] = pieces[p * size + h][...]


def join_halves(pieces):
    size = lax.axis_size("tensor")
    step, width = pieces[0].shape
    whole = pl.BlockSpec(memory_space=pltpu.VMEM)
    return pl.pallas_call(
        functools.partial(join_kernel, size),
        out_shape=jax.ShapeDtypeStruct((2 * SPREAD_PIECES * step, width), BF16),
        in_specs=[whole] * len(pieces),
        out_specs=whole,
        compiler_params=pltpu.CompilerParams(vmem_limit_bytes=40 * 2**20),
    )(*pieces)


def rotary_tables(positions):
    inverse = 1.0 / 10000.0 ** (jnp.arange(0, HEAD_DIM, 2, dtype=F32) / HEAD_DIM)
    angle = positions.astype(F32)[:, None] * inverse[None, :]
    return (jnp.cos(angle), jnp.sin(angle))


def contract_rows(left, right):
    return jnp.einsum("rd,rf->df", left, right, preferred_element_type=F32)


def contract_cols(left, right):
    return jnp.einsum("rc,dc->rd", left, right, preferred_element_type=F32)


def norm_back(dnormed, unit, inverse, gain):
    scaled = dnormed * gain
    return inverse * (scaled - unit * jnp.mean(scaled * unit, axis=-1, keepdims=True))


def flags_kernel(size, mine, everyone, send_sem, recv_sem):
    me = lax.axis_index("dp")
    barrier = pltpu.get_barrier_semaphore()
    others = [lax.rem(me + s, size) for s in range(1, size)]
    for other in others:
        pl.semaphore_signal(
            barrier, inc=1, device_id={"dp": other}, device_id_type=pl.DeviceIdType.MESH
        )
    pl.semaphore_wait(barrier, size - 1)

    def send(s, slot):
        return pltpu.make_async_remote_copy(
            src_ref=mine,
            dst_ref=everyone.at[slot],
            send_sem=send_sem.at[s],
            recv_sem=recv_sem.at[s],
            device_id={"dp": others[s]},
            device_id_type=pl.DeviceIdType.MESH,
        )

    for s in range(size - 1):
        send(s, me).start()
    everyone[me] = mine[...]
    for s in range(size - 1):
        send(s, me).wait_send()
        send(s, lax.rem(me + 2 * size - 1 - s, size)).wait_recv()


def share_flags(row):
    size = lax.axis_size("dp")
    tile = jnp.zeros((8, 128), jnp.int32).at[0, : row.shape[0]].set(row)
    sems = pltpu.SemaphoreType.DMA((size - 1,))
    whole = pl.BlockSpec(memory_space=pltpu.VMEM)
    shared = pl.pallas_call(
        functools.partial(flags_kernel, size),
        out_shape=jax.ShapeDtypeStruct((size, 8, 128), jnp.int32),
        in_specs=[whole],
        out_specs=whole,
        scratch_shapes=[sems, sems],
        compiler_params=pltpu.CompilerParams(collective_id=1, has_side_effects=True),
    )(tile)
    return shared[:, 0, : row.shape[0]]


def shift_ctx(part, s):
    size = lax.axis_size("ctx")
    return lax.ppermute(part, "ctx", [(i, (i + s) % size) for i in range(size)])


def swap_core(part):
    return lax.ppermute(part, "dp", [(i, i ^ 1) for i in range(lax.axis_size("dp"))])


def gather_parts(own, paired):
    parts = []
    for s in range(lax.axis_size("ctx")):
        here = own if s == 0 else shift_ctx(own, s)
        parts += [here, swap_core(here)] if paired else [here]
    return parts


def collect_parts(parts, paired):
    terms = [parts[0]]
    if paired:
        terms.append(swap_core(parts[1]))
    per = 2 if paired else 1
    for s in range(1, lax.axis_size("ctx")):
        near = parts[per * s]
        if paired:
            near = (near.astype(F32) + swap_core(parts[per * s + 1]).astype(F32)).astype(BF16)
        terms.append(shift_ctx(near, -s))
    return terms


def block_pass(
    paired,
    first_id,
    span,
    x_low,
    cot_low,
    keep,
    scale,
    order_row,
    attn_gain,
    ffn_gain,
    w_query,
    w_key,
    w_value,
    w_output,
    w_gate,
    w_up,
    w_down,
):
    rows, width = x_low.shape
    dp_size, ctx_size = lax.axis_size("dp"), lax.axis_size("ctx")
    spans = order_row.shape[0]
    ctx = lax.axis_index("ctx")
    core = lax.axis_index("dp") % 2
    per_part = rows // span
    order_parts = []
    for s in range(ctx_size):
        group = (ctx + ctx_size - s) % ctx_size
        places = [group * 2 + core, group * 2 + 1 - core] if paired else [group]
        order_parts += [
            lax.dynamic_slice_in_dim(order_row, place * per_part, per_part) for place in places
        ]
    query_order, key_order = order_parts[0], jnp.concatenate(order_parts)
    row_index = jnp.arange(rows, dtype=jnp.int32)
    starts = jnp.sum(
        jnp.where(
            (row_index // span)[:, None] == jnp.arange(per_part, dtype=jnp.int32)[None, :],
            query_order[None, :],
            0,
        ),
        axis=1,
    )
    cosine, sine = rotary_tables(starts * span + row_index % span)

    wide_cosine = jnp.concatenate([cosine, cosine], axis=1)
    wide_sine = jnp.concatenate([-sine, sine], axis=1)
    attn_row, ffn_row = attn_gain[None, :], ffn_gain[None, :]
    normed_one, queries, kv_own = project(
        x_low, attn_row, wide_cosine, wide_sine, w_query, w_key, w_value
    )
    kv_parts = gather_parts(kv_own, paired)
    dffn = (cot_low.astype(F32) * (keep * scale)).astype(BF16)
    dacted = contract_cols(dffn, w_down)
    if not paired:
        queries, dacted = lax.optimization_barrier((queries, dacted))
    mixed, logs = attend(queries, kv_parts, query_order, key_order, span)

    half_rows = jax.ShapeDtypeStruct((rows // 2, width), F32)
    gain_row = jax.ShapeDtypeStruct((1, width), F32)
    attn_part = nn_dot(mixed, w_output).astype(BF16)
    normed_two, hidden = line_sum(
        [attn_part], [own_hidden], [x_low, ffn_row], [half_rows], first_id
    )

    factors = jnp.stack([keep * scale, keep])
    acted, dgate, dupward = hidden_units(normed_two, dacted, w_gate, w_up)
    early_grads = [
        contract_rows(acted, dffn).astype(BF16),
        contract_rows(normed_two, dgate).astype(BF16),
        contract_rows(normed_two, dupward).astype(BF16),
    ]
    late_grads = [early_grads.pop()] if paired else []
    acted, dgate, dupward, early_grads, late_grads = lax.optimization_barrier(
        (acted, dgate, dupward, early_grads, late_grads)
    )
    early_grads = lax.psum(early_grads, ("dp", "ctx"))
    dnormed_part, ffn_part = width_parts(acted, dgate, dupward, w_gate, w_up, w_down)
    dattn, dhidden, ffn_gain_part, output_half = line_sum(
        [dnormed_part, ffn_part],
        [own_dhidden, own_output],
        [x_low, hidden, cot_low, ffn_row, factors],
        [half_rows, gain_row, jax.ShapeDtypeStruct((rows // 2, width), BF16)],
        first_id + 1,
        (True, False),
    )
    pieces = cut_half(output_half)
    send_wave(pieces, 0)
    dmixed = contract_cols(dattn, w_output).astype(BF16)
    dq_proj, *dkv_parts = attend_back(
        queries, dmixed, mixed, logs, cosine, sine, kv_parts, query_order, key_order, span
    )
    dq_proj, dkv_parts = tie(pieces, (dq_proj, dkv_parts))
    send_wave(pieces, 1)
    terms = collect_parts(dkv_parts, paired)
    grad_query = contract_rows(dq_proj, normed_one).astype(BF16)
    grad_output = contract_rows(mixed, dattn).astype(BF16)
    grad_query, grad_output = tie(pieces, (grad_query, grad_output))
    send_wave(pieces, 2)
    if not paired:
        early_grads = [g.astype(F32) for g in early_grads]
        terms, early_grads = lax.optimization_barrier((terms, early_grads))
    terms, grad_query, grad_output = lax.optimization_barrier((terms, grad_query, grad_output))
    dkv_proj, dnormed_one, attn_gain_part = project_back(
        x_low, dq_proj, terms, wide_cosine, wide_sine, w_query, w_key, w_value
    )
    gain_parts = jnp.concatenate(
        [attn_gain_part, ffn_gain_part, jnp.zeros((6, width), F32)], axis=0
    )
    grad_kv = contract_rows(dkv_proj, normed_one).astype(BF16)
    dnormed_one, early_grads, late_grads = tie(pieces, (dnormed_one, early_grads, late_grads))
    late_grads = lax.psum(late_grads, ("ctx", "dp")) if paired else []
    for wave in range(3, lax.axis_size("tensor") + SPREAD_PIECES):
        send_wave(pieces, wave)
    through, gains, attn_grads = line_sum(
        [dnormed_one],
        [own_dinput],
        [x_low, dhidden, attn_row, gain_parts],
        [jax.ShapeDtypeStruct((8, width), F32)],
        first_id + 2,
        (True,),
        tuple(pair_steps((dp_size, ctx_size, lax.axis_size("tensor")))),
        plane_steps(dp_size, ctx_size),
        [grad_query, grad_kv, grad_output],
    )
    through, gains, attn_grads, early_grads, late_grads, pieces = lax.optimization_barrier(
        (through, gains, attn_grads, early_grads, late_grads, pieces)
    )
    output = join_halves([hop for hops in pieces for hop in hops])
    grads = (attn_grads, *early_grads, *late_grads)
    return output, through, gains, grads


def per_device(
    inputs,
    cotangent,
    skip_mask,
    group_ids,
    span_order,
    exit_scale,
    attn_gain,
    ffn_gain,
    *weights,
):
    _, rows, width = inputs.shape
    spans = span_order.shape[1]
    own_spans = spans // lax.axis_size("ctx")
    span = rows // own_spans
    me = lax.axis_index("dp")
    core = me % 2
    x_low, cot_low = inputs[0], cotangent[0]
    flags = share_flags(jnp.concatenate([skip_mask, group_ids, span_order[0]]))
    runs, groups = flags[:, 0], flags[:, 1]
    scale_of = lambda group: jnp.where(group == 1, exit_scale[1], exit_scale[0])
    own_run, own_scale = skip_mask[0], scale_of(group_ids[0])
    gains = (attn_gain, ffn_gain)

    def alone():
        return block_pass(
            False,
            2,
            span,
            x_low,
            cot_low,
            own_run.astype(F32),
            own_scale,
            span_order[0],
            *gains,
            *weights,
        )

    def shared():
        half = rows // 2
        other = me + 1 - 2 * core
        take = lambda a, i: lax.dynamic_slice_in_dim(a, i * half, half, 0)
        pick = lambda a: lax.dynamic_index_in_dim(a, other, 0, keepdims=False)
        other_run = pick(runs)
        use_own = (own_run == 1) | ((other_run == 0) & (core == 0))
        choose = lambda mine, theirs: jnp.where(use_own, mine, theirs)
        work = lambda a: choose(take(a, core), swap_core(take(a, 1 - core)))
        output, through, *rest = block_pass(
            True,
            5,
            span,
            work(x_low),
            work(cot_low),
            choose(own_run, other_run).astype(F32),
            choose(own_scale, scale_of(pick(groups))),
            choose(span_order[0], pick(flags[:, 2:])),
            *gains,
            *weights,
        )

        def whole(part):
            theirs = swap_core(part)
            first, second = jnp.where(core == 0, part, theirs), jnp.where(core == 0, theirs, part)
            return jnp.concatenate([first, second], 0)

        through = jnp.where(own_run == 1, whole(through), 0)
        return whole(output), through, *rest

    def finish(output, through, sums, grads):
        output = jnp.where(own_run == 1, output, x_low)
        input_grad = cot_low.astype(F32) * own_scale + through.astype(F32)
        attn_grads = unpack(grads[0], *[w.shape[1] for w in weights[:3]])
        grads = [g.astype(F32) for g in grads[1:]]
        return lax.optimization_barrier(
            (output, input_grad, sums[0], sums[1], *attn_grads, *grads)
        )

    if own_spans % 2 == 0 and lax.axis_size("dp") % 2 == 0:
        pairs = runs.reshape(-1, 2)
        results = lax.cond(
            jnp.all(pairs[:, 0] * pairs[:, 1] == 0),
            lambda: finish(*shared()),
            lambda: finish(*alone()),
        )
    else:
        results = finish(*alone())
    output, input_grad, grad_attn_gain, grad_ffn_gain = results[:4]
    grad_query, grad_key, grad_value, grad_output, grad_down, grad_gate, grad_up = results[4:]
    return (
        output.reshape(inputs.shape),
        input_grad.reshape(inputs.shape),
        grad_attn_gain,
        grad_ffn_gain,
        grad_query,
        grad_key,
        grad_value,
        grad_output,
        grad_gate,
        grad_up,
        grad_down,
    )


def solution(mesh):
    rows = P("dp", "ctx", None)
    by_column, by_row = P(None, "tensor"), P("tensor", None)
    in_specs = (rows, rows, P("dp"), P("dp"), P("dp", None), P(), P(), P())
    in_specs += (by_column,) * 3 + (by_row,) + (by_column,) * 2 + (by_row,)
    out_specs = (rows, rows, P(), P()) + (by_column,) * 3 + (by_row,) + (by_column,) * 2 + (by_row,)
    return jax.shard_map(
        per_device, mesh=mesh, in_specs=in_specs, out_specs=out_specs, check_vma=False
    )
```

```python
import functools

import jax
import jax.numpy as jnp
from jax import lax
from jax.experimental import pallas as pl
from jax.experimental.pallas import tpu as pltpu
from jax.sharding import PartitionSpec as P

HEAD_DIM = 128
EPSILON = 1e-05
NEG_BIG = -1e30
FACTOR = HEAD_DIM ** (-0.5)
LOG2E = 1.4426950408889634
QUERY_BLOCK = 256
BF16 = jnp.bfloat16
F32 = jnp.float32

NT = (((1,), (1,)), ((), ()))


def nt_dot(left, right):
    return lax.dot_general(left, right, NT, preferred_element_type=F32)


def nn_dot(left, right):
    return jnp.dot(left, right, preferred_element_type=F32)


def stack_heads(block, group):
    return jnp.concatenate(
        [block[:, h * HEAD_DIM : (h + 1) * HEAD_DIM] for h in range(group)], axis=0
    )


def hide_later(scores, first_row, rows, fill):
    key_row = lax.broadcasted_iota(jnp.int32, scores.shape, 0)
    query_row = lax.broadcasted_iota(jnp.int32, scores.shape, 1) % rows + first_row
    return jnp.where(key_row <= query_row, scores, fill)


def over_spans(kv_refs, span, visit, query_order, key_order, first):
    order = query_order[first // span]
    seen = 0
    for part, kv_ref in enumerate(kv_refs):
        count = kv_ref.shape[1] // span

        def one_span(j, carry, part=part, seen=seen):
            place = pl.multiple_of(j * span, span)
            column = pl.multiple_of((seen + j) * span, span)
            pl.when(key_order[seen + j] < order)(lambda: visit(part, place, column, False))
            pl.when(key_order[seen + j] == order)(lambda: visit(part, place, column, True))
            return carry

        lax.fori_loop(0, count, one_span, 0)
        seen += count


def attend_kernel(group, span, parts, query_order, key_order, q_ref, *refs):
    kv_refs, (o_ref, lse_ref, vt_ref, top, total, acc) = refs[:parts], refs[parts:]
    rows = q_ref.shape[0]
    step = pl.program_id(1)
    first = step * rows

    @pl.when(step == 0)
    def _():
        for part, kv_ref in enumerate(kv_refs):
            size = kv_ref.shape[1]
            vt_ref[:, part * size : (part + 1) * size] = kv_ref[1].T

    queries = stack_heads(q_ref[...], group)
    top[...] = jnp.full_like(top, NEG_BIG)
    total[...] = jnp.zeros_like(total)
    acc[...] = jnp.zeros_like(acc)

    def visit(part, place, column, diagonal):
        keys = kv_refs[part][0, pl.ds(place, span), :]
        scores = nt_dot(keys, queries) * (FACTOR * LOG2E)
        if diagonal:
            scores = hide_later(scores, first % span, rows, NEG_BIG)
        before = top[...]
        now = jnp.maximum(before, jnp.max(scores, axis=0, keepdims=True))
        weights = jnp.exp2(scores - now)
        shrink = jnp.exp2(before - now)
        top[...] = now
        total[...] = total[...] * shrink + jnp.sum(weights, axis=0, keepdims=True)
        acc[...] = acc[...] * shrink + nn_dot(
            vt_ref[:, pl.ds(column, span)], weights.astype(BF16)
        )

    over_spans(kv_refs, span, visit, query_order, key_order, first)
    mixed = acc[...] / total[...]
    logs = top[...] + jnp.log2(total[...])
    for h in range(group):
        part = slice(h * rows, (h + 1) * rows)
        o_ref[:, h * HEAD_DIM : (h + 1) * HEAD_DIM] = mixed[:, part].T.astype(BF16)
        lse_ref[0, h : h + 1, :] = logs[:, part]


def attend(queries, kv_parts, query_order, key_order, span):
    rows, width = queries.shape
    part_rows, kv_width = kv_parts[0].shape[1:]
    full = part_rows * len(kv_parts)
    kv_heads = kv_width // HEAD_DIM
    group = width // kv_width
    block = min(QUERY_BLOCK, span)
    query_spec = pl.BlockSpec((block, group * HEAD_DIM), lambda g, i, *_: (i, g))
    kv_spec = pl.BlockSpec((2, part_rows, HEAD_DIM), lambda g, i, *_: (0, 0, g))
    return pl.pallas_call(
        functools.partial(attend_kernel, group, span, len(kv_parts)),
        grid_spec=pltpu.PrefetchScalarGridSpec(
            num_scalar_prefetch=2,
            grid=(kv_heads, rows // block),
            in_specs=[query_spec] + [kv_spec] * len(kv_parts),
            out_specs=[
                query_spec,
                pl.BlockSpec((1, group, block), lambda g, i, *_: (g, 0, i)),
            ],
            scratch_shapes=[
                pltpu.VMEM((HEAD_DIM, full), BF16),
                pltpu.VMEM((1, group * block), F32),
                pltpu.VMEM((1, group * block), F32),
                pltpu.VMEM((HEAD_DIM, group * block), F32),
            ],
        ),
        out_shape=[
            jax.ShapeDtypeStruct((rows, width), BF16),
            jax.ShapeDtypeStruct((kv_heads, group, rows), F32),
        ],
        compiler_params=pltpu.CompilerParams(vmem_limit_bytes=32 * 2**20),
        cost_estimate=pl.CostEstimate(
            flops=4 * rows * full * width,
            bytes_accessed=4 * rows * width + 4 * full * kv_width,
            transcendentals=rows * full * width // HEAD_DIM,
        ),
    )(query_order, key_order, queries, *kv_parts)


def attend_back_kernel(
    group,
    span,
    parts,
    query_order,
    key_order,
    q_ref,
    do_ref,
    o_ref,
    lse_ref,
    cos_ref,
    sin_ref,
    *refs,
):
    kv_refs, dq_ref, dkv_refs = refs[:parts], refs[parts], refs[parts + 1 : 2 * parts + 1]
    kt_ref, acc, sums = refs[2 * parts + 1 :]
    rows = q_ref.shape[0]
    step = pl.program_id(1)
    first = step * rows
    queries = stack_heads(q_ref[...], group)
    dmixed = stack_heads(do_ref[...], group)
    mixed = stack_heads(o_ref[...], group)
    product = dmixed.astype(F32) * mixed.astype(F32)
    delta = jnp.sum(product.T, axis=0, keepdims=True)
    logs = jnp.concatenate([lse_ref[0, h : h + 1, :] for h in range(group)], axis=1)
    acc[...] = jnp.zeros_like(acc)

    @pl.when(step == 0)
    def _():
        sums[...] = jnp.zeros_like(sums)
        for part, kv_ref in enumerate(kv_refs):
            size = kv_ref.shape[1]
            kt_ref[:, part * size : (part + 1) * size] = kv_ref[0].T

    def visit(part, place, column, diagonal):
        here = pl.ds(place, span)
        scores = nt_dot(kv_refs[part][0, here, :], queries) * (FACTOR * LOG2E)
        probs = jnp.exp2(scores - logs)
        if diagonal:
            probs = hide_later(probs, first % span, rows, 0.0)
        dprobs = nt_dot(kv_refs[part][1, here, :], dmixed)
        dscore = (probs * (dprobs - delta)).astype(BF16)
        sums[part, 1, here, :] += nn_dot(probs.astype(BF16), dmixed)
        sums[part, 0, here, :] += nn_dot(dscore, queries)
        acc[...] += nn_dot(kt_ref[:, pl.ds(column, span)], dscore)

    over_spans(kv_refs, span, visit, query_order, key_order, first)
    for h in range(group):
        grad = acc[:, h * rows : (h + 1) * rows] * FACTOR
        half = HEAD_DIM // 2
        leading, trailing = grad[:half], grad[half:]
        cosine, sine = cos_ref[...], sin_ref[...]
        turned = jnp.concatenate(
            [leading * cosine + trailing * sine, trailing * cosine - leading * sine], axis=0
        )
        dq_ref[:, h * HEAD_DIM : (h + 1) * HEAD_DIM] = turned.T.astype(BF16)

    @pl.when(step == pl.num_programs(1) - 1)
    def _():
        for part, dkv_ref in enumerate(dkv_refs):
            dkv_ref[0] = (sums[part, 0] * FACTOR).astype(dkv_ref.dtype)
            dkv_ref[1] = sums[part, 1].astype(dkv_ref.dtype)


def attend_back(
    queries, dmixed, mixed, logs, cosine, sine, kv_parts, query_order, key_order, span
):
    rows, width = queries.shape
    part_rows, kv_width = kv_parts[0].shape[1:]
    parts = len(kv_parts)
    full = part_rows * parts
    kv_heads = kv_width // HEAD_DIM
    group = width // kv_width
    block = min(QUERY_BLOCK, span)
    half = HEAD_DIM // 2
    query_spec = pl.BlockSpec((block, group * HEAD_DIM), lambda g, i, *_: (i, g))
    kv_spec = pl.BlockSpec((2, part_rows, HEAD_DIM), lambda g, i, *_: (0, 0, g))
    table_spec = pl.BlockSpec((half, block), lambda g, i, *_: (0, i))
    kinds = [F32] + [BF16] * (parts - 1)
    return pl.pallas_call(
        functools.partial(attend_back_kernel, group, span, parts),
        grid_spec=pltpu.PrefetchScalarGridSpec(
            num_scalar_prefetch=2,
            grid=(kv_heads, rows // block),
            in_specs=[
                query_spec,
                query_spec,
                query_spec,
                pl.BlockSpec((1, group, block), lambda g, i, *_: (g, 0, i)),
                table_spec,
                table_spec,
            ]
            + [kv_spec] * parts,
            out_specs=[query_spec] + [kv_spec] * parts,
            scratch_shapes=[
                pltpu.VMEM((HEAD_DIM, full), BF16),
                pltpu.VMEM((HEAD_DIM, group * block), F32),
                pltpu.VMEM((parts, 2, part_rows, HEAD_DIM), F32),
            ],
        ),
        out_shape=[jax.ShapeDtypeStruct((rows, width), BF16)]
        + [jax.ShapeDtypeStruct((2, part_rows, kv_width), kind) for kind in kinds],
        compiler_params=pltpu.CompilerParams(vmem_limit_bytes=40 * 2**20),
        cost_estimate=pl.CostEstimate(
            flops=10 * rows * full * width,
            bytes_accessed=8 * rows * width + 14 * full * kv_width,
            transcendentals=rows * full * width // HEAD_DIM,
        ),
    )(
        query_order,
        key_order,
        queries,
        dmixed,
        mixed,
        logs,
        cosine.T,
        sine.T,
        *kv_parts,
    )


ROW_BLOCK = 256


def by_rows(block, width):
    return pl.BlockSpec((block, width), lambda i: (i, 0))


def held(array):
    return pl.BlockSpec(
        array.shape, lambda i: (0,) * array.ndim, pipeline_mode=pl.Buffered(1)
    )


def column_cuts(width, size=512):
    return [slice(c, min(c + size, width)) for c in range(0, width, size)]


def turn(field, cosine, sine):
    return field * cosine + pltpu.roll(field, HEAD_DIM // 2, 1) * sine


def project_kernel(x_ref, gain_ref, cos_ref, sin_ref, wq, wk, wv, n_ref, q_ref, kv_ref):
    unit, _ = unit_of(x_ref[...].astype(F32))
    normed = (unit * gain_ref[...]).astype(BF16)
    n_ref[...] = normed
    cosine, sine = cos_ref[...], sin_ref[...]
    queries, keys = nn_dot(normed, wq[...]), nn_dot(normed, wk[...])
    for h in range(q_ref.shape[1] // HEAD_DIM):
        head = slice(h * HEAD_DIM, (h + 1) * HEAD_DIM)
        q_ref[:, head] = turn(queries[:, head], cosine, sine).astype(BF16)
    for h in range(kv_ref.shape[2] // HEAD_DIM):
        head = slice(h * HEAD_DIM, (h + 1) * HEAD_DIM)
        kv_ref[0, :, head] = turn(keys[:, head], cosine, sine).astype(BF16)
    kv_ref[1] = nn_dot(normed, wv[...]).astype(BF16)


def project(x_low, gain_row, cosine, sine, w_query, w_key, w_value):
    rows, width = x_low.shape
    block = min(ROW_BLOCK, rows)
    heads_width, kv_width = w_query.shape[1], w_key.shape[1]
    return pl.pallas_call(
        project_kernel,
        grid=(rows // block,),
        in_specs=[
            by_rows(block, width),
            held(gain_row),
            by_rows(block, HEAD_DIM),
            by_rows(block, HEAD_DIM),
            held(w_query),
            held(w_key),
            held(w_value),
        ],
        out_specs=[
            by_rows(block, width),
            by_rows(block, heads_width),
            pl.BlockSpec((2, block, kv_width), lambda i: (0, i, 0)),
        ],
        out_shape=[
            jax.ShapeDtypeStruct((rows, width), BF16),
            jax.ShapeDtypeStruct((rows, heads_width), BF16),
            jax.ShapeDtypeStruct((2, rows, kv_width), BF16),
        ],
        compiler_params=pltpu.CompilerParams(vmem_limit_bytes=40 * 2**20),
        cost_estimate=pl.CostEstimate(
            flops=2 * rows * width * (heads_width + 2 * kv_width),
            bytes_accessed=6 * rows * width + 2 * width * (heads_width + 2 * kv_width),
            transcendentals=rows,
        ),
    )(x_low, gain_row, cosine, sine, w_query, w_key, w_value)


def stream_cuts(sources, targets, sems, cuts):
    first = pl.program_id(0) == 0

    def copies(n):
        out = []
        for w, (source, target, by_column) in enumerate(zip(sources, targets, cuts[1])):
            start, size = cuts[0][n].start, cuts[0][n].stop - cuts[0][n].start
            place = (slice(None), pl.ds(start, size)) if by_column else (pl.ds(start, size),)
            out.append(
                pltpu.make_async_copy(source.at[place], target.at[place], sems.at[w, n])
            )
        return out

    @pl.when(first)
    def _():
        for n in range(len(cuts[0])):
            for copy in copies(n):
                copy.start()

    def ready(n):
        @pl.when(first)
        def _():
            for copy in copies(n):
                copy.wait()

    return ready


def hidden_kernel(n_ref, da_ref, wg_ref, wu_ref, a_ref, dg_ref, du_ref, wg, wu, sems):
    cuts = column_cuts(a_ref.shape[1])
    ready = stream_cuts((wg_ref, wu_ref), (wg, wu), sems, (cuts, (True, True)))
    normed = n_ref[...]
    for n, cut in enumerate(cuts):
        ready(n)
        gate, upward = nn_dot(normed, wg[:, cut]), nn_dot(normed, wu[:, cut])
        dacted = da_ref[:, cut]
        sigmoid = jax.nn.sigmoid(gate)
        silu = gate * sigmoid
        a_ref[:, cut] = (silu * upward).astype(BF16)
        slope = sigmoid * (1.0 + gate * (1.0 - sigmoid))
        dg_ref[:, cut] = (dacted * upward * slope).astype(BF16)
        du_ref[:, cut] = (dacted * silu).astype(BF16)


def hidden_units(normed, dacted, w_gate, w_up):
    rows, width = normed.shape
    units = w_gate.shape[1]
    block = min(ROW_BLOCK, rows)
    anywhere = pl.BlockSpec(memory_space=pl.ANY)
    return pl.pallas_call(
        hidden_kernel,
        grid=(rows // block,),
        in_specs=[by_rows(block, width), by_rows(block, units), anywhere, anywhere],
        out_specs=[by_rows(block, units)] * 3,
        out_shape=[jax.ShapeDtypeStruct((rows, units), BF16)] * 3,
        scratch_shapes=[pltpu.VMEM(w.shape, BF16) for w in (w_gate, w_up)]
        + [pltpu.SemaphoreType.DMA((2, len(column_cuts(units))))],
        compiler_params=pltpu.CompilerParams(vmem_limit_bytes=44 * 2**20),
        cost_estimate=pl.CostEstimate(
            flops=4 * rows * width * units,
            bytes_accessed=2 * rows * width + 4 * width * units + 10 * rows * units,
            transcendentals=rows * units,
        ),
    )(normed, dacted, w_gate, w_up)


def parts_kernel(
    a_ref, dg_ref, du_ref, wg_ref, wu_ref, wd_ref, dn_ref, f_ref, wg, wu, wd, sems
):
    cuts = column_cuts(dn_ref.shape[1])
    weights = (wg_ref, wu_ref, wd_ref), (wg, wu, wd)
    ready = stream_cuts(*weights, sems, (cuts, (False, False, True)))
    for n, cut in enumerate(cuts):
        ready(n)
        dnormed = nt_dot(dg_ref[...], wg[cut, :]) + nt_dot(du_ref[...], wu[cut, :])
        dn_ref[:, cut] = dnormed.astype(BF16)
        f_ref[:, cut] = nn_dot(a_ref[...], wd[:, cut]).astype(BF16)


def width_parts(acted, dgate, dupward, w_gate, w_up, w_down):
    rows, units = acted.shape
    width = w_gate.shape[0]
    block = min(ROW_BLOCK, rows)
    weights = (w_gate, w_up, w_down)
    return pl.pallas_call(
        parts_kernel,
        grid=(rows // block,),
        in_specs=[by_rows(block, units)] * 3 + [pl.BlockSpec(memory_space=pl.ANY)] * 3,
        out_specs=[by_rows(block, width)] * 2,
        out_shape=[jax.ShapeDtypeStruct((rows, width), BF16)] * 2,
        scratch_shapes=[pltpu.VMEM(w.shape, BF16) for w in weights]
        + [pltpu.SemaphoreType.DMA((3, len(column_cuts(width))))],
        compiler_params=pltpu.CompilerParams(vmem_limit_bytes=44 * 2**20),
        cost_estimate=pl.CostEstimate(
            flops=6 * rows * width * units,
            bytes_accessed=4 * rows * width + 6 * width * units + 6 * rows * units,
            transcendentals=0,
        ),
    )(acted, dgate, dupward, *weights)


def project_back_kernel(
    addends, x_ref, dq_ref, cos_ref, sin_ref, wq, wk, wv, *refs
):
    terms, (dkv_ref, dn_ref, gain_ref) = refs[:addends], refs[addends:]
    kv_width = terms[0].shape[2]
    cosine, sine = cos_ref[...], -sin_ref[...]
    dkeys, dvalues = terms[0][0], terms[0][1]
    for term in terms[1:]:
        dkeys, dvalues = dkeys + term[0].astype(F32), dvalues + term[1].astype(F32)
    for h in range(kv_width // HEAD_DIM):
        head = slice(h * HEAD_DIM, (h + 1) * HEAD_DIM)
        dkv_ref[:, head] = turn(dkeys[:, head], cosine, sine).astype(BF16)
    dkv_ref[:, kv_width:] = dvalues.astype(BF16)
    unit, _ = unit_of(x_ref[...].astype(F32))

    @pl.when(pl.program_id(0) == 0)
    def _():
        gain_ref[...] = jnp.zeros_like(gain_ref)

    for cut in column_cuts(dn_ref.shape[1]):
        dnormed = nt_dot(dq_ref[...], wq[cut, :])
        dnormed = dnormed + nt_dot(dkv_ref[:, :kv_width], wk[cut, :])
        dnormed = dnormed + nt_dot(dkv_ref[:, kv_width:], wv[cut, :])
        dn_ref[:, cut] = dnormed.astype(BF16)
        gain_ref[:, cut] += jnp.sum(dnormed * unit[:, cut], axis=0, keepdims=True)


def project_back(x_low, dq, terms, cosine, sine, w_query, w_key, w_value):
    rows, width = x_low.shape
    block = min(ROW_BLOCK, rows)
    heads_width, kv_width = w_query.shape[1], w_key.shape[1]
    kv_spec = pl.BlockSpec((2, block, kv_width), lambda i: (0, i, 0))
    return pl.pallas_call(
        functools.partial(project_back_kernel, len(terms)),
        grid=(rows // block,),
        in_specs=[
            by_rows(block, width),
            by_rows(block, heads_width),
            by_rows(block, HEAD_DIM),
            by_rows(block, HEAD_DIM),
            held(w_query),
            held(w_key),
            held(w_value),
        ]
        + [kv_spec] * len(terms),
        out_specs=[
            by_rows(block, 2 * kv_width),
            by_rows(block, width),
            pl.BlockSpec((1, width), lambda i: (0, 0)),
        ],
        out_shape=[
            jax.ShapeDtypeStruct((rows, 2 * kv_width), BF16),
            jax.ShapeDtypeStruct((rows, width), BF16),
            jax.ShapeDtypeStruct((1, width), F32),
        ],
        compiler_params=pltpu.CompilerParams(vmem_limit_bytes=40 * 2**20),
        cost_estimate=pl.CostEstimate(
            flops=2 * rows * width * (heads_width + 2 * kv_width),
            bytes_accessed=6 * rows * width + 2 * width * (heads_width + 2 * kv_width),
            transcendentals=rows,
        ),
    )(x_low, dq, cosine, sine, w_query, w_key, w_value, *terms)


def unpack_kernel(packed, *outs):
    row = 0
    for out in outs[:-1]:
        height = out.shape[1]
        out[...] = packed[row : row + height, :].astype(F32).T
        row += height
    outs[-1][...] = packed[row:, :].astype(F32)


def unpack(packed, *widths):
    total, width = packed.shape
    last = total - sum(widths)
    block = min(ROW_BLOCK, width)
    return pl.pallas_call(
        unpack_kernel,
        grid=(width // block,),
        in_specs=[pl.BlockSpec((total, block), lambda i: (0, i))],
        out_specs=[by_rows(block, w) for w in widths]
        + [pl.BlockSpec((last, block), lambda i: (0, i))],
        out_shape=[jax.ShapeDtypeStruct((width, w), F32) for w in widths]
        + [jax.ShapeDtypeStruct((last, width), F32)],
        compiler_params=pltpu.CompilerParams(vmem_limit_bytes=32 * 2**20),
    )(packed)


LINE_CHUNK = 32
LINE_WINDOW = 2
LINE_SKEW = 2
MESH_AXES = ("dp", "ctx", "tensor")
SPREAD_PIECES = 2
PLANE_ROWS = 16
PLANE_SKEW = 2


def pair_steps(sizes):
    steps = []
    for axis, size in zip(MESH_AXES, sizes):
        bit = 1
        while bit < size:
            steps.append((axis, bit))
            bit *= 2
    return steps


def partner(axis, bit):
    index = lax.axis_index(axis)
    return jnp.where((index // bit) % 2 == 0, index + bit, index - bit)


def plane_steps(dp_size, ctx_size):
    across, along, bit = [], [], 1
    while bit < ctx_size:
        across.append(("ctx", bit))
        bit *= 2
    bit = 2
    while bit < dp_size:
        along.append(("dp", bit))
        bit *= 2
    first = [(("dp", 1), ("dp", 1))] if dp_size > 1 else []
    return tuple(first + list(zip(across + along, along + across)))


class PlaneSum:
    def __init__(self, stages, sources, out, inbox, send_sem, recv_sem):
        self.stages, self.sources, self.out, self.inbox = stages, sources, out, inbox
        self.send_sem, self.recv_sem = send_sem, recv_sem
        self.unit = 2 ** len(stages) * PLANE_ROWS
        self.count = out.shape[0] // self.unit
        odd = lax.axis_index("dp") % 2
        self.bits, self.peers = [], []
        for even_step, odd_step in stages:
            ids = {}
            for axis, bit, here in ((*even_step, odd == 0), (*odd_step, odd == 1)):
                index = ids.get(axis, lax.axis_index(axis))
                ids[axis] = jnp.where(here, partner(axis, bit), index)
            pick = lambda step: (lax.axis_index(step[0]) // step[1]) % 2
            self.bits.append(jnp.where(odd == 0, pick(even_step), pick(odd_step)))
            self.peers.append(ids)

    def start_row(self, c, k):
        row = c * self.unit
        for n in range(k):
            row = row + self.bits[n] * (self.unit >> (n + 1))
        return row

    def rows(self, start, size):
        return pl.ds(pl.multiple_of(start, PLANE_ROWS), size)

    def copy(self, slot, c, peer, source, target):
        return pltpu.make_async_remote_copy(
            src_ref=source,
            dst_ref=target,
            send_sem=self.send_sem.at[slot, c],
            recv_sem=self.recv_sem.at[slot, c],
            device_id=peer,
            device_id_type=pl.DeviceIdType.MESH,
        )

    def inward(self, k, c, source_ref, base):
        size = self.unit >> (k + 1)
        start = self.start_row(c, k) + (1 - self.bits[k]) * size - base
        target = self.inbox[k].at[self.rows(c * size, size)]
        return self.copy(k, c, self.peers[k], source_ref.at[self.rows(start, size)], target)

    def inward_wait(self, k, c):
        size = self.unit >> (k + 1)
        target = self.inbox[k].at[self.rows(c * size, size)]
        return self.copy(k, c, self.peers[k], target, target)

    def outward(self, k, c):
        size = self.unit >> (k + 1)
        block = self.out.at[self.rows(self.start_row(c, k + 1), size)]
        return self.copy(2 * len(self.stages) - 1 - k, c, self.peers[k], block, block)

    def at_source(self, c, act):
        base = 0
        for ref in self.sources:
            height = ref.shape[0]
            inside = (c * self.unit >= base) & (c * self.unit < base + height)
            pl.when(inside)(functools.partial(act, ref, base))
            base += height

    def stage(self, slot, c):
        total = len(self.stages)
        if slot == 0:
            self.at_source(c, lambda ref, base: self.inward(0, c, ref, base).start())
        elif slot <= total:
            k = slot - 1
            size = self.unit >> slot
            got = self.inbox[k].at[self.rows(c * size, size)]
            self.inward_wait(k, c).wait_recv()
            last = slot == total
            kept = self.out if last else self.inbox[k]
            place = self.rows(self.start_row(c, slot), size)
            where = place if last else self.rows(c * size, size)
            if k == 0:

                def add(ref, base):
                    mine = ref[self.rows(self.start_row(c, 1) - base, size), :]
                    kept[where, :] = (mine.astype(F32) + got[...].astype(F32)).astype(BF16)

                self.at_source(c, add)
            else:
                before = c * (2 * size) + self.bits[k] * size
                mine = self.inbox[k - 1][self.rows(before, size), :]
                kept[where, :] = (mine.astype(F32) + got[...].astype(F32)).astype(BF16)
            if last:
                self.outward(total - 1, c).start()
            else:
                base = self.start_row(c, slot) - c * size
                self.inward(slot, c, kept, base).start()
        else:
            k = 2 * total - slot
            self.outward(k, c).wait_recv()
            if k > 0:
                self.outward(k - 1, c).start()

    def steps(self):
        return self.count + PLANE_SKEW * 2 * len(self.stages)

    def step(self, s):
        for slot in range(2 * len(self.stages) + 1):
            c = s - PLANE_SKEW * slot
            pl.when((c >= 0) & (c < self.count))(functools.partial(self.stage, slot, c))

    def drain(self):
        def one(c, carry):
            for k in range(len(self.stages)):
                self.inward_wait(k, c).wait_send()
                self.outward(k, c).wait_send()
            return carry

        lax.fori_loop(0, self.count, one, 0)


def line_kernel(
    size,
    chunk,
    returns,
    owners,
    pairs,
    stages,
    source_count,
    side_count,
    out_count,
    far_count,
    *refs,
):
    streams = len(returns)
    returned = [k for k in range(streams) if returns[k]]
    parts, refs = refs[:streams], refs[streams:]
    sides, refs = refs[:side_count], refs[side_count:]
    shared, refs = dict(zip(returned, refs)), refs[len(returned) :]
    kept, refs = refs[:out_count], refs[out_count:]
    inbox, send_up, recv_up, send_back, recv_back = refs[:5]
    far, near, far_sems = sides[:far_count], refs[-1 - far_count : -1], refs[-1]
    refs = refs[: -1 - far_count]
    sides = sides[far_count:]
    plane = None
    if source_count:
        plane_inbox, plane_send, plane_recv = refs[9 : 9 + len(stages)], *refs[9 + len(stages) :]
        plane = PlaneSum(
            stages, sides[:source_count], kept[1], plane_inbox, plane_send, plane_recv
        )
        sides = sides[source_count:]
    sides = [*near, *sides]
    half = parts[0].shape[0] // 2
    count = half // chunk
    last = size - 1
    me = lax.axis_index("tensor")
    above, below = jnp.minimum(me + 1, last), jnp.maximum(me - 1, 0)
    flows = ((me, above, below), (last - me, below, above))

    def fetch(act):
        for n in range(far_count):
            for owner, start in ((last, 0), (0, half)):
                rows = pl.ds(start if far[n].shape[0] > half else 0, half)
                copy = pltpu.make_async_copy(far[n].at[rows], near[n], far_sems.at[n])
                pl.when(me == owner)(functools.partial(act, copy))

    fetch(lambda copy: copy.start())

    barrier = pltpu.get_barrier_semaphore()

    def greet(axis, other):
        pl.semaphore_signal(
            barrier, inc=1, device_id={axis: other}, device_id_type=pl.DeviceIdType.MESH
        )

    if pairs:
        for axis, bit in pairs:
            greet(axis, partner(axis, bit))
        far_above = jnp.where(me % 2 == 0, 0, 1) * jnp.where(me < last, 1, 0)
        far_below = jnp.where(me % 2 == 0, 1, 0) * jnp.where(me > 0, 1, 0)
        pl.when(far_above == 1)(lambda: greet("tensor", above))
        pl.when(far_below == 1)(lambda: greet("tensor", below))
        pl.semaphore_wait(barrier, len(pairs) + far_above + far_below)
    else:
        pl.when(me < last)(lambda: greet("tensor", above))
        pl.when(me > 0)(lambda: greet("tensor", below))
        pl.semaphore_wait(barrier, jnp.where((me > 0) & (me < last), 2, 1))

    def place(f, i):
        return pl.ds(pl.multiple_of(f * half + i * chunk, chunk), chunk)

    def local(i):
        return pl.ds(pl.multiple_of(i * chunk, chunk), chunk)

    def onward(k, f, i, source):
        return pltpu.make_async_remote_copy(
            src_ref=source,
            dst_ref=inbox.at[k, f, local(i)],
            send_sem=send_up.at[k, f, i],
            recv_sem=recv_up.at[k, f, i],
            device_id={"tensor": flows[f][1]},
            device_id_type=pl.DeviceIdType.MESH,
        )

    def backward(k, f, i):
        block = shared[k].at[place(f, i)]
        return pltpu.make_async_remote_copy(
            src_ref=block,
            dst_ref=block,
            send_sem=send_back.at[k, f, i],
            recv_sem=recv_back.at[k, f, i],
            device_id={"tensor": flows[f][2]},
            device_id_type=pl.DeviceIdType.MESH,
        )

    def reduce_chunk(k, f, i):
        position = flows[f][0]
        mine = parts[k].at[place(f, i)]
        slot = inbox.at[k, f, local(i)]

        @pl.when(position == 0)
        def _():
            pl.when(i >= LINE_WINDOW)(lambda: onward(k, f, i - LINE_WINDOW, mine).wait_send())
            onward(k, f, i, mine).start()

        @pl.when(position > 0)
        def _():
            onward(k, f, i, slot).wait_recv()
            total = slot[...].astype(F32) + mine[...].astype(F32)

            @pl.when(position < last)
            def _():
                slot[...] = total.astype(BF16)
                onward(k, f, i, slot).start()

            @pl.when(position == last)
            def _():
                result = owners[k](total, local(i), sides, kept)
                if returns[k]:
                    shared[k][place(f, i), :] = result.astype(BF16)
                    backward(k, f, i).start()

    def pass_back(k, f, i):
        position = flows[f][0]

        @pl.when((position < last) & (i >= 0) & (i < count))
        def _():
            backward(k, f, i).wait_recv()
            pl.when(position > 0)(lambda: backward(k, f, i).start())

    def step(s, carry):
        pl.when(s == LINE_SKEW * last)(lambda: fetch(lambda copy: copy.wait()))
        for k in range(streams):
            for f in range(2):
                i = s - LINE_SKEW * flows[f][0]
                pl.when((i >= 0) & (i < count))(lambda: reduce_chunk(k, f, i))
        for k in returned:
            for f in range(2):
                pass_back(k, f, s - LINE_SKEW * (2 * last - flows[f][0]))
        if plane:
            plane.step(s)
        for n in range(len(pairs) + 1 if pairs else 0):
            pl.when(s == n * gap)(lambda: advance_gains(n))
        return carry

    steps = count + 2 * LINE_SKEW * last
    if plane:
        steps = max(steps, plane.steps())
    gap = steps // (len(pairs) + 1)
    if pairs:
        slots, sums, send_pair, recv_pair = refs[5:9]
        sums[0] = sides[-1][...]
    elif len(kept) > 1:
        kept[1][...] = jnp.zeros_like(kept[1])

    def swap_gains(n):
        return pltpu.make_async_remote_copy(
            src_ref=sums.at[n],
            dst_ref=slots.at[n],
            send_sem=send_pair.at[n],
            recv_sem=recv_pair.at[n],
            device_id={pairs[n][0]: partner(*pairs[n])},
            device_id_type=pl.DeviceIdType.MESH,
        )

    def advance_gains(n):
        if n > 0:
            swap_gains(n - 1).wait()
            sums[n] = sums[n - 1] + slots[n - 1]
        if n < len(pairs):
            swap_gains(n).start()
        else:
            kept[0][...] = sums[n]

    lax.fori_loop(0, steps, step, 0)

    def drain(i, carry):
        for k in range(streams):
            for f in range(2):
                position = flows[f][0]
                waited = (position == 0) & (i < count - LINE_WINDOW)
                pl.when((position < last) & ~waited)(
                    lambda: onward(k, f, i, inbox.at[k, f, local(i)]).wait_send()
                )
                if returns[k]:
                    pl.when(position > 0)(lambda: backward(k, f, i).wait_send())
        return carry

    lax.fori_loop(0, count, drain, 0)
    if plane:
        plane.drain()


def line_sum(
    parts, owners, far, sides, kept, collective_id, returns=(True,), pairs=(), stages=(), sources=()
):
    rows, width = parts[0].shape
    size = lax.axis_size("tensor")
    streams = len(parts)
    chunk = max(16, min(LINE_CHUNK, rows // 32))
    count = rows // 2 // chunk
    whole = pl.BlockSpec(memory_space=pltpu.VMEM)
    scalar = pl.BlockSpec(memory_space=pltpu.SMEM)
    sems = pltpu.SemaphoreType.DMA((streams, 2, count))
    outs = [jax.ShapeDtypeStruct((rows, width), BF16)] * sum(returns) + list(kept)
    extra = []
    if pairs:
        pair_sems = pltpu.SemaphoreType.DMA((len(pairs),))
        extra = [
            pltpu.VMEM((len(pairs), 8, width), F32),
            pltpu.VMEM((len(pairs) + 1, 8, width), F32),
            pair_sems,
            pair_sems,
        ]
    if sources:
        plane_rows = sum(source.shape[0] for source in sources)
        unit = 2 ** len(stages) * PLANE_ROWS
        kept = [*kept, jax.ShapeDtypeStruct((plane_rows, width), BF16)]
        outs.append(kept[-1])
        extra += [pltpu.VMEM((plane_rows >> (k + 1), width), BF16) for k in range(len(stages))]
        extra += [pltpu.SemaphoreType.DMA((2 * len(stages), plane_rows // unit))] * 2
        sides = [*sources, *sides]
    extra += [pltpu.VMEM((rows // 2, width), array.dtype) for array in far]
    extra.append(pltpu.SemaphoreType.DMA((max(len(far), 1),)))
    return pl.pallas_call(
        functools.partial(
            line_kernel,
            size,
            chunk,
            returns,
            owners,
            pairs,
            stages,
            len(sources),
            len(far) + len(sides),
            len(kept),
            len(far),
        ),
        out_shape=outs,
        in_specs=[whole] * streams
        + [pl.BlockSpec(memory_space=pl.ANY)] * len(far)
        + [scalar if s.ndim == 1 else whole for s in sides],
        out_specs=[whole] * len(outs),
        scratch_shapes=[pltpu.VMEM((streams, 2, rows // 2, width), BF16)] + [sems] * 4 + extra,
        compiler_params=pltpu.CompilerParams(
            collective_id=collective_id, has_side_effects=True, vmem_limit_bytes=56 * 2**20
        ),
        cost_estimate=pl.CostEstimate(
            flops=streams * rows * width,
            bytes_accessed=streams * 300 * 2**20,
            transcendentals=0,
        ),
    )(*parts, *far, *sides)


def unit_of(rows):
    inverse = lax.rsqrt(jnp.mean(rows * rows, axis=-1, keepdims=True) + EPSILON)
    return rows * inverse, inverse


def own_hidden(total, here, sides, kept):
    x_ref, gain_ref = sides
    hidden = x_ref[here, :].astype(F32) + total
    kept[0][here, :] = hidden
    return unit_of(hidden)[0] * gain_ref[...]


def own_dhidden(total, here, sides, kept):
    x_ref, hidden_ref, cot_ref, gain_ref, factor = sides
    unit, inverse = unit_of(hidden_ref[here, :])
    kept[1][...] += jnp.sum(total * unit, axis=0, keepdims=True)
    dhidden = norm_back(total, unit, inverse, gain_ref[...])
    kept[0][here, :] = dhidden
    return cot_ref[here, :].astype(F32) * factor[0] + dhidden


def own_output(total, here, sides, kept):
    x_ref, hidden_ref, cot_ref, gain_ref, factor = sides
    x = x_ref[here, :].astype(F32)
    result = x + factor[1] * ((hidden_ref[here, :] - x) + total)
    kept[2][here, :] = result.astype(BF16)


def own_dinput(total, here, sides, kept):
    x_ref, dhidden_ref, gain_ref, _ = sides
    unit, inverse = unit_of(x_ref[here, :].astype(F32))
    return dhidden_ref[here, :] + norm_back(total, unit, inverse, gain_ref[...])


def cut_half(own):
    step = own.shape[0] // SPREAD_PIECES
    return [[own[p * step : (p + 1) * step]] for p in range(SPREAD_PIECES)]


def send_wave(pieces, wave):
    size = lax.axis_size("tensor")
    for p, hops in enumerate(pieces):
        h = wave - p
        if 0 <= h < size - 1:
            perm = [(size - 1 - h, size - 2 - h), (h, h + 1)]
            hops.append(lax.ppermute(hops[-1], "tensor", perm))


def tie(pieces, others):
    heads, others = lax.optimization_barrier(([hops[-1] for hops in pieces], others))
    for hops, head in zip(pieces, heads):
        hops[-1] = head
    return others


def join_kernel(size, *refs):
    pieces, out = refs[:-1], refs[-1]
    me = lax.axis_index("tensor")
    step = pieces[0].shape[0]
    half = out.shape[0] // 2
    for p in range(SPREAD_PIECES):
        for h in range(size):
            for f, wanted in enumerate((size - 1 - me, me)):

                @pl.when(wanted == h)
                def _():
                    out[pl.ds(f * half + p * step, step), :] = pieces[p * size + h][...]


def join_halves(pieces):
    size = lax.axis_size("tensor")
    step, width = pieces[0].shape
    whole = pl.BlockSpec(memory_space=pltpu.VMEM)
    return pl.pallas_call(
        functools.partial(join_kernel, size),
        out_shape=jax.ShapeDtypeStruct((2 * SPREAD_PIECES * step, width), BF16),
        in_specs=[whole] * len(pieces),
        out_specs=whole,
        compiler_params=pltpu.CompilerParams(vmem_limit_bytes=40 * 2**20),
    )(*pieces)


def rotary_tables(positions):
    inverse = 1.0 / 10000.0 ** (jnp.arange(0, HEAD_DIM, 2, dtype=F32) / HEAD_DIM)
    angle = positions.astype(F32)[:, None] * inverse[None, :]
    return (jnp.cos(angle), jnp.sin(angle))


def contract_rows(left, right):
    return jnp.einsum("rd,rf->df", left, right, preferred_element_type=F32)


def contract_cols(left, right):
    return jnp.einsum("rc,dc->rd", left, right, preferred_element_type=F32)


def norm_back(dnormed, unit, inverse, gain):
    scaled = dnormed * gain
    return inverse * (scaled - unit * jnp.mean(scaled * unit, axis=-1, keepdims=True))


def flags_kernel(size, mine, everyone, send_sem, recv_sem):
    me = lax.axis_index("dp")
    barrier = pltpu.get_barrier_semaphore()
    others = [lax.rem(me + s, size) for s in range(1, size)]
    for other in others:
        pl.semaphore_signal(
            barrier, inc=1, device_id={"dp": other}, device_id_type=pl.DeviceIdType.MESH
        )
    pl.semaphore_wait(barrier, size - 1)

    def send(s, slot):
        return pltpu.make_async_remote_copy(
            src_ref=mine,
            dst_ref=everyone.at[slot],
            send_sem=send_sem.at[s],
            recv_sem=recv_sem.at[s],
            device_id={"dp": others[s]},
            device_id_type=pl.DeviceIdType.MESH,
        )

    for s in range(size - 1):
        send(s, me).start()
    everyone[me] = mine[...]
    for s in range(size - 1):
        send(s, me).wait_send()
        send(s, lax.rem(me + 2 * size - 1 - s, size)).wait_recv()


def share_flags(row):
    size = lax.axis_size("dp")
    tile = jnp.zeros((8, 128), jnp.int32).at[0, : row.shape[0]].set(row)
    sems = pltpu.SemaphoreType.DMA((size - 1,))
    whole = pl.BlockSpec(memory_space=pltpu.VMEM)
    shared = pl.pallas_call(
        functools.partial(flags_kernel, size),
        out_shape=jax.ShapeDtypeStruct((size, 8, 128), jnp.int32),
        in_specs=[whole],
        out_specs=whole,
        scratch_shapes=[sems, sems],
        compiler_params=pltpu.CompilerParams(collective_id=1, has_side_effects=True),
    )(tile)
    return shared[:, 0, : row.shape[0]]


def shift_ctx(part, s):
    size = lax.axis_size("ctx")
    return lax.ppermute(part, "ctx", [(i, (i + s) % size) for i in range(size)])


def swap_core(part):
    return lax.ppermute(part, "dp", [(i, i ^ 1) for i in range(lax.axis_size("dp"))])


def gather_parts(own, paired):
    parts = []
    for s in range(lax.axis_size("ctx")):
        here = own if s == 0 else shift_ctx(own, s)
        parts += [here, swap_core(here)] if paired else [here]
    return parts


def collect_parts(parts, paired):
    terms = [parts[0]]
    if paired:
        terms.append(swap_core(parts[1]))
    per = 2 if paired else 1
    for s in range(1, lax.axis_size("ctx")):
        near = parts[per * s]
        if paired:
            near = (near.astype(F32) + swap_core(parts[per * s + 1]).astype(F32)).astype(BF16)
        terms.append(shift_ctx(near, -s))
    return terms


def block_pass(
    paired,
    first_id,
    span,
    x_low,
    cot_low,
    keep,
    scale,
    order_row,
    attn_gain,
    ffn_gain,
    w_query,
    w_key,
    w_value,
    w_output,
    w_gate,
    w_up,
    w_down,
):
    rows, width = x_low.shape
    dp_size, ctx_size = lax.axis_size("dp"), lax.axis_size("ctx")
    spans = order_row.shape[0]
    ctx = lax.axis_index("ctx")
    core = lax.axis_index("dp") % 2
    per_part = rows // span
    places = []
    for s in range(ctx_size):
        group = (ctx + ctx_size - s) % ctx_size
        places += [group * 2 + core, group * 2 + 1 - core] if paired else [group]
    spread = jnp.arange(per_part, dtype=jnp.int32)
    places = jnp.concatenate([place * per_part + spread for place in places])
    chosen = places[:, None] == jnp.arange(spans, dtype=jnp.int32)[None, :]
    key_order = jnp.sum(jnp.where(chosen, order_row[None, :], 0), axis=1)
    query_order = key_order[:per_part]
    row_index = jnp.arange(rows, dtype=jnp.int32)
    starts = jnp.sum(
        jnp.where(
            (row_index // span)[:, None] == jnp.arange(per_part, dtype=jnp.int32)[None, :],
            query_order[None, :],
            0,
        ),
        axis=1,
    )
    cosine, sine = rotary_tables(starts * span + row_index % span)

    wide_cosine = jnp.concatenate([cosine, cosine], axis=1)
    wide_sine = jnp.concatenate([-sine, sine], axis=1)
    attn_row, ffn_row = attn_gain[None, :], ffn_gain[None, :]
    normed_one, queries, kv_own = project(
        x_low, attn_row, wide_cosine, wide_sine, w_query, w_key, w_value
    )
    kv_parts = gather_parts(kv_own, paired)
    dffn = (cot_low.astype(F32) * (keep * scale)).astype(BF16)
    dacted = contract_cols(dffn, w_down)
    queries, dacted = lax.optimization_barrier((queries, dacted))
    mixed, logs = attend(queries, kv_parts, query_order, key_order, span)

    half_rows = jax.ShapeDtypeStruct((rows // 2, width), F32)
    gain_row = jax.ShapeDtypeStruct((1, width), F32)
    attn_part = nn_dot(mixed, w_output).astype(BF16)
    normed_two, hidden = line_sum(
        [attn_part], [own_hidden], [x_low], [ffn_row], [half_rows], first_id
    )

    factors = jnp.stack([keep * scale, keep])
    acted, dgate, dupward = hidden_units(normed_two, dacted, w_gate, w_up)
    early_grads = [
        contract_rows(acted, dffn).astype(BF16),
        contract_rows(normed_two, dgate).astype(BF16),
        contract_rows(normed_two, dupward).astype(BF16),
    ]
    late_grads = [early_grads.pop()] if paired else []
    acted, dgate, dupward, early_grads, late_grads = lax.optimization_barrier(
        (acted, dgate, dupward, early_grads, late_grads)
    )
    early_grads = lax.psum(early_grads, ("dp", "ctx"))
    dnormed_part, ffn_part = width_parts(acted, dgate, dupward, w_gate, w_up, w_down)
    dattn, dhidden, ffn_gain_part, output_half = line_sum(
        [dnormed_part, ffn_part],
        [own_dhidden, own_output],
        [x_low, hidden, cot_low],
        [ffn_row, factors],
        [half_rows, gain_row, jax.ShapeDtypeStruct((rows // 2, width), BF16)],
        first_id + 1,
        (True, False),
    )
    pieces = cut_half(output_half)
    send_wave(pieces, 0)
    dmixed = contract_cols(dattn, w_output).astype(BF16)
    dq_proj, *dkv_parts = attend_back(
        queries, dmixed, mixed, logs, cosine, sine, kv_parts, query_order, key_order, span
    )
    dq_proj, dkv_parts = tie(pieces, (dq_proj, dkv_parts))
    send_wave(pieces, 1)
    terms = collect_parts(dkv_parts, paired)
    grad_query = contract_rows(dq_proj, normed_one).astype(BF16)
    grad_output = contract_rows(mixed, dattn).astype(BF16)
    grad_query, grad_output = tie(pieces, (grad_query, grad_output))
    send_wave(pieces, 2)
    if not paired:
        early_grads = [g.astype(F32) for g in early_grads]
        terms, early_grads = lax.optimization_barrier((terms, early_grads))
    terms, grad_query, grad_output = lax.optimization_barrier((terms, grad_query, grad_output))
    dkv_proj, dnormed_one, attn_gain_part = project_back(
        x_low, dq_proj, terms, wide_cosine, wide_sine, w_query, w_key, w_value
    )
    gain_parts = jnp.concatenate(
        [attn_gain_part, ffn_gain_part, jnp.zeros((6, width), F32)], axis=0
    )
    grad_kv = contract_rows(dkv_proj, normed_one).astype(BF16)
    dnormed_one, early_grads, late_grads = tie(pieces, (dnormed_one, early_grads, late_grads))
    if paired:
        late_grads = lax.psum(late_grads, ("ctx", "dp"))
        early_grads = [g.astype(F32) for g in early_grads]
        dnormed_one, early_grads = lax.optimization_barrier((dnormed_one, early_grads))
    for wave in range(3, lax.axis_size("tensor") + SPREAD_PIECES):
        send_wave(pieces, wave)
    through, gains, attn_grads = line_sum(
        [dnormed_one],
        [own_dinput],
        [x_low, dhidden],
        [attn_row, gain_parts],
        [jax.ShapeDtypeStruct((8, width), F32)],
        first_id + 2,
        (True,),
        tuple(pair_steps((dp_size, ctx_size, lax.axis_size("tensor")))),
        plane_steps(dp_size, ctx_size),
        [grad_query, grad_kv, grad_output],
    )
    through, gains, attn_grads, early_grads, late_grads, pieces = lax.optimization_barrier(
        (through, gains, attn_grads, early_grads, late_grads, pieces)
    )
    output = join_halves([hop for hops in pieces for hop in hops])
    grads = (attn_grads, *early_grads, *late_grads)
    return output, through, gains, grads


def per_device(
    inputs,
    cotangent,
    skip_mask,
    group_ids,
    span_order,
    exit_scale,
    attn_gain,
    ffn_gain,
    *weights,
):
    _, rows, width = inputs.shape
    spans = span_order.shape[1]
    own_spans = spans // lax.axis_size("ctx")
    span = rows // own_spans
    me = lax.axis_index("dp")
    core = me % 2
    x_low, cot_low = inputs[0], cotangent[0]
    flags = share_flags(jnp.concatenate([skip_mask, group_ids, span_order[0]]))
    runs, groups = flags[:, 0], flags[:, 1]
    scale_of = lambda group: jnp.where(group == 1, exit_scale[1], exit_scale[0])
    own_run, own_scale = skip_mask[0], scale_of(group_ids[0])
    gains = (attn_gain, ffn_gain)

    def alone():
        return block_pass(
            False,
            2,
            span,
            x_low,
            cot_low,
            own_run.astype(F32),
            own_scale,
            span_order[0],
            *gains,
            *weights,
        )

    def shared():
        half = rows // 2
        other = me + 1 - 2 * core
        take = lambda a, i: lax.dynamic_slice_in_dim(a, i * half, half, 0)
        pick = lambda a: lax.dynamic_index_in_dim(a, other, 0, keepdims=False)
        other_run = pick(runs)
        use_own = (own_run == 1) | ((other_run == 0) & (core == 0))
        choose = lambda mine, theirs: jnp.where(use_own, mine, theirs)
        work = lambda a: choose(take(a, core), swap_core(take(a, 1 - core)))
        output, through, *rest = block_pass(
            True,
            5,
            span,
            work(x_low),
            work(cot_low),
            choose(own_run, other_run).astype(F32),
            choose(own_scale, scale_of(pick(groups))),
            choose(span_order[0], pick(flags[:, 2:])),
            *gains,
            *weights,
        )

        def whole(part):
            theirs = swap_core(part)
            first, second = jnp.where(core == 0, part, theirs), jnp.where(core == 0, theirs, part)
            return jnp.concatenate([first, second], 0)

        through = jnp.where(own_run == 1, whole(through), 0)
        return whole(output), through, *rest

    def finish(output, through, sums, grads):
        output = jnp.where(own_run == 1, output, x_low)
        input_grad = cot_low.astype(F32) * own_scale + through.astype(F32)
        attn_grads = unpack(grads[0], *[w.shape[1] for w in weights[:3]])
        grads = [g.astype(F32) for g in grads[1:]]
        return lax.optimization_barrier(
            (output, input_grad, sums[0], sums[1], *attn_grads, *grads)
        )

    if own_spans % 2 == 0 and lax.axis_size("dp") % 2 == 0:
        pairs = runs.reshape(-1, 2)
        results = lax.cond(
            jnp.all(pairs[:, 0] * pairs[:, 1] == 0),
            lambda: finish(*shared()),
            lambda: finish(*alone()),
        )
    else:
        results = finish(*alone())
    output, input_grad, grad_attn_gain, grad_ffn_gain = results[:4]
    grad_query, grad_key, grad_value, grad_output, grad_down, grad_gate, grad_up = results[4:]
    return (
        output.reshape(inputs.shape),
        input_grad.reshape(inputs.shape),
        grad_attn_gain,
        grad_ffn_gain,
        grad_query,
        grad_key,
        grad_value,
        grad_output,
        grad_gate,
        grad_up,
        grad_down,
    )


def solution(mesh):
    rows = P("dp", "ctx", None)
    by_column, by_row = P(None, "tensor"), P("tensor", None)
    in_specs = (rows, rows, P("dp"), P("dp"), P("dp", None), P(), P(), P())
    in_specs += (by_column,) * 3 + (by_row,) + (by_column,) * 2 + (by_row,)
    out_specs = (rows, rows, P(), P()) + (by_column,) * 3 + (by_row,) + (by_column,) * 2 + (by_row,)
    return jax.shard_map(
        per_device, mesh=mesh, in_specs=in_specs, out_specs=out_specs, check_vma=False
    )
```

```python
import functools

import jax
import jax.numpy as jnp
from jax import lax
from jax.experimental import pallas as pl
from jax.experimental.pallas import tpu as pltpu
from jax.sharding import PartitionSpec as P

HEAD_DIM = 128
EPSILON = 1e-05
NEG_BIG = -1e30
FACTOR = HEAD_DIM ** (-0.5)
LOG2E = 1.4426950408889634
QUERY_BLOCK = 256
BF16 = jnp.bfloat16
F32 = jnp.float32

NT = (((1,), (1,)), ((), ()))


def nt_dot(left, right):
    return lax.dot_general(left, right, NT, preferred_element_type=F32)


def nn_dot(left, right):
    return jnp.dot(left, right, preferred_element_type=F32)


def stack_heads(block, group):
    return jnp.concatenate(
        [block[:, h * HEAD_DIM : (h + 1) * HEAD_DIM] for h in range(group)], axis=0
    )


def hide_later(scores, first_row, rows, fill):
    key_row = lax.broadcasted_iota(jnp.int32, scores.shape, 0)
    query_row = lax.broadcasted_iota(jnp.int32, scores.shape, 1) % rows + first_row
    return jnp.where(key_row <= query_row, scores, fill)


def over_spans(kv_refs, span, visit, query_order, key_order, first):
    order = query_order[first // span]
    seen = 0
    for part, kv_ref in enumerate(kv_refs):
        count = kv_ref.shape[1] // span

        def one_span(j, carry, part=part, seen=seen):
            place = pl.multiple_of(j * span, span)
            column = pl.multiple_of((seen + j) * span, span)
            pl.when(key_order[seen + j] < order)(lambda: visit(part, place, column, False))
            pl.when(key_order[seen + j] == order)(lambda: visit(part, place, column, True))
            return carry

        lax.fori_loop(0, count, one_span, 0)
        seen += count


def attend_kernel(group, span, parts, query_order, key_order, q_ref, *refs):
    kv_refs, (o_ref, lse_ref, vt_ref, top, total, acc) = refs[:parts], refs[parts:]
    rows = q_ref.shape[0]
    step = pl.program_id(1)
    first = step * rows

    @pl.when(step == 0)
    def _():
        for part, kv_ref in enumerate(kv_refs):
            size = kv_ref.shape[1]
            vt_ref[:, part * size : (part + 1) * size] = kv_ref[1].T

    queries = stack_heads(q_ref[...], group)
    top[...] = jnp.full_like(top, NEG_BIG)
    total[...] = jnp.zeros_like(total)
    acc[...] = jnp.zeros_like(acc)

    def visit(part, place, column, diagonal):
        keys = kv_refs[part][0, pl.ds(place, span), :]
        scores = nt_dot(keys, queries) * (FACTOR * LOG2E)
        if diagonal:
            scores = hide_later(scores, first % span, rows, NEG_BIG)
        before = top[...]
        now = jnp.maximum(before, jnp.max(scores, axis=0, keepdims=True))
        weights = jnp.exp2(scores - now)
        shrink = jnp.exp2(before - now)
        top[...] = now
        total[...] = total[...] * shrink + jnp.sum(weights, axis=0, keepdims=True)
        acc[...] = acc[...] * shrink + nn_dot(
            vt_ref[:, pl.ds(column, span)], weights.astype(BF16)
        )

    over_spans(kv_refs, span, visit, query_order, key_order, first)
    mixed = acc[...] / total[...]
    logs = top[...] + jnp.log2(total[...])
    for h in range(group):
        part = slice(h * rows, (h + 1) * rows)
        o_ref[:, h * HEAD_DIM : (h + 1) * HEAD_DIM] = mixed[:, part].T.astype(BF16)
        lse_ref[0, h : h + 1, :] = logs[:, part]


def attend(queries, kv_parts, query_order, key_order, span):
    rows, width = queries.shape
    part_rows, kv_width = kv_parts[0].shape[1:]
    full = part_rows * len(kv_parts)
    kv_heads = kv_width // HEAD_DIM
    group = width // kv_width
    block = min(QUERY_BLOCK, span)
    query_spec = pl.BlockSpec((block, group * HEAD_DIM), lambda g, i, *_: (i, g))
    kv_spec = pl.BlockSpec((2, part_rows, HEAD_DIM), lambda g, i, *_: (0, 0, g))
    return pl.pallas_call(
        functools.partial(attend_kernel, group, span, len(kv_parts)),
        grid_spec=pltpu.PrefetchScalarGridSpec(
            num_scalar_prefetch=2,
            grid=(kv_heads, rows // block),
            in_specs=[query_spec] + [kv_spec] * len(kv_parts),
            out_specs=[
                query_spec,
                pl.BlockSpec((1, group, block), lambda g, i, *_: (g, 0, i)),
            ],
            scratch_shapes=[
                pltpu.VMEM((HEAD_DIM, full), BF16),
                pltpu.VMEM((1, group * block), F32),
                pltpu.VMEM((1, group * block), F32),
                pltpu.VMEM((HEAD_DIM, group * block), F32),
            ],
        ),
        out_shape=[
            jax.ShapeDtypeStruct((rows, width), BF16),
            jax.ShapeDtypeStruct((kv_heads, group, rows), F32),
        ],
        compiler_params=pltpu.CompilerParams(vmem_limit_bytes=32 * 2**20),
        cost_estimate=pl.CostEstimate(
            flops=4 * rows * full * width,
            bytes_accessed=4 * rows * width + 4 * full * kv_width,
            transcendentals=rows * full * width // HEAD_DIM,
        ),
    )(query_order, key_order, queries, *kv_parts)


def attend_back_kernel(
    group,
    span,
    parts,
    query_order,
    key_order,
    q_ref,
    do_ref,
    o_ref,
    lse_ref,
    cos_ref,
    sin_ref,
    *refs,
):
    kv_refs, dq_ref, dkv_refs = refs[:parts], refs[parts], refs[parts + 1 : 2 * parts + 1]
    kt_ref, acc, sums = refs[2 * parts + 1 :]
    rows = q_ref.shape[0]
    step = pl.program_id(1)
    first = step * rows
    queries = stack_heads(q_ref[...], group)
    dmixed = stack_heads(do_ref[...], group)
    mixed = stack_heads(o_ref[...], group)
    product = dmixed.astype(F32) * mixed.astype(F32)
    delta = jnp.sum(product.T, axis=0, keepdims=True)
    logs = jnp.concatenate([lse_ref[0, h : h + 1, :] for h in range(group)], axis=1)
    acc[...] = jnp.zeros_like(acc)

    @pl.when(step == 0)
    def _():
        sums[...] = jnp.zeros_like(sums)
        for part, kv_ref in enumerate(kv_refs):
            size = kv_ref.shape[1]
            kt_ref[:, part * size : (part + 1) * size] = kv_ref[0].T

    def visit(part, place, column, diagonal):
        here = pl.ds(place, span)
        scores = nt_dot(kv_refs[part][0, here, :], queries) * (FACTOR * LOG2E)
        probs = jnp.exp2(scores - logs)
        if diagonal:
            probs = hide_later(probs, first % span, rows, 0.0)
        dprobs = nt_dot(kv_refs[part][1, here, :], dmixed)
        dscore = (probs * (dprobs - delta)).astype(BF16)
        sums[part, 1, here, :] += nn_dot(probs.astype(BF16), dmixed)
        sums[part, 0, here, :] += nn_dot(dscore, queries)
        acc[...] += nn_dot(kt_ref[:, pl.ds(column, span)], dscore)

    over_spans(kv_refs, span, visit, query_order, key_order, first)
    for h in range(group):
        grad = acc[:, h * rows : (h + 1) * rows] * FACTOR
        half = HEAD_DIM // 2
        leading, trailing = grad[:half], grad[half:]
        cosine, sine = cos_ref[...], sin_ref[...]
        turned = jnp.concatenate(
            [leading * cosine + trailing * sine, trailing * cosine - leading * sine], axis=0
        )
        dq_ref[:, h * HEAD_DIM : (h + 1) * HEAD_DIM] = turned.T.astype(BF16)

    @pl.when(step == pl.num_programs(1) - 1)
    def _():
        for part, dkv_ref in enumerate(dkv_refs):
            dkv_ref[0] = (sums[part, 0] * FACTOR).astype(dkv_ref.dtype)
            dkv_ref[1] = sums[part, 1].astype(dkv_ref.dtype)


def attend_back(
    queries, dmixed, mixed, logs, cosine, sine, kv_parts, query_order, key_order, span
):
    rows, width = queries.shape
    part_rows, kv_width = kv_parts[0].shape[1:]
    parts = len(kv_parts)
    full = part_rows * parts
    kv_heads = kv_width // HEAD_DIM
    group = width // kv_width
    block = min(QUERY_BLOCK, span)
    half = HEAD_DIM // 2
    query_spec = pl.BlockSpec((block, group * HEAD_DIM), lambda g, i, *_: (i, g))
    kv_spec = pl.BlockSpec((2, part_rows, HEAD_DIM), lambda g, i, *_: (0, 0, g))
    table_spec = pl.BlockSpec((half, block), lambda g, i, *_: (0, i))
    kinds = [F32] + [BF16] * (parts - 1)
    return pl.pallas_call(
        functools.partial(attend_back_kernel, group, span, parts),
        grid_spec=pltpu.PrefetchScalarGridSpec(
            num_scalar_prefetch=2,
            grid=(kv_heads, rows // block),
            in_specs=[
                query_spec,
                query_spec,
                query_spec,
                pl.BlockSpec((1, group, block), lambda g, i, *_: (g, 0, i)),
                table_spec,
                table_spec,
            ]
            + [kv_spec] * parts,
            out_specs=[query_spec] + [kv_spec] * parts,
            scratch_shapes=[
                pltpu.VMEM((HEAD_DIM, full), BF16),
                pltpu.VMEM((HEAD_DIM, group * block), F32),
                pltpu.VMEM((parts, 2, part_rows, HEAD_DIM), F32),
            ],
        ),
        out_shape=[jax.ShapeDtypeStruct((rows, width), BF16)]
        + [jax.ShapeDtypeStruct((2, part_rows, kv_width), kind) for kind in kinds],
        compiler_params=pltpu.CompilerParams(vmem_limit_bytes=40 * 2**20),
        cost_estimate=pl.CostEstimate(
            flops=10 * rows * full * width,
            bytes_accessed=8 * rows * width + 14 * full * kv_width,
            transcendentals=rows * full * width // HEAD_DIM,
        ),
    )(
        query_order,
        key_order,
        queries,
        dmixed,
        mixed,
        logs,
        cosine.T,
        sine.T,
        *kv_parts,
    )


ROW_BLOCK = 256


def by_rows(block, width):
    return pl.BlockSpec((block, width), lambda i: (i, 0))


def held(array):
    return pl.BlockSpec(
        array.shape, lambda i: (0,) * array.ndim, pipeline_mode=pl.Buffered(1)
    )


def column_cuts(width, size=512):
    return [slice(c, min(c + size, width)) for c in range(0, width, size)]


def turn(field, cosine, sine):
    return field * cosine + pltpu.roll(field, HEAD_DIM // 2, 1) * sine


def project_kernel(x_ref, gain_ref, cos_ref, sin_ref, wq, wk, wv, n_ref, q_ref, kv_ref):
    unit, _ = unit_of(x_ref[...].astype(F32))
    normed = (unit * gain_ref[...]).astype(BF16)
    n_ref[...] = normed
    cosine, sine = cos_ref[...], sin_ref[...]
    queries, keys = nn_dot(normed, wq[...]), nn_dot(normed, wk[...])
    for h in range(q_ref.shape[1] // HEAD_DIM):
        head = slice(h * HEAD_DIM, (h + 1) * HEAD_DIM)
        q_ref[:, head] = turn(queries[:, head], cosine, sine).astype(BF16)
    for h in range(kv_ref.shape[2] // HEAD_DIM):
        head = slice(h * HEAD_DIM, (h + 1) * HEAD_DIM)
        kv_ref[0, :, head] = turn(keys[:, head], cosine, sine).astype(BF16)
    kv_ref[1] = nn_dot(normed, wv[...]).astype(BF16)


def project(x_low, gain_row, cosine, sine, w_query, w_key, w_value):
    rows, width = x_low.shape
    block = min(ROW_BLOCK, rows)
    heads_width, kv_width = w_query.shape[1], w_key.shape[1]
    return pl.pallas_call(
        project_kernel,
        grid=(rows // block,),
        in_specs=[
            by_rows(block, width),
            held(gain_row),
            by_rows(block, HEAD_DIM),
            by_rows(block, HEAD_DIM),
            held(w_query),
            held(w_key),
            held(w_value),
        ],
        out_specs=[
            by_rows(block, width),
            by_rows(block, heads_width),
            pl.BlockSpec((2, block, kv_width), lambda i: (0, i, 0)),
        ],
        out_shape=[
            jax.ShapeDtypeStruct((rows, width), BF16),
            jax.ShapeDtypeStruct((rows, heads_width), BF16),
            jax.ShapeDtypeStruct((2, rows, kv_width), BF16),
        ],
        compiler_params=pltpu.CompilerParams(vmem_limit_bytes=40 * 2**20),
        cost_estimate=pl.CostEstimate(
            flops=2 * rows * width * (heads_width + 2 * kv_width),
            bytes_accessed=6 * rows * width + 2 * width * (heads_width + 2 * kv_width),
            transcendentals=rows,
        ),
    )(x_low, gain_row, cosine, sine, w_query, w_key, w_value)


def stream_cuts(sources, targets, sems, cuts):
    first = pl.program_id(0) == 0

    def copies(n):
        out = []
        for w, (source, target, by_column) in enumerate(zip(sources, targets, cuts[1])):
            start, size = cuts[0][n].start, cuts[0][n].stop - cuts[0][n].start
            place = (slice(None), pl.ds(start, size)) if by_column else (pl.ds(start, size),)
            out.append(
                pltpu.make_async_copy(source.at[place], target.at[place], sems.at[w, n])
            )
        return out

    @pl.when(first)
    def _():
        for n in range(len(cuts[0])):
            for copy in copies(n):
                copy.start()

    def ready(n):
        @pl.when(first)
        def _():
            for copy in copies(n):
                copy.wait()

    return ready


def hidden_kernel(n_ref, da_ref, wg_ref, wu_ref, a_ref, dg_ref, du_ref, wg, wu, sems):
    cuts = column_cuts(a_ref.shape[1])
    ready = stream_cuts((wg_ref, wu_ref), (wg, wu), sems, (cuts, (True, True)))
    normed = n_ref[...]
    for n, cut in enumerate(cuts):
        ready(n)
        gate, upward = nn_dot(normed, wg[:, cut]), nn_dot(normed, wu[:, cut])
        dacted = da_ref[:, cut]
        sigmoid = jax.nn.sigmoid(gate)
        silu = gate * sigmoid
        a_ref[:, cut] = (silu * upward).astype(BF16)
        slope = sigmoid * (1.0 + gate * (1.0 - sigmoid))
        dg_ref[:, cut] = (dacted * upward * slope).astype(BF16)
        du_ref[:, cut] = (dacted * silu).astype(BF16)


def hidden_units(normed, dacted, w_gate, w_up):
    rows, width = normed.shape
    units = w_gate.shape[1]
    block = min(ROW_BLOCK, rows)
    anywhere = pl.BlockSpec(memory_space=pl.ANY)
    return pl.pallas_call(
        hidden_kernel,
        grid=(rows // block,),
        in_specs=[by_rows(block, width), by_rows(block, units), anywhere, anywhere],
        out_specs=[by_rows(block, units)] * 3,
        out_shape=[jax.ShapeDtypeStruct((rows, units), BF16)] * 3,
        scratch_shapes=[pltpu.VMEM(w.shape, BF16) for w in (w_gate, w_up)]
        + [pltpu.SemaphoreType.DMA((2, len(column_cuts(units))))],
        compiler_params=pltpu.CompilerParams(vmem_limit_bytes=44 * 2**20),
        cost_estimate=pl.CostEstimate(
            flops=4 * rows * width * units,
            bytes_accessed=2 * rows * width + 4 * width * units + 10 * rows * units,
            transcendentals=rows * units,
        ),
    )(normed, dacted, w_gate, w_up)


def parts_kernel(
    a_ref, dg_ref, du_ref, wg_ref, wu_ref, wd_ref, dn_ref, f_ref, wg, wu, wd, sems
):
    cuts = column_cuts(dn_ref.shape[1])
    weights = (wg_ref, wu_ref, wd_ref), (wg, wu, wd)
    ready = stream_cuts(*weights, sems, (cuts, (False, False, True)))
    for n, cut in enumerate(cuts):
        ready(n)
        dnormed = nt_dot(dg_ref[...], wg[cut, :]) + nt_dot(du_ref[...], wu[cut, :])
        dn_ref[:, cut] = dnormed.astype(BF16)
        f_ref[:, cut] = nn_dot(a_ref[...], wd[:, cut]).astype(BF16)


def width_parts(acted, dgate, dupward, w_gate, w_up, w_down):
    rows, units = acted.shape
    width = w_gate.shape[0]
    block = min(ROW_BLOCK, rows)
    weights = (w_gate, w_up, w_down)
    return pl.pallas_call(
        parts_kernel,
        grid=(rows // block,),
        in_specs=[by_rows(block, units)] * 3 + [pl.BlockSpec(memory_space=pl.ANY)] * 3,
        out_specs=[by_rows(block, width)] * 2,
        out_shape=[jax.ShapeDtypeStruct((rows, width), BF16)] * 2,
        scratch_shapes=[pltpu.VMEM(w.shape, BF16) for w in weights]
        + [pltpu.SemaphoreType.DMA((3, len(column_cuts(width))))],
        compiler_params=pltpu.CompilerParams(vmem_limit_bytes=44 * 2**20),
        cost_estimate=pl.CostEstimate(
            flops=6 * rows * width * units,
            bytes_accessed=4 * rows * width + 6 * width * units + 6 * rows * units,
            transcendentals=0,
        ),
    )(acted, dgate, dupward, *weights)


def project_back_kernel(
    addends, x_ref, dq_ref, cos_ref, sin_ref, wq, wk, wv, *refs
):
    terms, (dkv_ref, dn_ref, gain_ref) = refs[:addends], refs[addends:]
    kv_width = terms[0].shape[2]
    cosine, sine = cos_ref[...], -sin_ref[...]
    dkeys, dvalues = terms[0][0], terms[0][1]
    for term in terms[1:]:
        dkeys, dvalues = dkeys + term[0].astype(F32), dvalues + term[1].astype(F32)
    for h in range(kv_width // HEAD_DIM):
        head = slice(h * HEAD_DIM, (h + 1) * HEAD_DIM)
        dkv_ref[:, head] = turn(dkeys[:, head], cosine, sine).astype(BF16)
    dkv_ref[:, kv_width:] = dvalues.astype(BF16)
    unit, _ = unit_of(x_ref[...].astype(F32))

    @pl.when(pl.program_id(0) == 0)
    def _():
        gain_ref[...] = jnp.zeros_like(gain_ref)

    for cut in column_cuts(dn_ref.shape[1]):
        dnormed = nt_dot(dq_ref[...], wq[cut, :])
        dnormed = dnormed + nt_dot(dkv_ref[:, :kv_width], wk[cut, :])
        dnormed = dnormed + nt_dot(dkv_ref[:, kv_width:], wv[cut, :])
        dn_ref[:, cut] = dnormed.astype(BF16)
        gain_ref[:, cut] += jnp.sum(dnormed * unit[:, cut], axis=0, keepdims=True)


def project_back(x_low, dq, terms, cosine, sine, w_query, w_key, w_value):
    rows, width = x_low.shape
    block = min(ROW_BLOCK, rows)
    heads_width, kv_width = w_query.shape[1], w_key.shape[1]
    kv_spec = pl.BlockSpec((2, block, kv_width), lambda i: (0, i, 0))
    return pl.pallas_call(
        functools.partial(project_back_kernel, len(terms)),
        grid=(rows // block,),
        in_specs=[
            by_rows(block, width),
            by_rows(block, heads_width),
            by_rows(block, HEAD_DIM),
            by_rows(block, HEAD_DIM),
            held(w_query),
            held(w_key),
            held(w_value),
        ]
        + [kv_spec] * len(terms),
        out_specs=[
            by_rows(block, 2 * kv_width),
            by_rows(block, width),
            pl.BlockSpec((1, width), lambda i: (0, 0)),
        ],
        out_shape=[
            jax.ShapeDtypeStruct((rows, 2 * kv_width), BF16),
            jax.ShapeDtypeStruct((rows, width), BF16),
            jax.ShapeDtypeStruct((1, width), F32),
        ],
        compiler_params=pltpu.CompilerParams(vmem_limit_bytes=40 * 2**20),
        cost_estimate=pl.CostEstimate(
            flops=2 * rows * width * (heads_width + 2 * kv_width),
            bytes_accessed=6 * rows * width + 2 * width * (heads_width + 2 * kv_width),
            transcendentals=rows,
        ),
    )(x_low, dq, cosine, sine, w_query, w_key, w_value, *terms)


def unpack_kernel(packed, *outs):
    row = 0
    for out in outs[:-1]:
        height = out.shape[1]
        out[...] = packed[row : row + height, :].astype(F32).T
        row += height
    outs[-1][...] = packed[row:, :].astype(F32)


def unpack(packed, *widths):
    total, width = packed.shape
    last = total - sum(widths)
    block = min(ROW_BLOCK, width)
    return pl.pallas_call(
        unpack_kernel,
        grid=(width // block,),
        in_specs=[pl.BlockSpec((total, block), lambda i: (0, i))],
        out_specs=[by_rows(block, w) for w in widths]
        + [pl.BlockSpec((last, block), lambda i: (0, i))],
        out_shape=[jax.ShapeDtypeStruct((width, w), F32) for w in widths]
        + [jax.ShapeDtypeStruct((last, width), F32)],
        compiler_params=pltpu.CompilerParams(vmem_limit_bytes=32 * 2**20),
    )(packed)


LINE_CHUNK = 32
MESH_AXES = ("dp", "ctx", "tensor")
SPREAD_PIECES = 2
PLANE_ROWS = 16
PLANE_SKEW = 2


def pair_steps(sizes):
    steps = []
    for axis, size in zip(MESH_AXES, sizes):
        bit = 1
        while bit < size:
            steps.append((axis, bit))
            bit *= 2
    return steps


def partner(axis, bit):
    index = lax.axis_index(axis)
    return jnp.where((index // bit) % 2 == 0, index + bit, index - bit)


def plane_steps(dp_size, ctx_size):
    across, along, bit = [], [], 1
    while bit < ctx_size:
        across.append(("ctx", bit))
        bit *= 2
    bit = 2
    while bit < dp_size:
        along.append(("dp", bit))
        bit *= 2
    first = [(("dp", 1), ("dp", 1))] if dp_size > 1 else []
    return tuple(first + list(zip(across + along, along + across)))


class PlaneSum:
    def __init__(self, stages, sources, out, inbox, send_sem, recv_sem):
        self.stages, self.sources, self.out, self.inbox = stages, sources, out, inbox
        self.send_sem, self.recv_sem = send_sem, recv_sem
        self.unit = 2 ** len(stages) * PLANE_ROWS
        self.count = out.shape[0] // self.unit
        odd = lax.axis_index("dp") % 2
        self.bits, self.peers = [], []
        for even_step, odd_step in stages:
            ids = {}
            for axis, bit, here in ((*even_step, odd == 0), (*odd_step, odd == 1)):
                index = ids.get(axis, lax.axis_index(axis))
                ids[axis] = jnp.where(here, partner(axis, bit), index)
            pick = lambda step: (lax.axis_index(step[0]) // step[1]) % 2
            self.bits.append(jnp.where(odd == 0, pick(even_step), pick(odd_step)))
            self.peers.append(ids)

    def start_row(self, c, k):
        row = c * self.unit
        for n in range(k):
            row = row + self.bits[n] * (self.unit >> (n + 1))
        return row

    def rows(self, start, size):
        return pl.ds(pl.multiple_of(start, PLANE_ROWS), size)

    def copy(self, slot, c, peer, source, target):
        return pltpu.make_async_remote_copy(
            src_ref=source,
            dst_ref=target,
            send_sem=self.send_sem.at[slot, c],
            recv_sem=self.recv_sem.at[slot, c],
            device_id=peer,
            device_id_type=pl.DeviceIdType.MESH,
        )

    def inward(self, k, c, source_ref, base):
        size = self.unit >> (k + 1)
        start = self.start_row(c, k) + (1 - self.bits[k]) * size - base
        target = self.inbox[k].at[self.rows(c * size, size)]
        return self.copy(k, c, self.peers[k], source_ref.at[self.rows(start, size)], target)

    def inward_wait(self, k, c):
        size = self.unit >> (k + 1)
        target = self.inbox[k].at[self.rows(c * size, size)]
        return self.copy(k, c, self.peers[k], target, target)

    def outward(self, k, c):
        size = self.unit >> (k + 1)
        block = self.out.at[self.rows(self.start_row(c, k + 1), size)]
        return self.copy(2 * len(self.stages) - 1 - k, c, self.peers[k], block, block)

    def at_source(self, c, act):
        base = 0
        for ref in self.sources:
            height = ref.shape[0]
            inside = (c * self.unit >= base) & (c * self.unit < base + height)
            pl.when(inside)(functools.partial(act, ref, base))
            base += height

    def stage(self, slot, c):
        total = len(self.stages)
        if slot == 0:
            self.at_source(c, lambda ref, base: self.inward(0, c, ref, base).start())
        elif slot <= total:
            k = slot - 1
            size = self.unit >> slot
            got = self.inbox[k].at[self.rows(c * size, size)]
            self.inward_wait(k, c).wait_recv()
            last = slot == total
            kept = self.out if last else self.inbox[k]
            place = self.rows(self.start_row(c, slot), size)
            where = place if last else self.rows(c * size, size)
            if k == 0:

                def add(ref, base):
                    mine = ref[self.rows(self.start_row(c, 1) - base, size), :]
                    kept[where, :] = (mine.astype(F32) + got[...].astype(F32)).astype(BF16)

                self.at_source(c, add)
            else:
                before = c * (2 * size) + self.bits[k] * size
                mine = self.inbox[k - 1][self.rows(before, size), :]
                kept[where, :] = (mine.astype(F32) + got[...].astype(F32)).astype(BF16)
            if last:
                self.outward(total - 1, c).start()
            else:
                base = self.start_row(c, slot) - c * size
                self.inward(slot, c, kept, base).start()
        else:
            k = 2 * total - slot
            self.outward(k, c).wait_recv()
            if k > 0:
                self.outward(k - 1, c).start()

    def steps(self):
        return self.count + PLANE_SKEW * 2 * len(self.stages)

    def step(self, s):
        for slot in range(2 * len(self.stages) + 1):
            c = s - PLANE_SKEW * slot
            pl.when((c >= 0) & (c < self.count))(functools.partial(self.stage, slot, c))

    def drain(self):
        def one(c, carry):
            for k in range(len(self.stages)):
                self.inward_wait(k, c).wait_send()
                self.outward(k, c).wait_send()
            return carry

        lax.fori_loop(0, self.count, one, 0)


def line_kernel(
    size,
    chunk,
    returns,
    owners,
    pairs,
    stages,
    source_count,
    side_count,
    out_count,
    far_count,
    *refs,
):
    streams = len(returns)
    returned = [k for k in range(streams) if returns[k]]
    parts, refs = refs[:streams], refs[streams:]
    sides, refs = refs[:side_count], refs[side_count:]
    shared, refs = dict(zip(returned, refs)), refs[len(returned) :]
    kept, refs = refs[:out_count], refs[out_count:]
    inbox, send_up, recv_up, send_back, recv_back = refs[:5]
    far, near, far_sems = sides[:far_count], refs[-1 - far_count : -1], refs[-1]
    refs = refs[: -1 - far_count]
    sides = sides[far_count:]
    plane = None
    if source_count:
        plane_inbox, plane_send, plane_recv = refs[9 : 9 + len(stages)], *refs[9 + len(stages) :]
        plane = PlaneSum(
            stages, sides[:source_count], kept[1], plane_inbox, plane_send, plane_recv
        )
        sides = sides[source_count:]
    sides = [*near, *sides]
    half = parts[0].shape[0] // 2
    count = half // chunk
    skew, window = (2, 2) if chunk > 16 else (3, 4)
    last = size - 1
    me = lax.axis_index("tensor")
    above, below = jnp.minimum(me + 1, last), jnp.maximum(me - 1, 0)
    flows = ((me, above, below), (last - me, below, above))

    def fetch(act):
        for n in range(far_count):
            for owner, start in ((last, 0), (0, half)):
                rows = pl.ds(start if far[n].shape[0] > half else 0, half)
                copy = pltpu.make_async_copy(far[n].at[rows], near[n], far_sems.at[n])
                pl.when(me == owner)(functools.partial(act, copy))

    fetch(lambda copy: copy.start())

    barrier = pltpu.get_barrier_semaphore()

    def greet(axis, other):
        pl.semaphore_signal(
            barrier, inc=1, device_id={axis: other}, device_id_type=pl.DeviceIdType.MESH
        )

    if pairs:
        for axis, bit in pairs:
            greet(axis, partner(axis, bit))
        far_above = jnp.where(me % 2 == 0, 0, 1) * jnp.where(me < last, 1, 0)
        far_below = jnp.where(me % 2 == 0, 1, 0) * jnp.where(me > 0, 1, 0)
        pl.when(far_above == 1)(lambda: greet("tensor", above))
        pl.when(far_below == 1)(lambda: greet("tensor", below))
        pl.semaphore_wait(barrier, len(pairs) + far_above + far_below)
    else:
        pl.when(me < last)(lambda: greet("tensor", above))
        pl.when(me > 0)(lambda: greet("tensor", below))
        pl.semaphore_wait(barrier, jnp.where((me > 0) & (me < last), 2, 1))

    def place(f, i):
        return pl.ds(pl.multiple_of(f * half + i * chunk, chunk), chunk)

    def local(i):
        return pl.ds(pl.multiple_of(i * chunk, chunk), chunk)

    def onward(k, f, i, source):
        return pltpu.make_async_remote_copy(
            src_ref=source,
            dst_ref=inbox.at[k, f, local(i)],
            send_sem=send_up.at[k, f, i],
            recv_sem=recv_up.at[k, f, i],
            device_id={"tensor": flows[f][1]},
            device_id_type=pl.DeviceIdType.MESH,
        )

    def backward(k, f, i):
        block = shared[k].at[place(f, i)]
        return pltpu.make_async_remote_copy(
            src_ref=block,
            dst_ref=block,
            send_sem=send_back.at[k, f, i],
            recv_sem=recv_back.at[k, f, i],
            device_id={"tensor": flows[f][2]},
            device_id_type=pl.DeviceIdType.MESH,
        )

    def reduce_chunk(k, f, i):
        position = flows[f][0]
        mine = parts[k].at[place(f, i)]
        slot = inbox.at[k, f, local(i)]

        @pl.when(position == 0)
        def _():
            pl.when(i >= window)(lambda: onward(k, f, i - window, mine).wait_send())
            onward(k, f, i, mine).start()

        @pl.when(position > 0)
        def _():
            onward(k, f, i, slot).wait_recv()
            total = slot[...].astype(F32) + mine[...].astype(F32)

            @pl.when(position < last)
            def _():
                slot[...] = total.astype(BF16)
                onward(k, f, i, slot).start()

            @pl.when(position == last)
            def _():
                result = owners[k](total, local(i), sides, kept)
                if returns[k]:
                    shared[k][place(f, i), :] = result.astype(BF16)
                    backward(k, f, i).start()

    def pass_back(k, f, i):
        position = flows[f][0]

        @pl.when((position < last) & (i >= 0) & (i < count))
        def _():
            backward(k, f, i).wait_recv()
            pl.when(position > 0)(lambda: backward(k, f, i).start())

    def step(s, carry):
        pl.when(s == skew * last)(lambda: fetch(lambda copy: copy.wait()))
        for k in range(streams):
            for f in range(2):
                i = s - skew * flows[f][0]
                pl.when((i >= 0) & (i < count))(lambda: reduce_chunk(k, f, i))
        for k in returned:
            for f in range(2):
                pass_back(k, f, s - skew * (2 * last - flows[f][0]))
        if plane:
            plane.step(s)
        for n in range(len(pairs) + 1 if pairs else 0):
            pl.when(s == n * gap)(lambda: advance_gains(n))
        return carry

    steps = count + 2 * skew * last
    if plane:
        steps = max(steps, plane.steps())
    gap = steps // (len(pairs) + 1)
    if pairs:
        slots, sums, send_pair, recv_pair = refs[5:9]
        sums[0] = sides[-1][...]
    elif len(kept) > 1:
        kept[1][...] = jnp.zeros_like(kept[1])

    def swap_gains(n):
        return pltpu.make_async_remote_copy(
            src_ref=sums.at[n],
            dst_ref=slots.at[n],
            send_sem=send_pair.at[n],
            recv_sem=recv_pair.at[n],
            device_id={pairs[n][0]: partner(*pairs[n])},
            device_id_type=pl.DeviceIdType.MESH,
        )

    def advance_gains(n):
        if n > 0:
            swap_gains(n - 1).wait()
            sums[n] = sums[n - 1] + slots[n - 1]
        if n < len(pairs):
            swap_gains(n).start()
        else:
            kept[0][...] = sums[n]

    lax.fori_loop(0, steps, step, 0)

    def drain(i, carry):
        for k in range(streams):
            for f in range(2):
                position = flows[f][0]
                waited = (position == 0) & (i < count - window)
                pl.when((position < last) & ~waited)(
                    lambda: onward(k, f, i, inbox.at[k, f, local(i)]).wait_send()
                )
                if returns[k]:
                    pl.when(position > 0)(lambda: backward(k, f, i).wait_send())
        return carry

    lax.fori_loop(0, count, drain, 0)
    if plane:
        plane.drain()


def line_sum(
    parts, owners, far, sides, kept, collective_id, returns=(True,), pairs=(), stages=(), sources=()
):
    rows, width = parts[0].shape
    size = lax.axis_size("tensor")
    streams = len(parts)
    chunk = max(16, min(LINE_CHUNK, rows // 32))
    count = rows // 2 // chunk
    whole = pl.BlockSpec(memory_space=pltpu.VMEM)
    scalar = pl.BlockSpec(memory_space=pltpu.SMEM)
    sems = pltpu.SemaphoreType.DMA((streams, 2, count))
    outs = [jax.ShapeDtypeStruct((rows, width), BF16)] * sum(returns) + list(kept)
    extra = []
    if pairs:
        pair_sems = pltpu.SemaphoreType.DMA((len(pairs),))
        extra = [
            pltpu.VMEM((len(pairs), 8, width), F32),
            pltpu.VMEM((len(pairs) + 1, 8, width), F32),
            pair_sems,
            pair_sems,
        ]
    if sources:
        plane_rows = sum(source.shape[0] for source in sources)
        unit = 2 ** len(stages) * PLANE_ROWS
        kept = [*kept, jax.ShapeDtypeStruct((plane_rows, width), BF16)]
        outs.append(kept[-1])
        extra += [pltpu.VMEM((plane_rows >> (k + 1), width), BF16) for k in range(len(stages))]
        extra += [pltpu.SemaphoreType.DMA((2 * len(stages), plane_rows // unit))] * 2
        sides = [*sources, *sides]
    extra += [pltpu.VMEM((rows // 2, width), array.dtype) for array in far]
    extra.append(pltpu.SemaphoreType.DMA((max(len(far), 1),)))
    return pl.pallas_call(
        functools.partial(
            line_kernel,
            size,
            chunk,
            returns,
            owners,
            pairs,
            stages,
            len(sources),
            len(far) + len(sides),
            len(kept),
            len(far),
        ),
        out_shape=outs,
        in_specs=[whole] * streams
        + [pl.BlockSpec(memory_space=pl.ANY)] * len(far)
        + [scalar if s.ndim == 1 else whole for s in sides],
        out_specs=[whole] * len(outs),
        scratch_shapes=[pltpu.VMEM((streams, 2, rows // 2, width), BF16)] + [sems] * 4 + extra,
        compiler_params=pltpu.CompilerParams(
            collective_id=collective_id, has_side_effects=True, vmem_limit_bytes=56 * 2**20
        ),
        cost_estimate=pl.CostEstimate(
            flops=streams * rows * width,
            bytes_accessed=streams * 300 * 2**20,
            transcendentals=0,
        ),
    )(*parts, *far, *sides)


def unit_of(rows):
    inverse = lax.rsqrt(jnp.mean(rows * rows, axis=-1, keepdims=True) + EPSILON)
    return rows * inverse, inverse


def own_hidden(total, here, sides, kept):
    x_ref, gain_ref = sides
    hidden = x_ref[here, :].astype(F32) + total
    kept[0][here, :] = hidden
    return unit_of(hidden)[0] * gain_ref[...]


def own_dhidden(total, here, sides, kept):
    x_ref, hidden_ref, cot_ref, gain_ref, factor = sides
    unit, inverse = unit_of(hidden_ref[here, :])
    kept[1][...] += jnp.sum(total * unit, axis=0, keepdims=True)
    dhidden = norm_back(total, unit, inverse, gain_ref[...])
    kept[0][here, :] = dhidden
    return cot_ref[here, :].astype(F32) * factor[0] + dhidden


def own_output(total, here, sides, kept):
    x_ref, hidden_ref, cot_ref, gain_ref, factor = sides
    x = x_ref[here, :].astype(F32)
    result = x + factor[1] * ((hidden_ref[here, :] - x) + total)
    kept[2][here, :] = result.astype(BF16)


def own_dinput(total, here, sides, kept):
    x_ref, dhidden_ref, gain_ref, _ = sides
    unit, inverse = unit_of(x_ref[here, :].astype(F32))
    return dhidden_ref[here, :] + norm_back(total, unit, inverse, gain_ref[...])


def cut_half(own):
    step = own.shape[0] // SPREAD_PIECES
    return [[own[p * step : (p + 1) * step]] for p in range(SPREAD_PIECES)]


def send_wave(pieces, wave):
    size = lax.axis_size("tensor")
    for p, hops in enumerate(pieces):
        h = wave - p
        if 0 <= h < size - 1:
            perm = [(size - 1 - h, size - 2 - h), (h, h + 1)]
            hops.append(lax.ppermute(hops[-1], "tensor", perm))


def tie(pieces, others):
    heads, others = lax.optimization_barrier(([hops[-1] for hops in pieces], others))
    for hops, head in zip(pieces, heads):
        hops[-1] = head
    return others


def join_kernel(size, *refs):
    pieces, out = refs[:-1], refs[-1]
    me = lax.axis_index("tensor")
    step = pieces[0].shape[0]
    half = out.shape[0] // 2
    for p in range(SPREAD_PIECES):
        for h in range(size):
            for f, wanted in enumerate((size - 1 - me, me)):

                @pl.when(wanted == h)
                def _():
                    out[pl.ds(f * half + p * step, step), :] = pieces[p * size + h][...]


def join_halves(pieces):
    size = lax.axis_size("tensor")
    step, width = pieces[0].shape
    whole = pl.BlockSpec(memory_space=pltpu.VMEM)
    return pl.pallas_call(
        functools.partial(join_kernel, size),
        out_shape=jax.ShapeDtypeStruct((2 * SPREAD_PIECES * step, width), BF16),
        in_specs=[whole] * len(pieces),
        out_specs=whole,
        compiler_params=pltpu.CompilerParams(vmem_limit_bytes=40 * 2**20),
    )(*pieces)


def rotary_tables(positions):
    inverse = 1.0 / 10000.0 ** (jnp.arange(0, HEAD_DIM, 2, dtype=F32) / HEAD_DIM)
    angle = positions.astype(F32)[:, None] * inverse[None, :]
    return (jnp.cos(angle), jnp.sin(angle))


def contract_rows(left, right):
    return jnp.einsum("rd,rf->df", left, right, preferred_element_type=F32)


def contract_cols(left, right):
    return jnp.einsum("rc,dc->rd", left, right, preferred_element_type=F32)


def norm_back(dnormed, unit, inverse, gain):
    scaled = dnormed * gain
    return inverse * (scaled - unit * jnp.mean(scaled * unit, axis=-1, keepdims=True))


def flags_kernel(size, mine, everyone, send_sem, recv_sem):
    me = lax.axis_index("dp")
    barrier = pltpu.get_barrier_semaphore()
    others = [lax.rem(me + s, size) for s in range(1, size)]
    for other in others:
        pl.semaphore_signal(
            barrier, inc=1, device_id={"dp": other}, device_id_type=pl.DeviceIdType.MESH
        )
    pl.semaphore_wait(barrier, size - 1)

    def send(s, slot):
        return pltpu.make_async_remote_copy(
            src_ref=mine,
            dst_ref=everyone.at[slot],
            send_sem=send_sem.at[s],
            recv_sem=recv_sem.at[s],
            device_id={"dp": others[s]},
            device_id_type=pl.DeviceIdType.MESH,
        )

    for s in range(size - 1):
        send(s, me).start()
    everyone[me] = mine[...]
    for s in range(size - 1):
        send(s, me).wait_send()
        send(s, lax.rem(me + 2 * size - 1 - s, size)).wait_recv()


def share_flags(row):
    size = lax.axis_size("dp")
    tile = jnp.zeros((8, 128), jnp.int32).at[0, : row.shape[0]].set(row)
    sems = pltpu.SemaphoreType.DMA((size - 1,))
    whole = pl.BlockSpec(memory_space=pltpu.VMEM)
    shared = pl.pallas_call(
        functools.partial(flags_kernel, size),
        out_shape=jax.ShapeDtypeStruct((size, 8, 128), jnp.int32),
        in_specs=[whole],
        out_specs=whole,
        scratch_shapes=[sems, sems],
        compiler_params=pltpu.CompilerParams(collective_id=1, has_side_effects=True),
    )(tile)
    return shared[:, 0, : row.shape[0]]


def shift_ctx(part, s):
    size = lax.axis_size("ctx")
    return lax.ppermute(part, "ctx", [(i, (i + s) % size) for i in range(size)])


def swap_core(part):
    return lax.ppermute(part, "dp", [(i, i ^ 1) for i in range(lax.axis_size("dp"))])


def gather_parts(own, paired):
    parts = []
    for s in range(lax.axis_size("ctx")):
        here = own if s == 0 else shift_ctx(own, s)
        parts += [here, swap_core(here)] if paired else [here]
    return parts


def collect_parts(parts, paired):
    terms = [parts[0]]
    if paired:
        terms.append(swap_core(parts[1]))
    per = 2 if paired else 1
    for s in range(1, lax.axis_size("ctx")):
        near = parts[per * s]
        if paired:
            near = (near.astype(F32) + swap_core(parts[per * s + 1]).astype(F32)).astype(BF16)
        terms.append(shift_ctx(near, -s))
    return terms


def block_pass(
    paired,
    first_id,
    span,
    x_low,
    cot_low,
    keep,
    scale,
    order_row,
    attn_gain,
    ffn_gain,
    w_query,
    w_key,
    w_value,
    w_output,
    w_gate,
    w_up,
    w_down,
):
    rows, width = x_low.shape
    dp_size, ctx_size = lax.axis_size("dp"), lax.axis_size("ctx")
    spans = order_row.shape[0]
    ctx = lax.axis_index("ctx")
    core = lax.axis_index("dp") % 2
    per_part = rows // span
    places = []
    for s in range(ctx_size):
        group = (ctx + ctx_size - s) % ctx_size
        places += [group * 2 + core, group * 2 + 1 - core] if paired else [group]
    spread = jnp.arange(per_part, dtype=jnp.int32)
    places = jnp.concatenate([place * per_part + spread for place in places])
    chosen = places[:, None] == jnp.arange(spans, dtype=jnp.int32)[None, :]
    key_order = jnp.sum(jnp.where(chosen, order_row[None, :], 0), axis=1)
    query_order = key_order[:per_part]
    row_index = jnp.arange(rows, dtype=jnp.int32)
    starts = jnp.sum(
        jnp.where(
            (row_index // span)[:, None] == jnp.arange(per_part, dtype=jnp.int32)[None, :],
            query_order[None, :],
            0,
        ),
        axis=1,
    )
    cosine, sine = rotary_tables(starts * span + row_index % span)

    wide_cosine = jnp.concatenate([cosine, cosine], axis=1)
    wide_sine = jnp.concatenate([-sine, sine], axis=1)
    attn_row, ffn_row = attn_gain[None, :], ffn_gain[None, :]
    normed_one, queries, kv_own = project(
        x_low, attn_row, wide_cosine, wide_sine, w_query, w_key, w_value
    )
    kv_parts = gather_parts(kv_own, paired)
    dffn = (cot_low.astype(F32) * (keep * scale)).astype(BF16)
    dacted = contract_cols(dffn, w_down)
    queries, dacted = lax.optimization_barrier((queries, dacted))
    mixed, logs = attend(queries, kv_parts, query_order, key_order, span)

    half_rows = jax.ShapeDtypeStruct((rows // 2, width), F32)
    gain_row = jax.ShapeDtypeStruct((1, width), F32)
    attn_part = nn_dot(mixed, w_output).astype(BF16)
    normed_two, hidden = line_sum(
        [attn_part], [own_hidden], [x_low], [ffn_row], [half_rows], first_id
    )

    factors = jnp.stack([keep * scale, keep])
    acted, dgate, dupward = hidden_units(normed_two, dacted, w_gate, w_up)
    early_grads = [
        contract_rows(acted, dffn).astype(BF16),
        contract_rows(normed_two, dgate).astype(BF16),
        contract_rows(normed_two, dupward).astype(BF16),
    ]
    late_grads = [early_grads.pop()] if paired else []
    acted, dgate, dupward, early_grads, late_grads = lax.optimization_barrier(
        (acted, dgate, dupward, early_grads, late_grads)
    )
    early_grads = lax.psum(early_grads, ("dp", "ctx"))
    dnormed_part, ffn_part = width_parts(acted, dgate, dupward, w_gate, w_up, w_down)
    dattn, dhidden, ffn_gain_part, output_half = line_sum(
        [dnormed_part, ffn_part],
        [own_dhidden, own_output],
        [x_low, hidden, cot_low],
        [ffn_row, factors],
        [half_rows, gain_row, jax.ShapeDtypeStruct((rows // 2, width), BF16)],
        first_id + 1,
        (True, False),
    )
    pieces = cut_half(output_half)
    send_wave(pieces, 0)
    dmixed = contract_cols(dattn, w_output).astype(BF16)
    dq_proj, *dkv_parts = attend_back(
        queries, dmixed, mixed, logs, cosine, sine, kv_parts, query_order, key_order, span
    )
    dq_proj, dkv_parts = tie(pieces, (dq_proj, dkv_parts))
    send_wave(pieces, 1)
    terms = collect_parts(dkv_parts, paired)
    grad_query = contract_rows(dq_proj, normed_one).astype(BF16)
    grad_output = contract_rows(mixed, dattn).astype(BF16)
    grad_query, grad_output = tie(pieces, (grad_query, grad_output))
    send_wave(pieces, 2)
    if not paired:
        early_grads = [g.astype(F32) for g in early_grads]
        terms, early_grads = lax.optimization_barrier((terms, early_grads))
    terms, grad_query, grad_output = lax.optimization_barrier((terms, grad_query, grad_output))
    dkv_proj, dnormed_one, attn_gain_part = project_back(
        x_low, dq_proj, terms, wide_cosine, wide_sine, w_query, w_key, w_value
    )
    gain_parts = jnp.concatenate(
        [attn_gain_part, ffn_gain_part, jnp.zeros((6, width), F32)], axis=0
    )
    grad_kv = contract_rows(dkv_proj, normed_one).astype(BF16)
    dnormed_one, early_grads, late_grads = tie(pieces, (dnormed_one, early_grads, late_grads))
    if paired:
        late_grads = lax.psum(late_grads, ("ctx", "dp"))
        early_grads = [g.astype(F32) for g in early_grads]
        dnormed_one, early_grads = lax.optimization_barrier((dnormed_one, early_grads))
    for wave in range(3, lax.axis_size("tensor") + SPREAD_PIECES):
        send_wave(pieces, wave)
    through, gains, attn_grads = line_sum(
        [dnormed_one],
        [own_dinput],
        [x_low, dhidden],
        [attn_row, gain_parts],
        [jax.ShapeDtypeStruct((8, width), F32)],
        first_id + 2,
        (True,),
        tuple(pair_steps((dp_size, ctx_size, lax.axis_size("tensor")))),
        plane_steps(dp_size, ctx_size),
        [grad_query, grad_kv, grad_output],
    )
    through, gains, attn_grads, early_grads, late_grads, pieces = lax.optimization_barrier(
        (through, gains, attn_grads, early_grads, late_grads, pieces)
    )
    output = join_halves([hop for hops in pieces for hop in hops])
    grads = (attn_grads, *early_grads, *late_grads)
    return output, through, gains, grads


def per_device(
    inputs,
    cotangent,
    skip_mask,
    group_ids,
    span_order,
    exit_scale,
    attn_gain,
    ffn_gain,
    *weights,
):
    _, rows, width = inputs.shape
    spans = span_order.shape[1]
    own_spans = spans // lax.axis_size("ctx")
    span = rows // own_spans
    me = lax.axis_index("dp")
    core = me % 2
    x_low, cot_low = inputs[0], cotangent[0]
    flags = share_flags(jnp.concatenate([skip_mask, group_ids, span_order[0]]))
    runs, groups = flags[:, 0], flags[:, 1]
    scale_of = lambda group: jnp.where(group == 1, exit_scale[1], exit_scale[0])
    own_run, own_scale = skip_mask[0], scale_of(group_ids[0])
    gains = (attn_gain, ffn_gain)

    def alone():
        return block_pass(
            False,
            2,
            span,
            x_low,
            cot_low,
            own_run.astype(F32),
            own_scale,
            span_order[0],
            *gains,
            *weights,
        )

    def shared():
        half = rows // 2
        other = me + 1 - 2 * core
        take = lambda a, i: lax.dynamic_slice_in_dim(a, i * half, half, 0)
        pick = lambda a: lax.dynamic_index_in_dim(a, other, 0, keepdims=False)
        other_run = pick(runs)
        use_own = (own_run == 1) | ((other_run == 0) & (core == 0))
        choose = lambda mine, theirs: jnp.where(use_own, mine, theirs)
        work = lambda a: choose(take(a, core), swap_core(take(a, 1 - core)))
        output, through, *rest = block_pass(
            True,
            5,
            span,
            work(x_low),
            work(cot_low),
            choose(own_run, other_run).astype(F32),
            choose(own_scale, scale_of(pick(groups))),
            choose(span_order[0], pick(flags[:, 2:])),
            *gains,
            *weights,
        )

        def whole(part):
            theirs = swap_core(part)
            first, second = jnp.where(core == 0, part, theirs), jnp.where(core == 0, theirs, part)
            return jnp.concatenate([first, second], 0)

        through = jnp.where(own_run == 1, whole(through), 0)
        return whole(output), through, *rest

    def finish(output, through, sums, grads):
        output = jnp.where(own_run == 1, output, x_low)
        input_grad = cot_low.astype(F32) * own_scale + through.astype(F32)
        attn_grads = unpack(grads[0], *[w.shape[1] for w in weights[:3]])
        grads = [g.astype(F32) for g in grads[1:]]
        return lax.optimization_barrier(
            (output, input_grad, sums[0], sums[1], *attn_grads, *grads)
        )

    if own_spans % 2 == 0 and lax.axis_size("dp") % 2 == 0:
        pairs = runs.reshape(-1, 2)
        results = lax.cond(
            jnp.all(pairs[:, 0] * pairs[:, 1] == 0),
            lambda: finish(*shared()),
            lambda: finish(*alone()),
        )
    else:
        results = finish(*alone())
    output, input_grad, grad_attn_gain, grad_ffn_gain = results[:4]
    grad_query, grad_key, grad_value, grad_output, grad_down, grad_gate, grad_up = results[4:]
    return (
        output.reshape(inputs.shape),
        input_grad.reshape(inputs.shape),
        grad_attn_gain,
        grad_ffn_gain,
        grad_query,
        grad_key,
        grad_value,
        grad_output,
        grad_gate,
        grad_up,
        grad_down,
    )


def solution(mesh):
    rows = P("dp", "ctx", None)
    by_column, by_row = P(None, "tensor"), P("tensor", None)
    in_specs = (rows, rows, P("dp"), P("dp"), P("dp", None), P(), P(), P())
    in_specs += (by_column,) * 3 + (by_row,) + (by_column,) * 2 + (by_row,)
    out_specs = (rows, rows, P(), P()) + (by_column,) * 3 + (by_row,) + (by_column,) * 2 + (by_row,)
    return jax.shard_map(
        per_device, mesh=mesh, in_specs=in_specs, out_specs=out_specs, check_vma=False
    )
```
